32 devices in a mesh: ctx: 16 (over z, y, x), wa: 2 (over core).
Axes of the slice: x: 2, y: 2, z: 4, core: 2. Of those that a mesh axis runs over, the one named last changes fastest.
Arguments:
- hidden_in: bfloat16 [256, 16, 1024], P(None, 'ctx'), may hold values from -6 to 6
- attn_gain: float32 [1024], replicated, may hold values from 0.25 to 1.75
- query_weight: bfloat16 [1024, 1024], P(None, 'wa'), may hold values from -0.1875 to 0.1875
- key_weight: bfloat16 [1024, 512], P(None, 'wa'), may hold values from -0.1875 to 0.1875
- value_weight: bfloat16 [1024, 512], P(None, 'wa'), may hold values from -0.1875 to 0.1875
- query_gain: float32 [64], replicated, may hold values from 0.6 to 1.8
- key_gain: float32 [64], replicated, may hold values from 0.6 to 1.8
- out_weight: bfloat16 [1024, 1024], P('wa'), may hold values from -1.5 to 1.5
- ffn_gain: float32 [1024], replicated, may hold values from 0.25 to 1.75
- gate_weight: bfloat16 [1024, 4608], P(None, 'wa'), may hold values from -0.1875 to 0.1875
- up_weight: bfloat16 [1024, 4608], P(None, 'wa'), may hold values from -0.1875 to 0.1875
- down_weight: bfloat16 [4608, 1024], P('wa'), may hold values from -0.09375 to 0.09375
- query_adapt_in: bfloat16 [1024, 128], replicated, may hold values from -0.1875 to 0.1875
- query_adapt_out: bfloat16 [128, 1024], P(None, 'wa'), may hold values from -0.75 to 0.75
- key_adapt_in: bfloat16 [1024, 128], replicated, may hold values from -0.1875 to 0.1875
- key_adapt_out: bfloat16 [128, 512], P(None, 'wa'), may hold values from -0.75 to 0.75
- value_adapt_in: bfloat16 [1024, 128], replicated, may hold values from -0.1875 to 0.1875
- value_adapt_out: bfloat16 [128, 512], P(None, 'wa'), may hold values from -0.75 to 0.75
- out_adapt_in: bfloat16 [1024, 128], P('wa'), may hold values from -1.5 to 1.5
- out_adapt_out: bfloat16 [128, 1024], replicated, may hold values from -0.75 to 0.75
- gate_adapt_in: bfloat16 [1024, 128], replicated, may hold values from -0.1875 to 0.1875
- gate_adapt_out: bfloat16 [128, 4608], P(None, 'wa'), may hold values from -0.75 to 0.75
- up_adapt_in: bfloat16 [1024, 128], replicated, may hold values from -0.1875 to 0.1875
- up_adapt_out: bfloat16 [128, 4608], P(None, 'wa'), may hold values from -0.75 to 0.75
- down_adapt_in: bfloat16 [4608, 128], P('wa'), may hold values from -0.09375 to 0.09375
- down_adapt_out: bfloat16 [128, 1024], replicated, may hold values from -0.75 to 0.75
- document_extra: int32 [4], replicated, may hold values from 1 to 1801, 3300 in all
- document_adapter: int32 [4], replicated, may hold values from 0 to 7
- cotangent: bfloat16 [256, 16, 1024], P(None, 'ctx'), may hold values from -6 to 6
Outputs:
- output: bfloat16 [256, 16, 1024], P(None, 'ctx')
- input_grad: bfloat16 [256, 16, 1024], P(None, 'ctx')
- query_in_grad: float32 [1024, 128], replicated
- query_out_grad: float32 [128, 1024], P(None, 'wa')
- key_in_grad: float32 [1024, 128], replicated
- key_out_grad: float32 [128, 512], P(None, 'wa')
- value_in_grad: float32 [1024, 128], replicated
- value_out_grad: float32 [128, 512], P(None, 'wa')
- out_in_grad: float32 [1024, 128], P('wa')
- out_out_grad: float32 [128, 1024], replicated
- gate_in_grad: float32 [1024, 128], replicated
- gate_out_grad: float32 [128, 4608], P(None, 'wa')
- up_in_grad: float32 [1024, 128], replicated
- up_out_grad: float32 [128, 4608], P(None, 'wa')
- down_in_grad: float32 [4608, 128], P('wa')
- down_out_grad: float32 [128, 1024], replicated
The draws below stay inside these ranges and needn't reach their ends.
Inputs may be any that keep to these rules, and one draw needn't show every extreme that they name: Document j has document_extra[j] + 199 tokens; the documents fill the 4096 tokens in order, and one has exactly 2000 tokens.
All inputs are finite; a program needn't handle non-finite values.
Results may differ from the reference program's by a relative error of at most 0.02.
Values may be sent and summed in bfloat16 or wider, within the bound.
No kernel may reach another device: no remote copies, remote signals or barrier semaphores. Data moves between devices by JAX's collectives and lax.ppermute only.
A program may use at most 256 MiB of HBM per device.

```python
import math
import jax
import jax.numpy as jnp
import numpy as np
from jax import lax

D = 1024
HEADS = 16
KVH = 8
HD = 64
FF = 4608
ADAPT = 8
RANK = 16
TOK_DEV = 256
DOC_MIN = 200
DOC_MAX = 2000
STRIDE = 16
TOKENS = 4096
NDOC = 4


def touch_ends(drawn, key, least, largest):
    longest = drawn.shape.index(max(drawn.shape))
    spots = []
    for shift in (0, 1):
        where = [jax.random.randint(jax.random.fold_in(key, axis), (), 0, length) for axis, length in enumerate(drawn.shape)]
        where[longest] = (where[longest] + shift) % drawn.shape[longest]
        spots.append(tuple(where))
    return drawn.at[spots[0]].set(least).at[spots[1]].set(largest)


def block_scale(rng, dims, split, least, top_value):
    level = 1.0
    for dim, blocks in split:
        draws = jax.random.uniform(jax.random.fold_in(jax.random.fold_in(rng, 6), dim), (blocks,), jnp.float32, least / len(split), top_value / len(split))
        level = level * jnp.repeat(jnp.exp(draws), dims[dim] // blocks).reshape((-1,) + (1,) * (len(dims) - 1 - dim))
    return level


def length_profile(amount, total, reach, slope):
    portions = [(1 << 20) // math.isqrt(standing ** slope) + 1 for standing in range(2, amount + 1)]
    surplus, given = total - reach - (amount - 1), [1] * (amount - 1)
    while surplus > 0:
        movable = [i for i in range(amount - 1) if given[i] < reach]
        mass, remaining = sum([portions[i] for i in movable]), surplus
        for i in movable:
            more = min(reach - given[i], max(1, remaining * portions[i] // mass), surplus)
            given[i] = given[i] + more
            surplus = surplus - more
    return np.array([reach] + given)


def ragged_sizes(stream_key, count, total, bound, skew):
    if count == 2:
        one = jax.random.randint(stream_key, (), max(1, total - bound), min(bound, total - 1) + 1)
        return jnp.stack([one, total - one])
    tallies = jnp.asarray(length_profile(count, total, bound, skew), jnp.int32)
    pairs = (count - 1) // 2
    source_of, taker = tallies[1:1 + 2 * pairs:2], tallies[2:2 + 2 * pairs:2]
    margin = jnp.minimum(source_of - 1, bound - taker)
    passed = jax.random.randint(jax.random.fold_in(stream_key, 1), (pairs,), 0, 1 << 20) % (margin + 1)
    tallies = tallies.at[1:1 + 2 * pairs:2].set(source_of - passed).at[2:2 + 2 * pairs:2].set(taker + passed)
    return tallies[jax.random.permutation(jax.random.fold_in(stream_key, 2), count)]


def scatter_about(stream_key, dims, spread, reach, split=(), held_as=jnp.bfloat16):
    loudness = block_scale(stream_key, dims, split, -0.22, 0.18) if split else 1.0
    result = jax.random.normal(stream_key, dims, jnp.float32) * spread * loudness
    return jnp.minimum(jnp.maximum(result, -reach), reach).astype(held_as)


def setup_inputs(seed: int = 0) -> dict:
    seeds = jax.random.split(jax.random.key(seed), 30)
    return {
        "hidden_in": scatter_about(seeds[0], (TOK_DEV, STRIDE, D), 1.0, 6.0, ((1, 16),)),
        "attn_gain": jnp.clip(1.0 + 0.15 * jax.random.normal(seeds[1], (D,), jnp.float32), 0.25, 1.75),
        "query_weight": scatter_about(seeds[2], (D, HEADS * HD), D ** -0.5, 0.1875, ((1, 2),)),
        "key_weight": scatter_about(seeds[3], (D, KVH * HD), D ** -0.5, 0.1875, ((1, 2),)),
        "value_weight": scatter_about(seeds[4], (D, KVH * HD), D ** -0.5, 0.1875, ((1, 2),)),
        "query_gain": jnp.clip(jnp.exp(jax.random.uniform(seeds[5], (HD,), jnp.float32, math.log(0.6), math.log(1.8))), 0.6, 1.8),
        "key_gain": jnp.clip(jnp.exp(jax.random.uniform(seeds[6], (HD,), jnp.float32, math.log(0.6), math.log(1.8))), 0.6, 1.8),
        "out_weight": scatter_about(seeds[7], (HEADS * HD, D), 16 ** -0.5, 1.5, ((0, 2),)),
        "ffn_gain": jnp.clip(1.0 + 0.15 * jax.random.normal(seeds[8], (D,), jnp.float32), 0.25, 1.75),
        "gate_weight": scatter_about(seeds[9], (D, FF), D ** -0.5, 0.1875, ((1, 2),)),
        "up_weight": scatter_about(seeds[10], (D, FF), D ** -0.5, 0.1875, ((1, 2),)),
        "down_weight": scatter_about(seeds[11], (FF, D), FF ** -0.5, 0.09375, ((0, 2),)),
        "query_adapt_in": scatter_about(seeds[12], (D, ADAPT * RANK), D ** -0.5, 0.1875),
        "query_adapt_out": scatter_about(seeds[13], (ADAPT * RANK, HEADS * HD), 64 ** -0.5, 0.75, ((1, 2),)),
        "key_adapt_in": scatter_about(seeds[14], (D, ADAPT * RANK), D ** -0.5, 0.1875),
        "key_adapt_out": scatter_about(seeds[15], (ADAPT * RANK, KVH * HD), 64 ** -0.5, 0.75, ((1, 2),)),
        "value_adapt_in": scatter_about(seeds[16], (D, ADAPT * RANK), D ** -0.5, 0.1875),
        "value_adapt_out": scatter_about(seeds[17], (ADAPT * RANK, KVH * HD), 64 ** -0.5, 0.75, ((1, 2),)),
        "out_adapt_in": scatter_about(seeds[18], (HEADS * HD, ADAPT * RANK), 16 ** -0.5, 1.5, ((0, 2),)),
        "out_adapt_out": scatter_about(seeds[19], (ADAPT * RANK, D), 64 ** -0.5, 0.75),
        "gate_adapt_in": scatter_about(seeds[20], (D, ADAPT * RANK), D ** -0.5, 0.1875),
        "gate_adapt_out": scatter_about(seeds[21], (ADAPT * RANK, FF), 64 ** -0.5, 0.75, ((1, 2),)),
        "up_adapt_in": scatter_about(seeds[22], (D, ADAPT * RANK), D ** -0.5, 0.1875),
        "up_adapt_out": scatter_about(seeds[23], (ADAPT * RANK, FF), 64 ** -0.5, 0.75, ((1, 2),)),
        "down_adapt_in": scatter_about(seeds[24], (FF, ADAPT * RANK), FF ** -0.5, 0.09375, ((0, 2),)),
        "down_adapt_out": scatter_about(seeds[25], (ADAPT * RANK, D), 64 ** -0.5, 0.75),
        "document_extra": ragged_sizes(seeds[26], NDOC, TOKENS - NDOC * (DOC_MIN - 1), DOC_MAX - DOC_MIN + 1, 0).astype(jnp.int32),
        "document_adapter": touch_ends(jax.random.randint(seeds[27], (NDOC,), 0, ADAPT), jax.random.fold_in(seeds[27], 1), 0, ADAPT - 1).astype(jnp.int32),
        "cotangent": scatter_about(seeds[28], (TOK_DEV, STRIDE, D), 1.0, 6.0, ((1, 16),)),
    }


@jax.custom_vjp
def low(v):
    return lax.optimization_barrier(v.astype(jnp.bfloat16)).astype(jnp.float32)

@jax.custom_vjp
def low_back(v):
    return v

def low_keep(v):
    return (low(v), None)

def low_pass(kept, grad):
    return (grad,)

def back_keep(v):
    return (v, None)

def back_low(kept, grad):
    return (low(grad),)
low.defvjp(low_keep, low_pass)
low_back.defvjp(back_keep, back_low)
norm_eps = 1e-05
masked_score = -1e+30
theta_base = 1000000.0

def rms_gain(values, gain):
    return values * lax.rsqrt(lax.optimization_barrier(jnp.mean(values * values, axis=-1, keepdims=True)) + norm_eps) * gain

def rotate(values, cosine, sine):
    half_width = values.shape[-1] // 2
    first_half = values[..., :half_width]
    second = values[..., half_width:]
    return jnp.concatenate([first_half * cosine - second * sine, second * cosine + first_half * sine], axis=-1)

def head_prep(raw, gain, cosine, sine):
    heads = raw.reshape(raw.shape[0], -1, gain.shape[0])
    return rotate(rms_gain(heads, gain), cosine[:, None, :], sine[:, None, :])

def dense_dot(left, right):
    return jnp.dot(left, right, precision=lax.Precision.HIGHEST)

def adapted(inputs, weight, adapt_in, adapt_out, adapt_mask):
    side = low(low_back(adapt_mask * dense_dot(inputs, adapt_in)))
    return dense_dot(inputs, weight) + dense_dot(side, adapt_out)

def attend(queries, keys, values, token_index, doc_of):
    groups = HEADS // KVH
    block_rows = min(256, TOKENS)
    query_blocks = queries.reshape(TOKENS // block_rows, block_rows, KVH, groups, HD)
    index_blocks = token_index.reshape(-1, block_rows)
    doc_blocks = doc_of.reshape(-1, block_rows)

    def one_block(block_args):
        query_rows, query_index, query_doc = block_args
        scores = low_back(jnp.einsum('qhgd,khd->hgqk', query_rows, keys, precision=lax.Precision.HIGHEST) * HD ** (-0.5))
        seen = (query_doc[:, None] == doc_of[None, :]) & (token_index[None, :] <= query_index[:, None])
        scores = jnp.where(seen, scores, masked_score)
        log_totals = jax.nn.logsumexp(scores, axis=-1, keepdims=True)
        weights = low(jnp.exp(scores - log_totals))
        return jnp.einsum('hgqk,khd->qhgd', weights, values, precision=lax.Precision.HIGHEST)
    attended = lax.map(jax.checkpoint(one_block), (query_blocks, index_blocks, doc_blocks))
    return attended.reshape(TOKENS, HEADS * HD)

def reference(hidden_in, attn_gain, query_weight, key_weight, value_weight, query_gain, key_gain, out_weight, ffn_gain, gate_weight, up_weight, down_weight, query_adapt_in, query_adapt_out, key_adapt_in, key_adapt_out, value_adapt_in, value_adapt_out, out_adapt_in, out_adapt_out, gate_adapt_in, gate_adapt_out, up_adapt_in, up_adapt_out, down_adapt_in, down_adapt_out, document_extra, document_adapter, cotangent):
    token_index = jnp.arange(TOKENS, dtype=jnp.int32)
    lengths = (document_extra + (DOC_MIN - 1)).astype(jnp.int32)
    doc_ends = jnp.cumsum(lengths).astype(jnp.int32)
    doc_starts = (doc_ends - lengths).astype(jnp.int32)
    doc_of = lax.optimization_barrier(jnp.sum((doc_ends[None, :] <= token_index[:, None]).astype(jnp.int32), axis=1)).astype(jnp.int32)
    position = (token_index - doc_starts[doc_of]).astype(jnp.int32)
    adapter = document_adapter[doc_of]
    adapt_cols = jnp.arange(ADAPT * RANK, dtype=jnp.int32) // RANK
    adapt_mask = (adapter[:, None] == adapt_cols[None, :]).astype(jnp.float32)
    inverse = jnp.exp(jnp.arange(HD // 2, dtype=jnp.float32) * (-2.0 * math.log(theta_base) / HD))
    angle = position.astype(jnp.float32)[:, None] * inverse[None, :]
    cosine = jnp.cos(angle)
    sine = jnp.sin(angle)
    w_query = query_weight.astype(jnp.float32)
    w_key = key_weight.astype(jnp.float32)
    w_value = value_weight.astype(jnp.float32)
    w_out = out_weight.astype(jnp.float32)
    w_gate = gate_weight.astype(jnp.float32)
    w_upper = up_weight.astype(jnp.float32)
    w_down = down_weight.astype(jnp.float32)

    def forward(x_rows, factors):
        qin, qout, kin, kout, vin, vout, oin, oout, gin, gout, uin, uout, din, dout = factors
        normed = low(rms_gain(x_rows, attn_gain))
        query_raw = low_back(adapted(normed, w_query, qin, qout, adapt_mask))
        key_raw = low_back(adapted(normed, w_key, kin, kout, adapt_mask))
        values = low(low_back(adapted(normed, w_value, vin, vout, adapt_mask)))
        queries = low(head_prep(query_raw, query_gain, cosine, sine))
        keys = low(head_prep(key_raw, key_gain, cosine, sine))
        attended = low(low_back(attend(queries, keys, values.reshape(TOKENS, KVH, HD), token_index, doc_of)))
        mixed = x_rows + low_back(adapted(attended, w_out, oin, oout, adapt_mask))
        ffn_normed = low(rms_gain(mixed, ffn_gain))
        gate = low_back(adapted(ffn_normed, w_gate, gin, gout, adapt_mask))
        upper = low_back(adapted(ffn_normed, w_upper, uin, uout, adapt_mask))
        hidden = low(jax.nn.silu(gate) * upper)
        return mixed + low_back(adapted(hidden, w_down, din, dout, adapt_mask))
    x_rows = hidden_in.reshape(TOKENS, D).astype(jnp.float32)
    factors = tuple((factor.astype(jnp.float32) for factor in (query_adapt_in, query_adapt_out, key_adapt_in, key_adapt_out, value_adapt_in, value_adapt_out, out_adapt_in, out_adapt_out, gate_adapt_in, gate_adapt_out, up_adapt_in, up_adapt_out, down_adapt_in, down_adapt_out)))
    block_out, pullback = jax.vjp(forward, x_rows, factors)
    grad_x, grad_factors = pullback(cotangent.reshape(TOKENS, D).astype(jnp.float32))
    return (block_out.astype(jnp.bfloat16).reshape(TOK_DEV, STRIDE, D), grad_x.astype(jnp.bfloat16).reshape(TOK_DEV, STRIDE, D), grad_factors[0], grad_factors[1], grad_factors[2], grad_factors[3], grad_factors[4], grad_factors[5], grad_factors[6], grad_factors[7], grad_factors[8], grad_factors[9], grad_factors[10], grad_factors[11], grad_factors[12], grad_factors[13])
```

```python
import functools
import math

import jax
import jax.numpy as jnp
from jax import lax
from jax.experimental import pallas as pl
from jax.experimental.pallas import tpu as pltpu
from jax.sharding import PartitionSpec as P

RANK = 16
DOC_MIN = 200

norm_eps = 1e-05
theta_base = 1000000.0
BF = jnp.bfloat16
F32 = jnp.float32
LOG2E = 1.4426950408889634
VMEM_LIMIT = 56 * 1024 * 1024


def mm(left, right):
    return jnp.dot(left, right, preferred_element_type=F32)


def mm_nt(left, right):
    return lax.dot_general(left, right, (((1,), (1,)), ((), ())), preferred_element_type=F32)


def mm_tn(left, right):
    return lax.dot_general(left, right, (((0,), (0,)), ((), ())), preferred_element_type=F32)


def iota(shape, dim):
    return lax.broadcasted_iota(jnp.int32, shape, dim)


class Cfg:
    def __init__(self, tokens, n_ctx, heads_kv, groups, head_dim, docs, adapt_width, width, hidden):
        self.T = tokens
        self.n = n_ctx
        self.G = heads_kv
        self.lo = n_ctx // heads_kv
        self.groups = groups
        self.hd = head_dim
        self.docs = docs
        self.AW = adapt_width
        self.slots = min(docs, adapt_width // RANK)
        self.S = self.slots * RANK
        self.D = width
        self.F = hidden
        self.R = max(16, min(tokens, 512 // n_ctx))
        self.NT = tokens // self.R
        self.span = self.R * n_ctx
        self.QH = self.G * self.R
        self.KT = n_ctx * self.R


def doc_starts(cfg, meta):
    out = [jnp.int32(0)]
    for j in range(cfg.docs):
        out.append(out[-1] + meta[2 + j] + (DOC_MIN - 1))
    return out


def start_of(starts, token):
    out = jnp.zeros_like(token)
    for s in starts[1:-1]:
        out = jnp.where(token >= s, s, out)
    return out


def end_of(starts, token):
    out = starts[1]
    for j in range(1, len(starts) - 1):
        out = jnp.where(token >= starts[j], starts[j + 1], out)
    return out


def adapter_mask(cfg, meta):
    token = iota((cfg.T, cfg.AW), 0) * cfg.n + meta[0]
    starts = doc_starts(cfg, meta)
    adapter = jnp.full((cfg.T, cfg.AW), meta[2 + cfg.docs], jnp.int32)
    for j in range(1, cfg.docs):
        adapter = jnp.where(token >= starts[j], meta[2 + cfg.docs + j], adapter)
    return (adapter == iota((cfg.T, cfg.AW), 1) // RANK).astype(F32)


def slot_select(cfg, meta):
    row = iota((cfg.AW, cfg.S), 0)
    col = iota((cfg.AW, cfg.S), 1)
    if cfg.S == cfg.AW:
        return (row == col).astype(BF)
    target = jnp.full((cfg.AW, cfg.S), -1, jnp.int32)
    for s in range(cfg.slots):
        mine = meta[2 + cfg.docs + s]
        again = jnp.int32(0)
        for e in range(s):
            again = jnp.where(meta[2 + cfg.docs + e] == mine, 1, again)
        base = jnp.where(again == 1, -4 * cfg.AW, mine * RANK)
        target = jnp.where(col // RANK == s, base + col % RANK, target)
    return (row == target).astype(BF)


def block_mean(values, hd):
    width = values.shape[1]
    ones = (iota((width, width), 0) // hd == iota((width, width), 1) // hd).astype(BF)
    high = values.astype(BF)
    low = (values - high.astype(F32)).astype(BF)
    return (mm(high, ones) + mm(low, ones)) * (1.0 / hd)


def swap_halves(values, hd):
    width = values.shape[1]
    half = hd // 2
    first = iota(values.shape, 1) % hd < half
    return jnp.where(first, pltpu.roll(values, width - half, 1), pltpu.roll(values, half, 1))


def lanes(values, copies):
    return jnp.concatenate([values] * copies, axis=1) if copies > 1 else values


def params(**kw):
    return pltpu.CompilerParams(vmem_limit_bytes=VMEM_LIMIT, **kw)


SMEM = pl.BlockSpec(memory_space=pltpu.SMEM)


def call(kernel, outs, ins, scratch=(), flops=0, bytes_accessed=0, name=None):
    return pl.pallas_call(
        kernel,
        out_shape=[jax.ShapeDtypeStruct(s, d) for s, d in outs],
        in_specs=[SMEM] + [pl.BlockSpec(memory_space=pltpu.VMEM)] * (len(ins) - 1),
        out_specs=[pl.BlockSpec(memory_space=pltpu.VMEM)] * len(outs),
        scratch_shapes=list(scratch),
        compiler_params=params(),
        cost_estimate=pl.CostEstimate(
            flops=flops, bytes_accessed=bytes_accessed, transcendentals=0
        ),
        name=name,
    )(*ins)


def pre_kernel(
    cfg, meta, x_ref, gain, wq, wk, wv, aq, ak, av, bq, bk, bv, qg, kg, cos, sin, *refs
):
    G, hd = cfg.G, cfg.hd
    kv_out, q_out = refs[:G], refs[G : 2 * G]
    qraw_ref, kraw_ref, sides_ref, normed_ref, kv_scr, q_scr = refs[2 * G :]
    hi = meta[0] // cfg.lo
    x = x_ref[...].astype(F32)
    rr = lax.rsqrt(jnp.mean(x * x, axis=-1, keepdims=True) + norm_eps)
    normed = (x * rr * gain[...]).astype(BF)
    normed_ref[...] = normed
    mask = adapter_mask(cfg, meta)
    select = slot_select(cfg, meta)
    raws = []
    for i, (w, a, b) in enumerate(((wq, aq, bq), (wk, ak, bk), (wv, av, bv))):
        side = (mask * mm(normed, a[...])).astype(BF)
        sides_ref[i] = mm(side, select).astype(BF)
        raws.append(mm(normed, w[...]) + mm(side, b[...]))
    qraw, kraw, vraw = raws
    qraw_ref[...] = qraw
    kraw_ref[...] = kraw

    def prep(raw, g):
        copies = raw.shape[1] // hd
        scaled = raw * lax.rsqrt(block_mean(raw * raw, hd) + norm_eps) * lanes(g[...], copies)
        per = raw.shape[1] // cos.shape[1]
        return scaled * lanes(cos[...], per) + swap_halves(scaled, hd) * lanes(sin[...], per)

    query = prep(qraw, qg).astype(BF)
    key = prep(kraw, kg).astype(BF)
    value = vraw.astype(BF)
    gw = cfg.groups * hd
    for h in range(G):
        q_scr[h] = query[:, h * gw : (h + 1) * gw]
        kv_scr[h] = jnp.concatenate(
            [key[:, h * hd : (h + 1) * hd], value[:, h * hd : (h + 1) * hd]], axis=1
        )
    for k in range(G):
        kv_out[k][...] = kv_scr[hi ^ k]
        q_out[k][...] = q_scr[hi ^ k]


def load_tiles(cfg, scr, pieces):
    R = cfg.R
    for p, piece in enumerate(pieces):
        for t in range(cfg.NT):
            scr[t, p * R : (p + 1) * R, :] = piece[t * R : (t + 1) * R, :]


def split_pieces(ref, count):
    return [ref.at[i] for i in range(count)]


def token_in_span(cfg, meta, index):
    hi, lo = meta[0] // cfg.lo, meta[0] % cfg.lo
    piece, row = index // cfg.R, index % cfg.R
    j, k = piece // cfg.G, piece % cfg.G
    return row * cfg.n + (hi ^ k) * cfg.lo + (lo ^ j)


def pad_queries(cfg, qq, side):
    hd = cfg.hd
    wide = qq.astype(F32)
    first = iota(wide.shape, 1) < hd
    rolled = pltpu.roll(wide, hd, 1)
    if side == 0:
        parts = [jnp.where(first, wide, 0.0), jnp.where(first, rolled, 0.0)]
    else:
        parts = [jnp.where(first, 0.0, rolled), jnp.where(first, 0.0, wide)]
    return jnp.concatenate(parts, axis=0).astype(BF)


def query_tile_ranges(cfg, starts, qt):
    first = qt * cfg.span
    s_lo = start_of(starts, first) // cfg.span
    s_full = (start_of(starts, first + cfg.span - 1) + cfg.span - 1) // cfg.span
    return s_lo, jnp.minimum(s_full, qt)


def attend_kernel(cfg, meta, *refs):
    G, T, R, hd = cfg.G, cfg.T, cfg.R, cfg.hd
    q_in, own, others = refs[:G], refs[G], refs[G + 1 : G + cfg.lo]
    rest = refs[G + cfg.lo :]
    o_out, o_all, linv, kv_scr, va_scr, q_scr = rest[:G], *rest[G:]
    pieces = split_pieces(own, G)
    for ref in others:
        pieces = pieces + split_pieces(ref, G)
    load_tiles(cfg, kv_scr, pieces)
    load_tiles(cfg, q_scr, q_in)
    starts = doc_starts(cfg, meta)
    QH = cfg.QH
    scale = hd ** (-0.5) * LOG2E
    key_off = token_in_span(cfg, meta, iota((1, cfg.KT), 1))
    row_off = token_in_span(cfg, meta, iota((2 * QH, 1), 0) % QH)
    lane_first = iota((cfg.KT, 2 * hd), 1) < hd

    def fill(t, carry):
        va_scr[t] = jnp.where(lane_first, 1.0, kv_scr[t].astype(F32)).astype(BF)
        return carry

    lax.fori_loop(0, cfg.NT, fill, 0)
    half = iota((QH, 2 * hd), 1) < hd

    def query_tile(qt, carry):
        queries = pad_queries(cfg, q_scr[qt], 0)
        token = row_off + qt * cfg.span
        first_key = start_of(starts, token)
        s_lo, s_full = query_tile_ranges(cfg, starts, qt)

        def tile(s, acc, masked):
            e = jnp.exp2(mm_nt(queries, kv_scr[s]) * scale)
            if masked:
                key_token = key_off + s * cfg.span
                e = jnp.where((key_token <= token) & (key_token >= first_key), e, 0.0)
            return acc + mm(e.astype(BF), va_scr[s])

        acc = jnp.zeros((2 * QH, 2 * hd), F32)
        acc = lax.fori_loop(s_lo, s_full, lambda s, a: tile(s, a, True), acc)
        acc = lax.fori_loop(s_full, qt, lambda s, a: tile(s, a, False), acc)
        acc = tile(qt, acc, True)
        inv0 = 1.0 / acc[:QH]
        inv1 = 1.0 / acc[QH:]
        out0 = pltpu.roll(acc[:QH], hd, 1) * inv0
        out1 = acc[QH:] * pltpu.roll(inv1, hd, 1)
        out = jnp.where(half, out0, out1).astype(BF)
        inv = jnp.where(half, inv0, pltpu.roll(inv1, hd, 1))
        rows = pl.ds(pl.multiple_of(qt * R, R), R)
        for k in range(G):
            o_out[k][rows, :] = out[k * R : (k + 1) * R]
            o_all[k, rows, :] = out[k * R : (k + 1) * R]
            linv[k, rows, :] = inv[k * R : (k + 1) * R]
        return carry

    lax.fori_loop(0, cfg.NT, query_tile, 0)


def scale_kernel(cfg, meta, *refs):
    G = cfg.G
    for k in range(G):
        refs[G + 1][k] = (refs[k][...].astype(F32) * refs[G][k]).astype(BF)


def grad_query_kernel(cfg, meta, *refs):
    G, T, R, hd = cfg.G, cfg.T, cfg.R, cfg.hd
    q_in, own, others = refs[:G], refs[G], refs[G + 1 : G + cfg.lo]
    go_ref, o_ref = refs[G + cfg.lo : G + cfg.lo + 2]
    rest = refs[G + cfg.lo + 2 :]
    dq_out, kv_scr, q_scr, go_scr, o_scr = rest[:G], *rest[G:]
    pieces = split_pieces(own, G)
    for ref in others:
        pieces = pieces + split_pieces(ref, G)
    load_tiles(cfg, kv_scr, pieces)
    load_tiles(cfg, q_scr, q_in)
    load_tiles(cfg, go_scr, split_pieces(go_ref, G))
    load_tiles(cfg, o_scr, split_pieces(o_ref, G))
    starts = doc_starts(cfg, meta)
    QH = cfg.QH
    scale = hd ** (-0.5) * LOG2E
    key_off = token_in_span(cfg, meta, iota((1, cfg.KT), 1))
    row_off = token_in_span(cfg, meta, iota((2 * QH, 1), 0) % QH)
    half = iota((QH, 2 * hd), 1) < hd

    def query_tile(qt, carry):
        queries = pad_queries(cfg, q_scr[qt], 0)
        grads = pad_queries(cfg, go_scr[qt], 1)
        prod = go_scr[qt].astype(F32) * o_scr[qt].astype(F32)
        delta = jnp.concatenate(
            [
                jnp.sum(jnp.where(half, prod, 0.0), axis=1, keepdims=True),
                jnp.sum(jnp.where(half, 0.0, prod), axis=1, keepdims=True),
            ],
            axis=0,
        )
        token = row_off + qt * cfg.span
        first_key = start_of(starts, token)
        s_lo, s_full = query_tile_ranges(cfg, starts, qt)

        def tile(s, acc, masked):
            kv = kv_scr[s]
            e = jnp.exp2(mm_nt(queries, kv) * scale)
            if masked:
                key_token = key_off + s * cfg.span
                e = jnp.where((key_token <= token) & (key_token >= first_key), e, 0.0)
            ds = e * (mm_nt(grads, kv) - delta)
            return acc + mm(ds.astype(BF), kv)

        acc = jnp.zeros((2 * QH, 2 * hd), F32)
        acc = lax.fori_loop(s_lo, s_full, lambda s, a: tile(s, a, True), acc)
        acc = lax.fori_loop(s_full, qt, lambda s, a: tile(s, a, False), acc)
        acc = tile(qt, acc, True)
        out = jnp.where(half, acc[:QH], pltpu.roll(acc[QH:], hd, 1)) * hd ** (-0.5)
        out = out.astype(BF)
        rows = pl.ds(pl.multiple_of(qt * R, R), R)
        for k in range(G):
            dq_out[k][rows, :] = out[k * R : (k + 1) * R]
        return carry

    lax.fori_loop(0, cfg.NT, query_tile, 0)


def grad_key_kernel(cfg, meta, *refs):
    G, T, R, hd, lo = cfg.G, cfg.T, cfg.R, cfg.hd, cfg.lo
    own = refs[0]
    q_refs, go_refs, o_refs = (refs[1 + i * lo : 1 + (i + 1) * lo] for i in range(3))
    rest = refs[1 + 3 * lo :]
    dkv_out, kv_scr, q_scr, go_scr, o_scr, delta_scr = rest[:G], *rest[G:]
    load_tiles(cfg, kv_scr, split_pieces(own, G))
    for scr, group in ((q_scr, q_refs), (go_scr, go_refs), (o_scr, o_refs)):
        load_tiles(cfg, scr, [piece for ref in group for piece in split_pieces(ref, G)])
    starts = doc_starts(cfg, meta)
    QH = cfg.QH
    scale = hd ** (-0.5) * LOG2E
    pick = (iota((16, 2 * hd), 1) // hd == iota((16, 2 * hd), 0)).astype(BF)

    def deltas(t, carry):
        prod = go_scr[t].astype(F32) * o_scr[t].astype(F32)
        high = prod.astype(BF)
        low = (prod - high.astype(F32)).astype(BF)
        delta_scr[t] = mm_nt(pick, high) + mm_nt(pick, low)
        return carry

    lax.fori_loop(0, cfg.NT, deltas, 0)
    query_off = token_in_span(cfg, meta, iota((1, cfg.KT), 1))
    row_off = token_in_span(cfg, meta, iota((2 * QH, 1), 0) % QH)
    first = iota((QH, 2 * hd), 1) < hd

    def key_tile(kt, carry):
        kv = kv_scr[kt].astype(F32)
        rolled = pltpu.roll(kv, hd, 1)
        keys = jnp.concatenate(
            [jnp.where(first, kv, 0.0), jnp.where(first, 0.0, rolled)], axis=0
        ).astype(BF)
        values = jnp.concatenate(
            [jnp.where(first, rolled, 0.0), jnp.where(first, 0.0, kv)], axis=0
        ).astype(BF)
        key_token = row_off + kt * cfg.span
        end_first = end_of(starts, kt * cfg.span)
        end_last = end_of(starts, (kt + 1) * cfg.span - 1)
        q_full = jnp.maximum(end_first // cfg.span, kt + 1)
        q_stop = (end_last - 1) // cfg.span + 1

        def tile(t, acc, masked):
            grad_keys, grad_values = acc
            queries, grads = q_scr[t], go_scr[t]
            e = jnp.exp2(mm_nt(keys, queries) * scale)
            if masked:
                token = query_off + t * cfg.span
                e = jnp.where((key_token <= token) & (key_token >= start_of(starts, token)), e, 0.0)
            dp = mm_nt(values, grads)
            delta = delta_scr[t]
            ds = jnp.concatenate(
                [
                    (e[:QH] * (dp[:QH] - delta[0:1])).astype(BF),
                    (e[QH:] * (dp[QH:] - delta[1:2])).astype(BF),
                ],
                axis=0,
            )
            return grad_keys + mm(ds, queries), grad_values + mm(e.astype(BF), grads)

        zero = jnp.zeros((2 * QH, 2 * hd), F32)
        acc = tile(kt, (zero, zero), True)
        acc = lax.fori_loop(kt + 1, q_full, lambda t, a: tile(t, a, False), acc)
        acc = lax.fori_loop(q_full, q_stop, lambda t, a: tile(t, a, True), acc)
        grad_keys, grad_values = acc
        gk = (grad_keys[:QH] + pltpu.roll(grad_keys[QH:], hd, 1)) * hd ** (-0.5)
        gv = pltpu.roll(grad_values[:QH], hd, 1) + grad_values[QH:]
        out = jnp.where(first, gk, gv).astype(BF)
        rows = pl.ds(pl.multiple_of(kt * R, R), R)
        for k in range(G):
            dkv_out[k][rows, :] = out[k * R : (k + 1) * R]
        return carry

    lax.fori_loop(0, cfg.NT, key_tile, 0)


def place_pieces(cfg, hi, scr, pieces):
    w = pieces[0].shape[1]
    for k in range(cfg.G):
        at = pl.multiple_of((hi ^ k) * w, w)
        scr[:, pl.ds(at, w)] = pieces[k][...]


def out_kernel(cfg, meta, *refs):
    G = cfg.G
    wo, ao, part, attn = refs[G:]
    place_pieces(cfg, meta[0] // cfg.lo, attn, refs[:G])
    rows = attn[...]
    part[:, : cfg.D] = mm(rows, wo[...]).astype(BF)
    part[:, cfg.D :] = mm(rows, ao[...]).astype(BF)


def ffn_kernel(
    cfg, steps, meta, x_ref, own, other, bo, gain, wg, wu, wd, bg, bu, ag, au, ad, bd, cot_ref,
    mixed_ref, dfn_ref, part_ref, bgate, bup, adown, akeep, asend, oside,
    fn, sg, su, gsd, sgt, sut, gsdt, down, side_sum, dfn, gsg, gsu, a_scr,
):
    step = pl.program_id(0)
    S, D = cfg.S, cfg.D

    @pl.when(step == 0)
    def _():
        mask = adapter_mask(cfg, meta)
        select = slot_select(cfg, meta)
        total = own[...].astype(F32) + other[...].astype(F32)
        out_side = (mask * total[:, D:]).astype(BF)
        oside[...] = mm(out_side, select).astype(BF)
        mixed = x_ref[...].astype(F32) + total[:, :D] + mm(out_side, bo[...])
        mixed_ref[...] = mixed
        rr = lax.rsqrt(jnp.mean(mixed * mixed, axis=-1, keepdims=True) + norm_eps)
        normed = (mixed * rr * gain[...]).astype(BF)
        fn[...] = normed
        side_g = (mask * mm(normed, ag[...])).astype(BF)
        side_u = (mask * mm(normed, au[...])).astype(BF)
        grad_side = (mask * mm_nt(cot_ref[...], bd[...])).astype(BF)
        sg[...] = side_g
        su[...] = side_u
        gsd[...] = grad_side
        sgt[...] = mm(side_g, select).T.astype(BF)
        sut[...] = mm(side_u, select).T.astype(BF)
        gsdt[...] = mm(grad_side, select).T.astype(BF)
        down[...] = jnp.zeros_like(down)
        side_sum[...] = jnp.zeros_like(side_sum)
        dfn[...] = jnp.zeros_like(dfn)
        gsg[...] = jnp.zeros_like(gsg)
        gsu[...] = jnp.zeros_like(gsu)

    normed = fn[...]
    gate = mm(normed, wg[...]) + mm(sg[...], bg[...])
    upper = mm(normed, wu[...]) + mm(su[...], bu[...])
    grad_hidden = mm_nt(cot_ref[...], wd[...]) + mm_nt(gsd[...], ad[...])
    sigma = 1.0 / (1.0 + jnp.exp(-gate))
    silu = gate * sigma
    hidden = (silu * upper).astype(BF)
    grad_gate = (grad_hidden * upper * (sigma + silu * (1.0 - sigma))).astype(BF)
    grad_upper = (grad_hidden * silu).astype(BF)
    down[...] += mm(hidden, wd[...])
    side_sum[...] += mm(hidden, ad[...])
    dfn[...] += mm_nt(grad_gate, wg[...]) + mm_nt(grad_upper, wu[...])
    gsg[...] += mm_nt(grad_gate, bg[...])
    gsu[...] += mm_nt(grad_upper, bu[...])
    bgate[...] = mm(sgt[...], grad_gate).astype(BF)
    bup[...] = mm(sut[...], grad_upper).astype(BF)
    adown[...] = mm(gsdt[...], hidden).astype(BF)

    @pl.when(step == steps - 1)
    def _():
        mask = adapter_mask(cfg, meta)
        select = slot_select(cfg, meta)
        side_g = (mask * gsg[...]).astype(BF)
        side_u = (mask * gsu[...]).astype(BF)
        dfn_ref[...] = (dfn[...] + mm_nt(side_g, ag[...]) + mm_nt(side_u, au[...])).astype(BF)
        part_ref[:, :D] = down[...].astype(BF)
        part_ref[:, D:] = side_sum[...].astype(BF)
        a_scr[:S, :] = mm(mm(side_g, select).T.astype(BF), fn[...])
        a_scr[S:, :] = mm(mm(side_u, select).T.astype(BF), fn[...])
        half = D // 2
        keep = pl.ds(pl.multiple_of(meta[1] * half, half), half)
        send = pl.ds(pl.multiple_of((1 - meta[1]) * half, half), half)
        akeep[...] = a_scr[:, keep].astype(BF)
        asend[...] = a_scr[:, send].astype(BF)


def ffn_call(cfg, meta, x, own, other, bo, gain, wg, wu, wd, bg, bu, ag, au, ad, bd, cot):
    T, D, F, AW, S = cfg.T, cfg.D, cfg.F, cfg.AW, cfg.S
    tile = 256
    steps = F // tile
    whole = lambda shape: pl.BlockSpec(shape, lambda i: (0,) * len(shape))
    cols = lambda rows: pl.BlockSpec((rows, tile), lambda i: (0, i))
    rows = lambda width: pl.BlockSpec((tile, width), lambda i: (i, 0))
    outs = [
        ((T, D), F32),
        ((T, D), BF),
        ((T, D + AW), BF),
        ((S, F), BF),
        ((S, F), BF),
        ((S, F), BF),
        ((2 * S, D // 2), BF),
        ((2 * S, D // 2), BF),
        ((T, S), BF),
    ]
    out_specs = [
        whole((T, D)),
        whole((T, D)),
        whole((T, D + AW)),
        cols(S),
        cols(S),
        cols(S),
        whole((2 * S, D // 2)),
        whole((2 * S, D // 2)),
        whole((T, S)),
    ]
    flops = 2 * T * D * F * 6
    return pl.pallas_call(
        functools.partial(ffn_kernel, cfg, steps),
        grid=(steps,),
        out_shape=[jax.ShapeDtypeStruct(s, d) for s, d in outs],
        in_specs=[
            SMEM,
            whole((T, D)),
            whole((T, D + AW)),
            whole((T, D + AW)),
            whole((AW, D)),
            whole((1, D)),
            cols(D),
            cols(D),
            rows(D),
            cols(AW),
            cols(AW),
            whole((D, AW)),
            whole((D, AW)),
            rows(AW),
            whole((AW, D)),
            whole((T, D)),
        ],
        out_specs=out_specs,
        scratch_shapes=[
            pltpu.VMEM((T, D), BF),
            pltpu.VMEM((T, AW), BF),
            pltpu.VMEM((T, AW), BF),
            pltpu.VMEM((T, AW), BF),
            pltpu.VMEM((S, T), BF),
            pltpu.VMEM((S, T), BF),
            pltpu.VMEM((S, T), BF),
            pltpu.VMEM((T, D), F32),
            pltpu.VMEM((T, AW), F32),
            pltpu.VMEM((T, D), F32),
            pltpu.VMEM((T, AW), F32),
            pltpu.VMEM((T, AW), F32),
            pltpu.VMEM((2 * S, D), F32),
        ],
        compiler_params=params(dimension_semantics=("arbitrary",)),
        cost_estimate=pl.CostEstimate(
            flops=flops, bytes_accessed=3 * D * F * 2, transcendentals=T * F
        ),
        name="ffn",
    )(meta, x, own, other, bo, gain, wg, wu, wd, bg, bu, ag, au, ad, bd, cot)


def mixed_grad_kernel(cfg, meta, *refs):
    G, D = cfg.G, cfg.D
    mixed_ref, own, other, cot, gain = refs[:5]
    o_in = refs[5 : 5 + G]
    wo, ao, bo, oside = refs[5 + G : 9 + G]
    rest = refs[9 + G :]
    gm_ref, ograds, go_out, attn, go_scr, gm_scr = rest[0], rest[1], rest[2 : 2 + G], *rest[2 + G :]
    hi = meta[0] // cfg.lo
    mixed = mixed_ref[...]
    w = (own[...].astype(F32) + other[...].astype(F32)) * gain[...]
    rr = lax.rsqrt(jnp.mean(mixed * mixed, axis=-1, keepdims=True) + norm_eps)
    inner = jnp.mean(w * mixed, axis=-1, keepdims=True)
    gm = cot[...].astype(F32) + rr * w - (rr * rr * rr * inner) * mixed
    gm_ref[...] = gm
    gmb = gm.astype(BF)
    gm_scr[...] = gmb
    mask = adapter_mask(cfg, meta)
    select = slot_select(cfg, meta)
    grad_side = (mask * mm_nt(gmb, bo[...])).astype(BF)
    go = (mm_nt(gmb, wo[...]) + mm_nt(grad_side, ao[...])).astype(BF)
    w = cfg.groups * cfg.hd
    for h in range(G):
        go_scr[h] = go[:, h * w : (h + 1) * w]
    for k in range(G):
        go_out[k][...] = go_scr[hi ^ k]
    place_pieces(cfg, hi, attn, o_in)
    ograds[0] = mm(mm(grad_side, select).T.astype(BF), attn[...]).astype(BF)
    half = D // 2
    mine = gm_scr[:, pl.ds(pl.multiple_of(meta[1] * half, half), half)]
    ograds[1] = mm(oside[...].astype(F32).T.astype(BF), mine).astype(BF)


def output_kernel(cfg, meta, mixed, own, other, bd, cot, out_ref, dgrad):
    D = cfg.D
    total = own[...].astype(F32) + other[...].astype(F32)
    mask = adapter_mask(cfg, meta)
    side = (mask * total[:, D:]).astype(BF)
    out_ref[...] = (mixed[...] + total[:, :D] + mm(side, bd[...])).astype(BF)
    half = D // 2
    mine = cot[:, pl.ds(pl.multiple_of(meta[1] * half, half), half)]
    dgrad[...] = mm(mm(side, slot_select(cfg, meta)).T.astype(BF), mine).astype(BF)


def qkv_grad_kernel(cfg, meta, *refs):
    G, D, S, hd = cfg.G, cfg.D, cfg.S, cfg.hd
    dq_in, dkv_in = refs[:G], refs[G : 2 * G]
    (
        normed, qraw, kraw, sides, cos, sin, qg, kg, wq, wk, wv, aq, ak, av, bq, bk, bv,
        part, bgrad, akeep, asend, dq_scr, dkv_scr, a_scr,
    ) = refs[2 * G :]
    hi = meta[0] // cfg.lo
    place_pieces(cfg, hi, dq_scr, dq_in)
    place_pieces(cfg, hi, dkv_scr, dkv_in)
    mask = adapter_mask(cfg, meta)
    select = slot_select(cfg, meta)

    def back(grad, raw, g):
        copies = raw.shape[1] // hd
        per = raw.shape[1] // cos.shape[1]
        un = grad * lanes(cos[...], per) - swap_halves(grad, hd) * lanes(sin[...], per)
        w = un * lanes(g[...], copies)
        rr = lax.rsqrt(block_mean(raw * raw, hd) + norm_eps)
        return rr * w - rr * rr * rr * raw * block_mean(w * raw, hd)

    dkv = dkv_scr[...]
    dk = jnp.concatenate([dkv[:, 2 * h * hd : (2 * h + 1) * hd] for h in range(G)], axis=1)
    dv = jnp.concatenate([dkv[:, (2 * h + 1) * hd : (2 * h + 2) * hd] for h in range(G)], axis=1)
    gq = back(dq_scr[...].astype(F32), qraw[...], qg).astype(BF)
    gk = back(dk.astype(F32), kraw[...], kg).astype(BF)
    total = jnp.zeros((cfg.T, D), F32)
    at = 0
    for i, (g, w, a, b) in enumerate(((gq, wq, aq, bq), (gk, wk, ak, bk), (dv, wv, av, bv))):
        grad_side = (mask * mm_nt(g, b[...])).astype(BF)
        total = total + mm_nt(g, w[...]) + mm_nt(grad_side, a[...])
        a_scr[i * S : (i + 1) * S, :] = mm(mm(grad_side, select).T.astype(BF), normed[...])
        width = g.shape[1]
        bgrad[:, at : at + width] = mm(sides[i].astype(F32).T.astype(BF), g).astype(BF)
        at = at + width
    part[...] = total.astype(BF)
    half = D // 2
    keep = pl.ds(pl.multiple_of(meta[1] * half, half), half)
    send = pl.ds(pl.multiple_of((1 - meta[1]) * half, half), half)
    akeep[...] = a_scr[:, keep].astype(BF)
    asend[...] = a_scr[:, send].astype(BF)


def input_grad_kernel(cfg, meta, x_ref, gain, gm, own, other, out):
    x = x_ref[...].astype(F32)
    w = (own[...].astype(F32) + other[...].astype(F32)) * gain[...]
    rr = lax.rsqrt(jnp.mean(x * x, axis=-1, keepdims=True) + norm_eps)
    inner = jnp.mean(w * x, axis=-1, keepdims=True)
    out[...] = (gm[...] + rr * w - (rr * rr * rr * inner) * x).astype(BF)


class Units:
    def __init__(self, cfg, shared, private):
        self.n = cfg.n
        self.high = cfg.S // 16
        self.us = self._layout(shared, 0)
        self.up = self._layout(private, 0)
        self.u = self.us + self.up
        self.shared, self.private = shared, private

    def _layout(self, widths, _):
        count = sum(w // 128 for w in widths) * self.high
        return -(-count // self.n)

    def places(self, which):
        widths, per, base = (
            (self.shared, self.us, 0) if which == 0 else (self.private, self.up, self.us)
        )
        at, out = 0, []
        for w in widths:
            spots = []
            for c in range(w // 128):
                for a in range(self.high):
                    spots.append((at // per, base + at % per, a, c))
                    at += 1
            out.append(spots)
        return out

    def spare(self):
        out = []
        for widths, per, base in ((self.shared, self.us, 0), (self.private, self.up, self.us)):
            count = sum(w // 128 for w in widths) * self.high
            out += [(i // per, base + i % per) for i in range(count, per * self.n)]
        return out


def pack(units, idx, out, arrays):
    for spots, values in zip(units.places(0) + units.places(1), arrays):
        for chunk, off, a, c in spots:
            out[chunk ^ idx, off] = values[a * 16 : a * 16 + 16, c * 128 : c * 128 + 128]
    for chunk, off in units.spare():
        out[chunk ^ idx, off] = jnp.zeros((16, 128), BF)


def add_halves(keep, got, count):
    total = (keep[...].astype(F32) + got[...].astype(F32)).astype(BF)
    rows = total.shape[0] // count
    return [total[i * rows : (i + 1) * rows] for i in range(count)]


def pack_ffn_kernel(cfg, units, meta, keep, got, bdown, ograds, bgate, bup, adown, out):
    shared = add_halves(keep, got, 2) + [bdown[...], ograds[1]]
    pack(units, meta[0], out, shared + [bgate[...], bup[...], adown[...], ograds[0]])


def pack_qkv_kernel(cfg, units, qw, kw, meta, keep, got, bgrad, out):
    private = [bgrad[:, :qw], bgrad[:, qw : qw + kw], bgrad[:, qw + kw :]]
    pack(units, meta[0], out, add_halves(keep, got, 3) + private)


def unpack(units, idx, ref, spots, base=0):
    cols = {}
    for chunk, off, a, c in spots:
        cols.setdefault(c, []).append(ref[chunk ^ idx, off - base])
    return jnp.concatenate([jnp.concatenate(cols[c], axis=0) for c in sorted(cols)], axis=1)


def expand_kernel(cfg, units, plan, meta, own, other, *outs):
    idx, wa = meta[0], meta[1]
    select = slot_select(cfg, meta)

    def write(out, values, transposed, at):
        full = mm(select, values)
        if transposed:
            out[at : at + full.shape[1], :] = full.T
        else:
            out[:, at : at + full.shape[1]] = full

    for (which, i, transposed), out in zip(plan, outs):
        spots = units.places(which)[i]
        mine = unpack(units, idx, own, spots)
        if which == 1:
            write(out, mine, transposed, 0)
        else:
            theirs = unpack(units, idx, other, spots)
            width = mine.shape[1]
            write(out, jnp.where(wa == 0, mine, theirs), transposed, 0)
            write(out, jnp.where(wa == 0, theirs, mine), transposed, width)


def swap_cores(value):
    return lax.ppermute(value, "wa", [(0, 1), (1, 0)])


def permute(cfg, value, bits):
    return lax.ppermute(value, "ctx", [(i, i ^ bits) for i in range(cfg.n)])


def sum_chunks(cfg, cur):
    bits = []
    size = cfg.n // 2
    while size >= 1:
        half = cur.shape[0] // 2
        got = permute(cfg, cur[half:], size)
        cur = (cur[:half].astype(F32) + got.astype(F32)).astype(BF)
        bits.append(size)
        size //= 2
    for size in reversed(bits):
        cur = jnp.concatenate([cur, permute(cfg, cur, size)], axis=0)
    return cur


def per_device(
    hidden_in, attn_gain, query_weight, key_weight, value_weight, query_gain, key_gain, out_weight,
    ffn_gain, gate_weight, up_weight, down_weight, query_adapt_in, query_adapt_out, key_adapt_in,
    key_adapt_out, value_adapt_in, value_adapt_out, out_adapt_in, out_adapt_out, gate_adapt_in,
    gate_adapt_out, up_adapt_in, up_adapt_out, down_adapt_in, down_adapt_out, document_extra,
    document_adapter, cotangent,
):
    head_dim = query_gain.shape[0]
    cfg = Cfg(
        tokens=hidden_in.shape[0],
        n_ctx=lax.axis_size("ctx"),
        heads_kv=key_weight.shape[1] // head_dim,
        groups=query_weight.shape[1] // key_weight.shape[1],
        head_dim=head_dim,
        docs=document_extra.shape[0],
        adapt_width=query_adapt_in.shape[1],
        width=hidden_in.shape[2],
        hidden=gate_weight.shape[1],
    )
    T, D, G, S, AW, n, lo = cfg.T, cfg.D, cfg.G, cfg.S, cfg.AW, cfg.n, cfg.lo
    gw = cfg.groups * head_dim
    QW, KW = query_weight.shape[1], key_weight.shape[1]
    ctx_index = lax.axis_index("ctx")
    meta = jnp.concatenate(
        [
            jnp.stack([ctx_index, lax.axis_index("wa")]).astype(jnp.int32),
            document_extra,
            document_adapter,
        ]
    )
    x = hidden_in.reshape(T, D)
    cot = cotangent.reshape(T, D)
    gain_a = attn_gain.reshape(1, D)
    gain_f = ffn_gain.reshape(1, D)
    qg = query_gain.reshape(1, head_dim)
    kg = key_gain.reshape(1, head_dim)

    token = jnp.arange(T, dtype=jnp.int32) * n + ctx_index
    lengths = document_extra + (DOC_MIN - 1)
    starts = jnp.cumsum(lengths) - lengths
    position = token - jnp.max(jnp.where(token[:, None] >= starts[None, :], starts[None, :], 0), axis=1)
    half = head_dim // 2
    lane = jnp.arange(2 * head_dim, dtype=jnp.int32)
    inverse = jnp.exp((lane % half).astype(F32) * (-2.0 * math.log(theta_base) / head_dim))
    angle = position.astype(F32)[:, None] * inverse[None, :]
    cos = jnp.cos(angle)
    sin = jnp.sin(angle) * jnp.where(lane % head_dim < half, -1.0, 1.0)[None, :]

    piece = ((T, gw), BF)
    pre = call(
        functools.partial(pre_kernel, cfg),
        [piece] * (2 * G) + [((T, QW), F32), ((T, KW), F32), ((3, T, S), BF), ((T, D), BF)],
        [
            meta, x, gain_a, query_weight, key_weight, value_weight, query_adapt_in, key_adapt_in,
            value_adapt_in, query_adapt_out, key_adapt_out, value_adapt_out, qg, kg, cos, sin,
        ],
        scratch=[pltpu.VMEM((G, T, gw), BF), pltpu.VMEM((G, T, gw), BF)],
        flops=2 * T * D * (QW + 2 * KW),
        bytes_accessed=2 * D * (QW + 2 * KW),
        name="pre",
    )
    kv_send, q_send = pre[:G], pre[G : 2 * G]
    qraw, kraw, sides, normed = pre[2 * G :]

    def to_heads(pieces):
        return [pieces[0]] + [permute(cfg, pieces[k], k * lo) for k in range(1, G)]

    def to_plane(value):
        return [value] + [permute(cfg, value, j) for j in range(1, lo)]

    kv = to_plane(jnp.stack(to_heads(kv_send)))
    q = to_heads(q_send)
    tiles = lambda rows: pltpu.VMEM((cfg.NT, rows, gw), BF)
    attn = call(
        functools.partial(attend_kernel, cfg),
        [piece] * G + [((G, T, gw), BF), ((G, T, gw), F32)],
        [meta] + q + kv,
        scratch=[tiles(cfg.KT), tiles(cfg.KT), tiles(cfg.QH)],
        flops=2 * T * G * T * n * 2 * gw,
        name="attend",
    )
    o_send, o_all, linv = attn[:G], attn[G], attn[G + 1]
    o = to_heads(o_send)
    (opart,) = call(
        functools.partial(out_kernel, cfg),
        [((T, D + AW), BF)],
        [meta] + o + [out_weight, out_adapt_in],
        scratch=[pltpu.VMEM((T, QW), BF)],
        flops=2 * T * D * QW,
        bytes_accessed=2 * D * QW,
        name="out_proj",
    )
    ffn = ffn_call(
        cfg, meta, x, opart, swap_cores(opart), out_adapt_out, gain_f, gate_weight, up_weight,
        down_weight, gate_adapt_out, up_adapt_out, gate_adapt_in, up_adapt_in, down_adapt_in,
        down_adapt_out, cot,
    )
    mixed, dfn, dpart, bgate, bup, adown, akeep, asend, oside = ffn
    mg = call(
        functools.partial(mixed_grad_kernel, cfg),
        [((T, D), F32), ((2, S, D // 2), BF)] + [piece] * G,
        [meta, mixed, dfn, swap_cores(dfn), cot, gain_f]
        + o
        + [out_weight, out_adapt_in, out_adapt_out, oside],
        scratch=[pltpu.VMEM((T, QW), BF), pltpu.VMEM((G, T, gw), BF), pltpu.VMEM((T, D), BF)],
        flops=2 * T * D * QW,
        bytes_accessed=2 * D * QW,
        name="mixed_grad",
    )
    grad_mixed, ograds, go_send = mg[0], mg[1], mg[2:]
    go_heads = to_heads(go_send)
    (go_all,) = call(
        functools.partial(scale_kernel, cfg),
        [((G, T, gw), BF)],
        [meta] + go_heads + [linv],
        bytes_accessed=8 * G * T * gw,
        name="scale",
    )
    q_plane = to_plane(jnp.stack(q))
    o_plane = to_plane(o_all)
    go_plane = to_plane(go_all)
    dq_send = call(
        functools.partial(grad_query_kernel, cfg),
        [piece] * G,
        [meta] + q + kv + [go_all, o_all],
        scratch=[tiles(cfg.KT), tiles(cfg.QH), tiles(cfg.QH), tiles(cfg.QH)],
        flops=2 * T * G * T * n * 3 * gw,
        name="grad_query",
    )
    dq = to_heads(dq_send)
    dkv_send = call(
        functools.partial(grad_key_kernel, cfg),
        [piece] * G,
        [meta, kv[0]] + q_plane + go_plane + o_plane,
        scratch=[tiles(cfg.QH), tiles(cfg.KT), tiles(cfg.KT), tiles(cfg.KT)]
        + [pltpu.VMEM((cfg.NT, 16, cfg.KT), F32)],
        flops=2 * T * G * T * n * 4 * gw,
        name="grad_key",
    )
    dkv = to_heads(dkv_send)

    out_rows, bdown = call(
        functools.partial(output_kernel, cfg),
        [((T, D), BF), ((S, D // 2), BF)],
        [meta, mixed, dpart, swap_cores(dpart), down_adapt_out, cot],
        name="output",
    )
    units_f = Units(cfg, [D // 2] * 4, [cfg.F] * 3 + [QW])
    qkv = call(
        functools.partial(qkv_grad_kernel, cfg),
        [((T, D), BF), ((S, QW + 2 * KW), BF), ((3 * S, D // 2), BF), ((3 * S, D // 2), BF)],
        [meta]
        + dq
        + dkv
        + [
            normed, qraw, kraw, sides, cos, sin, qg, kg, query_weight, key_weight, value_weight,
            query_adapt_in, key_adapt_in, value_adapt_in, query_adapt_out, key_adapt_out,
            value_adapt_out,
        ],
        scratch=[
            pltpu.VMEM((T, QW), BF),
            pltpu.VMEM((T, 2 * KW), BF),
            pltpu.VMEM((3 * S, D), F32),
        ],
        flops=2 * T * D * (QW + 2 * KW),
        bytes_accessed=2 * D * (QW + 2 * KW),
        name="qkv_grad",
    )
    dnormed, bqkv, akeep_q, asend_q = qkv
    (input_rows,) = call(
        functools.partial(input_grad_kernel, cfg),
        [((T, D), BF)],
        [meta, x, gain_a, grad_mixed, dnormed, swap_cores(dnormed)],
        name="input_grad",
    )

    def reduce_and_expand(units, pack_in, pack_kern, plan, outs, tag):
        (buffer,) = call(pack_kern, [((n, units.u, 16, 128), BF)], [meta] + pack_in, name="pack_" + tag)
        total = sum_chunks(cfg, buffer)
        theirs = swap_cores(total[:, : units.us])
        return call(
            functools.partial(expand_kernel, cfg, units, plan),
            outs,
            [meta, total, theirs],
            name="expand_" + tag,
        )

    grads_f = reduce_and_expand(
        units_f,
        [akeep, swap_cores(asend), bdown, ograds, bgate, bup, adown],
        functools.partial(pack_ffn_kernel, cfg, units_f),
        [(0, 0, True), (0, 1, True), (0, 2, False), (0, 3, False)]
        + [(1, 0, False), (1, 1, False), (1, 2, True), (1, 3, True)],
        [((D, AW), F32), ((D, AW), F32), ((AW, D), F32), ((AW, D), F32)]
        + [((AW, cfg.F), F32), ((AW, cfg.F), F32), ((cfg.F, AW), F32), ((QW, AW), F32)],
        "ffn",
    )
    gate_in, up_in, down_out, out_out, gate_out, up_out, down_in, out_in = grads_f
    units_q = Units(cfg, [D // 2] * 3, [QW, KW, KW])
    grads_q = reduce_and_expand(
        units_q,
        [akeep_q, swap_cores(asend_q), bqkv],
        functools.partial(pack_qkv_kernel, cfg, units_q, QW, KW),
        [(0, 0, True), (0, 1, True), (0, 2, True), (1, 0, False), (1, 1, False), (1, 2, False)],
        [((D, AW), F32)] * 3 + [((AW, QW), F32), ((AW, KW), F32), ((AW, KW), F32)],
        "qkv",
    )
    query_in, key_in, value_in, query_out, key_out, value_out = grads_q
    return (
        out_rows.reshape(T, 1, D),
        input_rows.reshape(T, 1, D),
        query_in,
        query_out,
        key_in,
        key_out,
        value_in,
        value_out,
        out_in,
        out_out,
        gate_in,
        gate_out,
        up_in,
        up_out,
        down_in,
        down_out,
    )


def solution(mesh):
    return jax.shard_map(
        per_device,
        mesh=mesh,
        in_specs=(
            P(None, "ctx", None), P(), P(None, "wa"), P(None, "wa"), P(None, "wa"), P(), P(),
            P("wa", None), P(), P(None, "wa"), P(None, "wa"), P("wa", None), P(), P(None, "wa"),
            P(), P(None, "wa"), P(), P(None, "wa"), P("wa", None), P(), P(), P(None, "wa"), P(),
            P(None, "wa"), P("wa", None), P(), P(), P(), P(None, "ctx", None),
        ),
        out_specs=(
            P(None, "ctx", None), P(None, "ctx", None), P(), P(None, "wa"), P(), P(None, "wa"), P(),
            P(None, "wa"), P("wa", None), P(), P(), P(None, "wa"), P(), P(None, "wa"),
            P("wa", None), P(),
        ),
        check_vma=False,
    )
```

```python
import functools
import math

import jax
import jax.numpy as jnp
from jax import lax
from jax.experimental import pallas as pl
from jax.experimental.pallas import tpu as pltpu
from jax.sharding import PartitionSpec as P

RANK = 16
DOC_MIN = 200

norm_eps = 1e-05
theta_base = 1000000.0
BF = jnp.bfloat16
F32 = jnp.float32
LOG2E = 1.4426950408889634
VMEM_SMALL = 20 * 1024 * 1024
VMEM_LARGE = 56 * 1024 * 1024


def mm(left, right):
    return jnp.dot(left, right, preferred_element_type=F32)


def mm_nt(left, right):
    return lax.dot_general(left, right, (((1,), (1,)), ((), ())), preferred_element_type=F32)


def mm_tn(left, right):
    return lax.dot_general(left, right, (((0,), (0,)), ((), ())), preferred_element_type=F32)


def iota(shape, dim):
    return lax.broadcasted_iota(jnp.int32, shape, dim)


class Cfg:
    def __init__(self, tokens, n_ctx, heads_kv, groups, head_dim, docs, adapt_width, width, hidden):
        self.T = tokens
        self.n = n_ctx
        self.G = heads_kv
        self.lo = n_ctx // heads_kv
        self.groups = groups
        self.hd = head_dim
        self.docs = docs
        self.AW = adapt_width
        self.slots = min(docs, adapt_width // RANK)
        self.S = self.slots * RANK
        self.D = width
        self.F = hidden
        self.R = max(16, min(tokens, 512 // n_ctx))
        self.NT = tokens // self.R
        self.span = self.R * n_ctx
        self.QH = self.G * self.R
        self.KT = n_ctx * self.R


class Meta:
    def __init__(self, extra, adapter):
        self.refs, self.docs = (extra, adapter), extra.shape[0]

    def __getitem__(self, i):
        if i < 2:
            return lax.axis_index(("ctx", "wa")[i])
        return self.refs[(i - 2) // self.docs][(i - 2) % self.docs]


def with_meta(kernel):
    return lambda extra, adapter, *refs: kernel(Meta(extra, adapter), *refs)


def doc_starts(cfg, meta):
    out = [jnp.int32(0)]
    for j in range(cfg.docs):
        out.append(out[-1] + meta[2 + j] + (DOC_MIN - 1))
    return out


def start_of(starts, token):
    out = jnp.zeros_like(token)
    for s in starts[1:-1]:
        out = jnp.where(token >= s, s, out)
    return out


def end_of(starts, token):
    out = starts[1]
    for j in range(1, len(starts) - 1):
        out = jnp.where(token >= starts[j], starts[j + 1], out)
    return out


def adapter_mask(cfg, meta):
    token = iota((cfg.T, cfg.AW), 0) * cfg.n + meta[0]
    starts = doc_starts(cfg, meta)
    adapter = jnp.full((cfg.T, cfg.AW), meta[2 + cfg.docs], jnp.int32)
    for j in range(1, cfg.docs):
        adapter = jnp.where(token >= starts[j], meta[2 + cfg.docs + j], adapter)
    return (adapter == iota((cfg.T, cfg.AW), 1) // RANK).astype(F32)


def slot_select(cfg, meta):
    row = iota((cfg.AW, cfg.S), 0)
    col = iota((cfg.AW, cfg.S), 1)
    if cfg.S == cfg.AW:
        return (row == col).astype(BF)
    target = jnp.full((cfg.AW, cfg.S), -1, jnp.int32)
    for s in range(cfg.slots):
        mine = meta[2 + cfg.docs + s]
        again = jnp.int32(0)
        for e in range(s):
            again = jnp.where(meta[2 + cfg.docs + e] == mine, 1, again)
        base = jnp.where(again == 1, -4 * cfg.AW, mine * RANK)
        target = jnp.where(col // RANK == s, base + col % RANK, target)
    return (row == target).astype(BF)


def block_mean(values, hd):
    width = values.shape[1]
    ones = (iota((width, width), 0) // hd == iota((width, width), 1) // hd).astype(BF)
    high = values.astype(BF)
    low = (values - high.astype(F32)).astype(BF)
    return (mm(high, ones) + mm(low, ones)) * (1.0 / hd)


def swap_halves(values, hd):
    width = values.shape[1]
    half = hd // 2
    first = iota(values.shape, 1) % hd < half
    return jnp.where(first, pltpu.roll(values, width - half, 1), pltpu.roll(values, half, 1))


def lanes(values, copies):
    return jnp.concatenate([values] * copies, axis=1) if copies > 1 else values


def params(large=False, **kw):
    limit = VMEM_SMALL if lax.axis_size("ctx") <= 16 and not large else VMEM_LARGE
    return pltpu.CompilerParams(vmem_limit_bytes=limit, **kw)


SMEM = pl.BlockSpec(memory_space=pltpu.SMEM)


def cost(us):
    return pl.CostEstimate(flops=int(us * 1.15e9), bytes_accessed=0, transcendentals=0)


def call(kernel, outs, ins, scratch=(), us=1.0, name=None, large=False):
    ins = [*ins[0], *ins[1:]]
    return pl.pallas_call(
        with_meta(kernel),
        out_shape=[jax.ShapeDtypeStruct(s, d) for s, d in outs],
        in_specs=[SMEM] * 2 + [pl.BlockSpec(memory_space=pltpu.VMEM)] * (len(ins) - 2),
        out_specs=[pl.BlockSpec(memory_space=pltpu.VMEM)] * len(outs),
        scratch_shapes=list(scratch),
        compiler_params=params(large),
        cost_estimate=cost(us),
        name=name,
    )(*ins)


def pre_kernel(
    cfg, meta, x_ref, gain, wq, wk, wv, aq, ak, av, bq, bk, bv, qg, kg, inverse, *refs
):
    G, hd = cfg.G, cfg.hd
    kv_out, q_out = refs[:G], refs[G : 2 * G]
    qraw_ref, kraw_ref, sides_ref, normed_ref, cos, sin, kv_scr, q_scr = refs[2 * G :]
    hi = meta[0] // cfg.lo
    shape = cos.shape
    token = iota(shape, 0) * cfg.n + meta[0]
    angle = (token - start_of(doc_starts(cfg, meta), token)).astype(F32) * inverse[...]
    cos[...] = jnp.cos(angle)
    sin[...] = jnp.sin(angle) * jnp.where(iota(shape, 1) % hd < hd // 2, -1.0, 1.0)
    x = x_ref[...].astype(F32)
    rr = lax.rsqrt(jnp.mean(x * x, axis=-1, keepdims=True) + norm_eps)
    normed = (x * rr * gain[...]).astype(BF)
    normed_ref[...] = normed
    mask = adapter_mask(cfg, meta)
    select = slot_select(cfg, meta)
    raws = []
    for i, (w, a, b) in enumerate(((wq, aq, bq), (wk, ak, bk), (wv, av, bv))):
        side = (mask * mm(normed, a[...])).astype(BF)
        sides_ref[i] = mm(side, select).astype(BF)
        raws.append(mm(normed, w[...]) + mm(side, b[...]))
    qraw, kraw, vraw = raws
    qraw_ref[...] = qraw
    kraw_ref[...] = kraw

    def prep(raw, g):
        copies = raw.shape[1] // hd
        scaled = raw * lax.rsqrt(block_mean(raw * raw, hd) + norm_eps) * lanes(g[...], copies)
        per = raw.shape[1] // cos.shape[1]
        return scaled * lanes(cos[...], per) + swap_halves(scaled, hd) * lanes(sin[...], per)

    query = prep(qraw, qg).astype(BF)
    key = prep(kraw, kg).astype(BF)
    value = vraw.astype(BF)
    gw = cfg.groups * hd
    for h in range(G):
        q_scr[h] = query[:, h * gw : (h + 1) * gw]
        kv_scr[h] = jnp.concatenate(
            [key[:, h * hd : (h + 1) * hd], value[:, h * hd : (h + 1) * hd]], axis=1
        )
    for k in range(G):
        kv_out[k][...] = kv_scr[hi ^ k]
        q_out[k][...] = q_scr[hi ^ k]


def load_tiles(cfg, scr, pieces):
    R = cfg.R
    for p, piece in enumerate(pieces):
        for t in range(cfg.NT):
            scr[t, p * R : (p + 1) * R, :] = piece[t * R : (t + 1) * R, :]


def split_pieces(ref, count):
    return [ref.at[i] for i in range(count)]


def message_pieces(cfg, ref):
    return [ref.at[pl.ds(k * cfg.T, cfg.T)] for k in range(cfg.G)]


def token_in_span(cfg, meta, index):
    hi, lo = meta[0] // cfg.lo, meta[0] % cfg.lo
    piece, row = index // cfg.R, index % cfg.R
    j, k = piece // cfg.G, piece % cfg.G
    return row * cfg.n + (hi ^ k) * cfg.lo + (lo ^ j)


def pad_queries(cfg, qq, side):
    hd = cfg.hd
    wide = qq.astype(F32)
    first = iota(wide.shape, 1) < hd
    rolled = pltpu.roll(wide, hd, 1)
    if side == 0:
        parts = [jnp.where(first, wide, 0.0), jnp.where(first, rolled, 0.0)]
    else:
        parts = [jnp.where(first, 0.0, rolled), jnp.where(first, 0.0, wide)]
    return jnp.concatenate(parts, axis=0).astype(BF)


def query_tile_ranges(cfg, starts, qt):
    first = qt * cfg.span
    s_lo = start_of(starts, first) // cfg.span
    s_full = (start_of(starts, first + cfg.span - 1) + cfg.span - 1) // cfg.span
    return s_lo, jnp.minimum(s_full, qt)


def attend_kernel(cfg, meta, *refs):
    G, T, R, hd = cfg.G, cfg.T, cfg.R, cfg.hd
    q_in, own, others = refs[:G], refs[G], refs[G + 1 : G + cfg.lo]
    rest = refs[G + cfg.lo :]
    o_out, o_all, linv, kv_scr, va_scr, q_scr = rest[:G], *rest[G:]
    pieces = split_pieces(own, G)
    for ref in others:
        pieces = pieces + split_pieces(ref, G)
    load_tiles(cfg, kv_scr, pieces)
    load_tiles(cfg, q_scr, q_in)
    starts = doc_starts(cfg, meta)
    QH = cfg.QH
    scale = hd ** (-0.5) * LOG2E
    key_off = token_in_span(cfg, meta, iota((1, cfg.KT), 1))
    row_off = token_in_span(cfg, meta, iota((2 * QH, 1), 0) % QH)
    lane_first = iota((cfg.KT, 2 * hd), 1) < hd

    def fill(t, carry):
        va_scr[t] = jnp.where(lane_first, 1.0, kv_scr[t].astype(F32)).astype(BF)
        return carry

    lax.fori_loop(0, cfg.NT, fill, 0)
    half = iota((QH, 2 * hd), 1) < hd

    def query_tile(qt, carry):
        queries = pad_queries(cfg, q_scr[qt], 0)
        token = row_off + qt * cfg.span
        first_key = start_of(starts, token)
        s_lo, s_full = query_tile_ranges(cfg, starts, qt)

        def tile(s, acc, masked):
            e = jnp.exp2(mm_nt(queries, kv_scr[s]) * scale)
            if masked:
                key_token = key_off + s * cfg.span
                e = jnp.where((key_token <= token) & (key_token >= first_key), e, 0.0)
            return acc + mm(e.astype(BF), va_scr[s])

        acc = jnp.zeros((2 * QH, 2 * hd), F32)
        acc = lax.fori_loop(s_lo, s_full, lambda s, a: tile(s, a, True), acc)
        acc = lax.fori_loop(s_full, qt, lambda s, a: tile(s, a, False), acc)
        acc = tile(qt, acc, True)
        inv0 = 1.0 / acc[:QH]
        inv1 = 1.0 / acc[QH:]
        out0 = pltpu.roll(acc[:QH], hd, 1) * inv0
        out1 = acc[QH:] * pltpu.roll(inv1, hd, 1)
        out = jnp.where(half, out0, out1).astype(BF)
        inv = jnp.where(half, inv0, pltpu.roll(inv1, hd, 1))
        rows = pl.ds(pl.multiple_of(qt * R, R), R)
        for k in range(G):
            o_out[k][rows, :] = out[k * R : (k + 1) * R]
            o_all[k, rows, :] = out[k * R : (k + 1) * R]
            linv[k, rows, :] = inv[k * R : (k + 1) * R]
        return carry

    lax.fori_loop(0, cfg.NT, query_tile, 0)


def head_sums(cfg, prod):
    pick = (iota((16, prod.shape[1]), 1) // cfg.hd == iota((16, prod.shape[1]), 0)).astype(BF)
    high = prod.astype(BF)
    low = (prod - high.astype(F32)).astype(BF)
    return mm_nt(pick, high) + mm_nt(pick, low)


def scale_kernel(cfg, meta, *refs):
    G, T, R, NT, QH = cfg.G, cfg.T, cfg.R, cfg.NT, cfg.QH
    go, linv, o_all, out, scr, delta = refs[:G], refs[G], refs[G + 1], refs[G + 2], *refs[G + 3 :]
    delta[...] = jnp.zeros_like(delta)
    for k in range(G):
        scaled = (go[k][...].astype(F32) * linv[k]).astype(BF)
        out[k * T : (k + 1) * T, :] = scaled
        prod = scaled.astype(F32) * o_all[k].astype(F32)
        for t in range(NT):
            scr[t, k * R : (k + 1) * R, :] = prod[t * R : (t + 1) * R]
    for t in range(NT):
        sums = head_sums(cfg, scr[t])
        for h in range(cfg.groups):
            delta[h * NT + t : h * NT + t + 1, :QH] = sums[h : h + 1]
    high = delta[...].astype(BF)
    at = G * T
    rows = cfg.groups * NT
    out[at : at + rows, :] = high
    out[at + rows : at + 2 * rows, :] = (delta[...] - high.astype(F32)).astype(BF)


def grad_query_kernel(cfg, meta, *refs):
    G, T, R, hd = cfg.G, cfg.T, cfg.R, cfg.hd
    q_in, own, others = refs[:G], refs[G], refs[G + 1 : G + cfg.lo]
    go_ref, o_ref = refs[G + cfg.lo : G + cfg.lo + 2]
    rest = refs[G + cfg.lo + 2 :]
    dq_out, kv_scr, q_scr, go_scr, o_scr = rest[:G], *rest[G:]
    pieces = split_pieces(own, G)
    for ref in others:
        pieces = pieces + split_pieces(ref, G)
    load_tiles(cfg, kv_scr, pieces)
    load_tiles(cfg, q_scr, q_in)
    load_tiles(cfg, go_scr, message_pieces(cfg, go_ref))
    load_tiles(cfg, o_scr, split_pieces(o_ref, G))
    starts = doc_starts(cfg, meta)
    QH = cfg.QH
    scale = hd ** (-0.5) * LOG2E
    key_off = token_in_span(cfg, meta, iota((1, cfg.KT), 1))
    row_off = token_in_span(cfg, meta, iota((2 * QH, 1), 0) % QH)
    half = iota((QH, 2 * hd), 1) < hd

    def query_tile(qt, carry):
        queries = pad_queries(cfg, q_scr[qt], 0)
        grads = pad_queries(cfg, go_scr[qt], 1)
        prod = go_scr[qt].astype(F32) * o_scr[qt].astype(F32)
        delta = jnp.concatenate(
            [
                jnp.sum(jnp.where(half, prod, 0.0), axis=1, keepdims=True),
                jnp.sum(jnp.where(half, 0.0, prod), axis=1, keepdims=True),
            ],
            axis=0,
        )
        token = row_off + qt * cfg.span
        first_key = start_of(starts, token)
        s_lo, s_full = query_tile_ranges(cfg, starts, qt)

        def tile(s, acc, masked):
            kv = kv_scr[s]
            e = jnp.exp2(mm_nt(queries, kv) * scale)
            if masked:
                key_token = key_off + s * cfg.span
                e = jnp.where((key_token <= token) & (key_token >= first_key), e, 0.0)
            ds = e * (mm_nt(grads, kv) - delta)
            return acc + mm(ds.astype(BF), kv)

        acc = jnp.zeros((2 * QH, 2 * hd), F32)
        acc = lax.fori_loop(s_lo, s_full, lambda s, a: tile(s, a, True), acc)
        acc = lax.fori_loop(s_full, qt, lambda s, a: tile(s, a, False), acc)
        acc = tile(qt, acc, True)
        out = jnp.where(half, acc[:QH], pltpu.roll(acc[QH:], hd, 1)) * hd ** (-0.5)
        out = out.astype(BF)
        rows = pl.ds(pl.multiple_of(qt * R, R), R)
        for k in range(G):
            dq_out[k][rows, :] = out[k * R : (k + 1) * R]
        return carry

    lax.fori_loop(0, cfg.NT, query_tile, 0)


def grad_key_kernel(cfg, meta, *refs):
    G, T, R, hd, lo = cfg.G, cfg.T, cfg.R, cfg.hd, cfg.lo
    own = refs[0]
    q_refs, go_refs = (refs[1 + i * lo : 1 + (i + 1) * lo] for i in range(2))
    rest = refs[1 + 2 * lo :]
    dkv_out, kv_scr, q_scr, go_scr, delta_scr = rest[:G], *rest[G:]
    load_tiles(cfg, kv_scr, split_pieces(own, G))
    load_tiles(cfg, q_scr, [piece for ref in q_refs for piece in split_pieces(ref, G)])
    load_tiles(cfg, go_scr, [piece for ref in go_refs for piece in message_pieces(cfg, ref)])
    starts = doc_starts(cfg, meta)
    QH, NT = cfg.QH, cfg.NT
    scale = hd ** (-0.5) * LOG2E
    rows = cfg.groups * NT
    for j in range(lo):
        sums = go_refs[j][G * T : G * T + 2 * rows, :].astype(F32)
        sums = sums[:rows] + sums[rows:]
        for t in range(NT):
            for h in range(cfg.groups):
                at = h * NT + t
                delta_scr[t, h : h + 1, j * QH : (j + 1) * QH] = sums[at : at + 1, :QH]
    query_off = token_in_span(cfg, meta, iota((1, cfg.KT), 1))
    row_off = token_in_span(cfg, meta, iota((2 * QH, 1), 0) % QH)
    first = iota((QH, 2 * hd), 1) < hd

    def key_tile(kt, carry):
        kv = kv_scr[kt].astype(F32)
        rolled = pltpu.roll(kv, hd, 1)
        keys = jnp.concatenate(
            [jnp.where(first, kv, 0.0), jnp.where(first, 0.0, rolled)], axis=0
        ).astype(BF)
        values = jnp.concatenate(
            [jnp.where(first, rolled, 0.0), jnp.where(first, 0.0, kv)], axis=0
        ).astype(BF)
        key_token = row_off + kt * cfg.span
        end_first = end_of(starts, kt * cfg.span)
        end_last = end_of(starts, (kt + 1) * cfg.span - 1)
        q_full = jnp.maximum(end_first // cfg.span, kt + 1)
        q_stop = (end_last - 1) // cfg.span + 1

        def tile(t, acc, masked):
            grad_keys, grad_values = acc
            queries, grads = q_scr[t], go_scr[t]
            e = jnp.exp2(mm_nt(keys, queries) * scale)
            if masked:
                token = query_off + t * cfg.span
                e = jnp.where((key_token <= token) & (key_token >= start_of(starts, token)), e, 0.0)
            dp = mm_nt(values, grads)
            delta = delta_scr[t]
            ds = jnp.concatenate(
                [
                    (e[:QH] * (dp[:QH] - delta[0:1])).astype(BF),
                    (e[QH:] * (dp[QH:] - delta[1:2])).astype(BF),
                ],
                axis=0,
            )
            return grad_keys + mm(ds, queries), grad_values + mm(e.astype(BF), grads)

        zero = jnp.zeros((2 * QH, 2 * hd), F32)
        acc = tile(kt, (zero, zero), True)
        acc = lax.fori_loop(kt + 1, q_full, lambda t, a: tile(t, a, False), acc)
        acc = lax.fori_loop(q_full, q_stop, lambda t, a: tile(t, a, True), acc)
        grad_keys, grad_values = acc
        gk = (grad_keys[:QH] + pltpu.roll(grad_keys[QH:], hd, 1)) * hd ** (-0.5)
        gv = pltpu.roll(grad_values[:QH], hd, 1) + grad_values[QH:]
        out = jnp.where(first, gk, gv).astype(BF)
        rows = pl.ds(pl.multiple_of(kt * R, R), R)
        for k in range(G):
            dkv_out[k][rows, :] = out[k * R : (k + 1) * R]
        return carry

    lax.fori_loop(0, cfg.NT, key_tile, 0)


def place_pieces(cfg, hi, scr, pieces):
    w = pieces[0].shape[1]
    for k in range(cfg.G):
        at = pl.multiple_of((hi ^ k) * w, w)
        scr[:, pl.ds(at, w)] = pieces[k][...]


def out_kernel(cfg, meta, *refs):
    G = cfg.G
    wo, ao, part, attn = refs[G:]
    place_pieces(cfg, meta[0] // cfg.lo, attn, refs[:G])
    rows = attn[...]
    part[:, : cfg.D] = mm(rows, wo[...]).astype(BF)
    part[:, cfg.D :] = mm(rows, ao[...]).astype(BF)


def ffn_kernel(
    cfg, units, steps, meta, x_ref, own, other, bo, gain, wg, wu, wd, bg, bu, ag, au, ad, bd, cot_ref,
    mixed_ref, dfn_ref, part_ref, oside, *refs,
):
    step = pl.program_id(0)
    S, D = cfg.S, cfg.D
    chunks, refs = refs[: units.n], refs[units.n :]
    fn, sg, su, gsd, sgt, sut, gsdt, down, side_sum, dfn, gsg, gsu, grads = refs
    flip = meta[0] % cfg.lo

    @pl.when(step == 0)
    def _():
        mask = adapter_mask(cfg, meta)
        select = slot_select(cfg, meta)
        total = own[...].astype(F32) + other[...].astype(F32)
        out_side = (mask * total[:, D:]).astype(BF)
        oside[...] = mm(out_side, select).astype(BF)
        mixed = x_ref[...].astype(F32) + total[:, :D] + mm(out_side, bo[...])
        mixed_ref[...] = mixed
        rr = lax.rsqrt(jnp.mean(mixed * mixed, axis=-1, keepdims=True) + norm_eps)
        normed = (mixed * rr * gain[...]).astype(BF)
        fn[...] = normed
        side_g = (mask * mm(normed, ag[...])).astype(BF)
        side_u = (mask * mm(normed, au[...])).astype(BF)
        grad_side = (mask * mm_nt(cot_ref[...], bd[...])).astype(BF)
        sg[...] = side_g
        su[...] = side_u
        gsd[...] = grad_side
        sgt[...] = mm(side_g, select).T.astype(BF)
        sut[...] = mm(side_u, select).T.astype(BF)
        gsdt[...] = mm(grad_side, select).T.astype(BF)
        down[...] = jnp.zeros_like(down)
        side_sum[...] = jnp.zeros_like(side_sum)
        dfn[...] = jnp.zeros_like(dfn)
        gsg[...] = jnp.zeros_like(gsg)
        gsu[...] = jnp.zeros_like(gsu)

    normed = fn[...]
    gate = mm(normed, wg[...]) + mm(sg[...], bg[...])
    upper = mm(normed, wu[...]) + mm(su[...], bu[...])
    grad_hidden = mm_nt(cot_ref[...], wd[...]) + mm_nt(gsd[...], ad[...])
    sigma = 1.0 / (1.0 + jnp.exp(-gate))
    silu = gate * sigma
    hidden = (silu * upper).astype(BF)
    grad_gate = (grad_hidden * upper * (sigma + silu * (1.0 - sigma))).astype(BF)
    grad_upper = (grad_hidden * silu).astype(BF)
    down[...] += mm(hidden, wd[...])
    side_sum[...] += mm(hidden, ad[...])
    dfn[...] += mm_nt(grad_gate, wg[...]) + mm_nt(grad_upper, wu[...])
    gsg[...] += mm_nt(grad_gate, bg[...])
    gsu[...] += mm_nt(grad_upper, bu[...])
    for i, (left, right) in enumerate(((sgt, grad_gate), (sut, grad_upper), (gsdt, hidden))):
        first = step * (right.shape[1] // 128)
        units.store(grads, flip, 1, i, mm(left[...], right).astype(BF), first)

    @pl.when(step == steps - 1)
    def _():
        mask = adapter_mask(cfg, meta)
        select = slot_select(cfg, meta)
        side_g = (mask * gsg[...]).astype(BF)
        side_u = (mask * gsu[...]).astype(BF)
        dfn_ref[...] = (dfn[...] + mm_nt(side_g, ag[...]) + mm_nt(side_u, au[...])).astype(BF)
        part_ref[:, :D] = down[...].astype(BF)
        part_ref[:, D:] = side_sum[...].astype(BF)
        side_d = (mask * side_sum[...]).astype(BF)
        for i, (side, right) in enumerate(((side_g, fn), (side_u, fn), (side_d, cot_ref))):
            left = mm(side, select).T.astype(BF)
            units.store(grads, flip, 0, i, mm(left, right[...]).astype(BF), 0)
        units.clear_spare(grads, flip)
        for j, chunk in enumerate(chunks):
            chunk[...] = grads[j]


def ffn_call(cfg, units, meta, x, own, other, bo, gain, wg, wu, wd, bg, bu, ag, au, ad, bd, cot):
    T, D, F, AW, S = cfg.T, cfg.D, cfg.F, cfg.AW, cfg.S
    tile = 256
    steps = F // tile
    whole = lambda shape: pl.BlockSpec(shape, lambda i: (0,) * len(shape))
    cols = lambda rows: pl.BlockSpec((rows, tile), lambda i: (0, i))
    rows = lambda width: pl.BlockSpec((tile, width), lambda i: (i, 0))
    outs = [
        ((T, D), F32),
        ((T, D), BF),
        ((T, D + AW), BF),
        ((T, S), BF),
    ] + [((units.u, 16, 128), BF)] * units.n
    out_specs = [
        whole((T, D)),
        whole((T, D)),
        whole((T, D + AW)),
        whole((T, S)),
    ] + [whole((units.u, 16, 128))] * units.n
    return pl.pallas_call(
        with_meta(functools.partial(ffn_kernel, cfg, units, steps)),
        grid=(steps,),
        out_shape=[jax.ShapeDtypeStruct(s, d) for s, d in outs],
        in_specs=[
            SMEM,
            SMEM,
            whole((T, D)),
            whole((T, D + AW)),
            whole((T, D + AW)),
            whole((AW, D)),
            whole((1, D)),
            cols(D),
            cols(D),
            rows(D),
            cols(AW),
            cols(AW),
            whole((D, AW)),
            whole((D, AW)),
            rows(AW),
            whole((AW, D)),
            whole((T, D)),
        ],
        out_specs=out_specs,
        scratch_shapes=[
            pltpu.VMEM((T, D), BF),
            pltpu.VMEM((T, AW), BF),
            pltpu.VMEM((T, AW), BF),
            pltpu.VMEM((T, AW), BF),
            pltpu.VMEM((S, T), BF),
            pltpu.VMEM((S, T), BF),
            pltpu.VMEM((S, T), BF),
            pltpu.VMEM((T, D), F32),
            pltpu.VMEM((T, AW), F32),
            pltpu.VMEM((T, D), F32),
            pltpu.VMEM((T, AW), F32),
            pltpu.VMEM((T, AW), F32),
            pltpu.VMEM((units.n, units.u, 16, 128), BF),
        ],
        compiler_params=params(dimension_semantics=("arbitrary",)),
        cost_estimate=cost(19),
        name="ffn",
    )(*meta, x, own, other, bo, gain, wg, wu, wd, bg, bu, ag, au, ad, bd, cot)


def mixed_grad_kernel(cfg, meta, *refs):
    G, D = cfg.G, cfg.D
    mixed_ref, own, other, cot, gain = refs[:5]
    o_in = refs[5 : 5 + G]
    wo, ao, bo, oside = refs[5 + G : 9 + G]
    rest = refs[9 + G :]
    gm_ref, ograds, go_out, attn, go_scr, gm_scr = rest[0], rest[1], rest[2 : 2 + G], *rest[2 + G :]
    hi = meta[0] // cfg.lo
    mixed = mixed_ref[...]
    w = (own[...].astype(F32) + other[...].astype(F32)) * gain[...]
    rr = lax.rsqrt(jnp.mean(mixed * mixed, axis=-1, keepdims=True) + norm_eps)
    inner = jnp.mean(w * mixed, axis=-1, keepdims=True)
    gm = cot[...].astype(F32) + rr * w - (rr * rr * rr * inner) * mixed
    gm_ref[...] = gm
    gmb = gm.astype(BF)
    gm_scr[...] = gmb
    mask = adapter_mask(cfg, meta)
    select = slot_select(cfg, meta)
    grad_side = (mask * mm_nt(gmb, bo[...])).astype(BF)
    go = (mm_nt(gmb, wo[...]) + mm_nt(grad_side, ao[...])).astype(BF)
    w = cfg.groups * cfg.hd
    for h in range(G):
        go_scr[h] = go[:, h * w : (h + 1) * w]
    for k in range(G):
        go_out[k][...] = go_scr[hi ^ k]
    place_pieces(cfg, hi, attn, o_in)
    ograds[0] = mm(mm(grad_side, select).T.astype(BF), attn[...]).astype(BF)
    half = D // 2
    mine = gm_scr[:, pl.ds(pl.multiple_of(meta[1] * half, half), half)]
    ograds[1] = mm(oside[...].astype(F32).T.astype(BF), mine).astype(BF)


def output_kernel(cfg, meta, mixed, own, other, bd, out_ref):
    D = cfg.D
    total = own[...].astype(F32) + other[...].astype(F32)
    side = (adapter_mask(cfg, meta) * total[:, D:]).astype(BF)
    out_ref[...] = (mixed[...] + total[:, :D] + mm(side, bd[...])).astype(BF)


def head_back(cfg, cos, sin, grad, raw, g):
    hd = cfg.hd
    copies = raw.shape[1] // hd
    per = raw.shape[1] // cos.shape[1]
    un = grad * lanes(cos[...], per) - swap_halves(grad, hd) * lanes(sin[...], per)
    w = un * lanes(g[...], copies)
    rr = lax.rsqrt(block_mean(raw * raw, hd) + norm_eps)
    return rr * w - rr * rr * rr * raw * block_mean(w * raw, hd)


def half_lanes(cfg, meta):
    half = cfg.D // 2
    keep = pl.ds(pl.multiple_of(meta[1] * half, half), half)
    send = pl.ds(pl.multiple_of((1 - meta[1]) * half, half), half)
    return keep, send


def query_back_kernel(cfg, meta, *refs):
    G, S = cfg.G, cfg.S
    normed, raw, sides, cos, sin, gain, w, a, b, part, bgrad, akeep, asend, dq_scr, a_scr = refs[G:]
    place_pieces(cfg, meta[0] // cfg.lo, dq_scr, refs[:G])
    g = head_back(cfg, cos, sin, dq_scr[...].astype(F32), raw[...], gain).astype(BF)
    select = slot_select(cfg, meta)
    grad_side = (adapter_mask(cfg, meta) * mm_nt(g, b[...])).astype(BF)
    part[...] = mm_nt(g, w[...]) + mm_nt(grad_side, a[...])
    a_scr[...] = mm(mm(grad_side, select).T.astype(BF), normed[...])
    bgrad[...] = mm(sides[0].astype(F32).T.astype(BF), g).astype(BF)
    keep, send = half_lanes(cfg, meta)
    akeep[...] = a_scr[:, keep].astype(BF)
    asend[...] = a_scr[:, send].astype(BF)


def key_value_back_kernel(cfg, meta, *refs):
    G, S, hd = cfg.G, cfg.S, cfg.hd
    (
        normed, raw, sides, cos, sin, gain, wk, wv, ak, av, bk, bv, qpart,
        part, bgrad, akeep, asend, dkv_scr, a_scr,
    ) = refs[G:]
    place_pieces(cfg, meta[0] // cfg.lo, dkv_scr, refs[:G])
    mask = adapter_mask(cfg, meta)
    select = slot_select(cfg, meta)
    dkv = dkv_scr[...]
    dk = jnp.concatenate([dkv[:, 2 * h * hd : (2 * h + 1) * hd] for h in range(G)], axis=1)
    dv = jnp.concatenate([dkv[:, (2 * h + 1) * hd : (2 * h + 2) * hd] for h in range(G)], axis=1)
    gk = head_back(cfg, cos, sin, dk.astype(F32), raw[...], gain).astype(BF)
    total = qpart[...]
    width = gk.shape[1]
    for i, (g, w, a, b) in enumerate(((gk, wk, ak, bk), (dv, wv, av, bv))):
        grad_side = (mask * mm_nt(g, b[...])).astype(BF)
        total = total + mm_nt(g, w[...]) + mm_nt(grad_side, a[...])
        a_scr[i * S : (i + 1) * S, :] = mm(mm(grad_side, select).T.astype(BF), normed[...])
        bgrad[:, i * width : (i + 1) * width] = mm(
            sides[i + 1].astype(F32).T.astype(BF), g
        ).astype(BF)
    part[...] = total.astype(BF)
    keep, send = half_lanes(cfg, meta)
    akeep[...] = a_scr[:, keep].astype(BF)
    asend[...] = a_scr[:, send].astype(BF)


def input_grad_kernel(cfg, meta, x_ref, gain, gm, own, other, out):
    x = x_ref[...].astype(F32)
    w = (own[...].astype(F32) + other[...].astype(F32)) * gain[...]
    rr = lax.rsqrt(jnp.mean(x * x, axis=-1, keepdims=True) + norm_eps)
    inner = jnp.mean(w * x, axis=-1, keepdims=True)
    out[...] = (gm[...] + rr * w - (rr * rr * rr * inner) * x).astype(BF)


class Units:
    def __init__(self, cfg, n, shared, private):
        self.n = n
        self.high = cfg.S // 16
        self.shared, self.private = shared, private
        self.us, self.up = self.per_chunk(shared), self.per_chunk(private)
        self.u = self.us + self.up

    def per_chunk(self, widths):
        return -(-sum(w // 128 for w in widths) * self.high // self.n)

    def places(self, which):
        widths, per, base = (
            (self.shared, self.us, 0) if which == 0 else (self.private, self.up, self.us)
        )
        at, out = 0, []
        for w in widths:
            spots = []
            for c in range(w // 128):
                for a in range(self.high):
                    spots.append((at // per, base + at % per, a, c))
                    at += 1
            out.append(spots)
        return out

    def spare(self):
        out = []
        for widths, per, base in ((self.shared, self.us, 0), (self.private, self.up, self.us)):
            count = sum(w // 128 for w in widths) * self.high
            out += [(i // per, base + i % per) for i in range(count, per * self.n)]
        return out

    def store(self, out, flip, which, array, values, first):
        widths, per, base = (
            (self.shared, self.us, 0) if which == 0 else (self.private, self.up, self.us)
        )
        at = sum(w // 128 for w in widths[:array]) * self.high + first * self.high
        for c in range(values.shape[1] // 128):
            for a in range(self.high):
                unit = at + c * self.high + a
                out[(unit // per) ^ flip, base + unit % per] = values[
                    a * 16 : a * 16 + 16, c * 128 : c * 128 + 128
                ]

    def clear_spare(self, out, flip):
        for chunk, off in self.spare():
            out[chunk ^ flip, off] = jnp.zeros((16, 128), BF)


def pack(units, out, flip, arrays):
    for i, values in enumerate(arrays):
        which = int(i >= len(units.shared))
        units.store(out, flip, which, i - which * len(units.shared), values, 0)
    units.clear_spare(out, flip)


def add_halves(keep, got, count):
    total = (keep[...].astype(F32) + got[...].astype(F32)).astype(BF)
    rows = total.shape[0] // count
    return [total[i * rows : (i + 1) * rows] for i in range(count)]


def pack_qkv_kernel(cfg, units, meta, keep_q, got_q, keep, got, ograds, bq, bkv, *outs):
    scr, outs = outs[-1], outs[:-1]
    kw = bkv.shape[1] // 2
    shared = add_halves(keep_q, got_q, 1) + add_halves(keep, got, 2) + [ograds[1]]
    private = [ograds[0], bq[...], bkv[:, :kw], bkv[:, kw:]]
    pack(units, scr, meta[0] % cfg.lo, shared + private)
    for j, out in enumerate(outs):
        out[...] = scr[j]


def unpack(ref, spots, place):
    cols = {}
    for chunk, off, a, c in spots:
        cols.setdefault(c, []).append(ref[place(chunk), off])
    return jnp.concatenate([jnp.concatenate(cols[c], axis=0) for c in sorted(cols)], axis=1)


def expand_kernel(cfg, units, plan, halves, meta, *refs):
    own_in, other, outs, own = refs[: cfg.lo], refs[cfg.lo], refs[cfg.lo + 1 : -1], refs[-1]
    for j in range(cfg.lo):
        own[j] = own_in[j][...]
    wa = meta[1]
    select = slot_select(cfg, meta)
    place = lambda chunk: chunk ^ (meta[0] % cfg.lo)

    def write(out, values, transposed, at):
        full = mm(select, values)
        if transposed:
            out[at : at + full.shape[1], :] = full.T
        else:
            out[:, at : at + full.shape[1]] = full

    for (which, i, transposed), out in zip(plan, outs):
        spots = units.places(which)[i]
        mine = unpack(own, spots, place)
        if which == 1:
            write(out, mine, transposed, 0)
        else:
            theirs = unpack(other, spots, place)
            if not halves:
                total = mine.astype(F32) + theirs.astype(F32)
                write(out, total.astype(BF), transposed, 0)
                continue
            width = mine.shape[1]
            write(out, jnp.where(wa == 0, mine, theirs), transposed, 0)
            write(out, jnp.where(wa == 0, theirs, mine), transposed, width)


def upper_bits(cfg):
    bits, bit = [], cfg.n // 2
    while bit >= cfg.lo:
        bits.append(bit)
        bit //= 2
    return bits


def after(*values):
    return lax.optimization_barrier(values)


def swap_cores(value):
    return lax.ppermute(value, "wa", [(0, 1), (1, 0)])


def permute(cfg, value, bits):
    return lax.ppermute(value, "ctx", [(i, i ^ bits) for i in range(cfg.n)])


def per_device(
    hidden_in, attn_gain, query_weight, key_weight, value_weight, query_gain, key_gain, out_weight,
    ffn_gain, gate_weight, up_weight, down_weight, query_adapt_in, query_adapt_out, key_adapt_in,
    key_adapt_out, value_adapt_in, value_adapt_out, out_adapt_in, out_adapt_out, gate_adapt_in,
    gate_adapt_out, up_adapt_in, up_adapt_out, down_adapt_in, down_adapt_out, document_extra,
    document_adapter, cotangent,
):
    head_dim = query_gain.shape[0]
    cfg = Cfg(
        tokens=hidden_in.shape[0],
        n_ctx=lax.axis_size("ctx"),
        heads_kv=key_weight.shape[1] // head_dim,
        groups=query_weight.shape[1] // key_weight.shape[1],
        head_dim=head_dim,
        docs=document_extra.shape[0],
        adapt_width=query_adapt_in.shape[1],
        width=hidden_in.shape[2],
        hidden=gate_weight.shape[1],
    )
    T, D, G, S, AW, n, lo = cfg.T, cfg.D, cfg.G, cfg.S, cfg.AW, cfg.n, cfg.lo
    gw = cfg.groups * head_dim
    QW, KW = query_weight.shape[1], key_weight.shape[1]
    meta = (document_extra, document_adapter)
    x = hidden_in.reshape(T, D)
    cot = cotangent.reshape(T, D)
    gain_a = attn_gain.reshape(1, D)
    gain_f = ffn_gain.reshape(1, D)
    qg = query_gain.reshape(1, head_dim)
    kg = key_gain.reshape(1, head_dim)

    lane = jnp.arange(2 * head_dim, dtype=jnp.int32) % (head_dim // 2)
    inverse = jnp.exp(lane.astype(F32) * (-2.0 * math.log(theta_base) / head_dim))[None, :]

    piece = ((T, gw), BF)
    pre = call(
        functools.partial(pre_kernel, cfg),
        [piece] * (2 * G)
        + [((T, QW), F32), ((T, KW), F32), ((3, T, S), BF), ((T, D), BF)]
        + [((T, 2 * head_dim), F32)] * 2,
        [
            meta, x, gain_a, query_weight, key_weight, value_weight, query_adapt_in, key_adapt_in,
            value_adapt_in, query_adapt_out, key_adapt_out, value_adapt_out, qg, kg, inverse,
        ],
        scratch=[pltpu.VMEM((G, T, gw), BF), pltpu.VMEM((G, T, gw), BF)],
        us=6,
        name="pre",
        large=True,
    )
    kv_send, q_send = pre[:G], pre[G : 2 * G]
    qraw, kraw, sides, normed, cos, sin = pre[2 * G :]

    def to_heads(pieces):
        return [pieces[0]] + [permute(cfg, pieces[k], k * lo) for k in range(1, G)]

    def add(values):
        return sum(value.astype(F32) for value in values).astype(BF)

    def to_plane(value):
        return [value] + [permute(cfg, value, j) for j in range(1, lo)]

    kv = to_plane(jnp.stack(to_heads(kv_send)))
    q = to_heads(q_send)
    tiles = lambda rows: pltpu.VMEM((cfg.NT, rows, gw), BF)
    attn = call(
        functools.partial(attend_kernel, cfg),
        [piece] * G + [((G, T, gw), BF), ((G, T, gw), F32)],
        [meta] + q + kv,
        scratch=[tiles(cfg.KT), tiles(cfg.KT), tiles(cfg.QH)],
        us=12,
        name="attend",
    )
    o_send, o_all, linv = attn[:G], attn[G], attn[G + 1]
    o = to_heads(o_send)
    q_stack, _ = after(jnp.stack(q), o_send[0])
    q_plane = to_plane(q_stack)
    (opart,) = call(
        functools.partial(out_kernel, cfg),
        [((T, D + AW), BF)],
        [meta] + o + [out_weight, out_adapt_in],
        scratch=[pltpu.VMEM((T, QW), BF)],
        us=3,
        name="out_proj",
    )
    units_f = Units(cfg, lo, [D] * 3, [cfg.F] * 3)
    ffn = ffn_call(
        cfg, units_f, meta, x, opart, swap_cores(opart), out_adapt_out, gain_f, gate_weight, up_weight,
        down_weight, gate_adapt_out, up_adapt_out, gate_adapt_in, up_adapt_in, down_adapt_in,
        down_adapt_out, cot,
    )
    mixed, dfn, dpart, oside, *parts_f = ffn
    dfn, *q_plane = after(dfn, *q_plane)
    parts_f = [parts_f[0]] + [permute(cfg, parts_f[j], j) for j in range(1, lo)]
    mg = call(
        functools.partial(mixed_grad_kernel, cfg),
        [((T, D), F32), ((2, S, D // 2), BF)] + [piece] * G,
        [meta, mixed, dfn, swap_cores(dfn), cot, gain_f]
        + o
        + [out_weight, out_adapt_in, out_adapt_out, oside],
        scratch=[pltpu.VMEM((T, QW), BF), pltpu.VMEM((G, T, gw), BF), pltpu.VMEM((T, D), BF)],
        us=4.5,
        name="mixed_grad",
    )
    grad_mixed, ograds, go_send = mg[0], mg[1], mg[2:]
    go_heads = to_heads(go_send)
    dpart, _ = after(dpart, go_send[0])
    (out_rows,) = call(
        functools.partial(output_kernel, cfg),
        [((T, D), BF)],
        [meta, mixed, dpart, swap_cores(dpart), down_adapt_out],
        us=2,
        name="output",
    )
    out_rows, *both = after(out_rows, *parts_f, *go_heads)
    parts_f, go_heads = both[:lo], both[lo:]
    sum_f = add(parts_f)
    message = G * T + -(-2 * cfg.groups * cfg.NT // 16) * 16
    (go_all,) = call(
        functools.partial(scale_kernel, cfg),
        [((message, gw), BF)],
        [meta] + go_heads + [linv, o_all],
        scratch=[
            pltpu.VMEM((cfg.NT, cfg.QH, gw), F32),
            pltpu.VMEM((cfg.groups * cfg.NT, gw), F32),
        ],
        us=2,
        name="scale",
    )
    go_plane = to_plane(go_all)
    dq_send = call(
        functools.partial(grad_query_kernel, cfg),
        [piece] * G,
        [meta] + q + kv + [go_all, o_all],
        scratch=[tiles(cfg.KT), tiles(cfg.QH), tiles(cfg.QH), tiles(cfg.QH)],
        us=13.5,
        name="grad_query",
    )
    near, far = upper_bits(cfg)[1], upper_bits(cfg)[0]
    got_f, *dq_send = after(permute(cfg, sum_f, near), *dq_send)
    sum_f = add([sum_f, got_f])
    dq = to_heads(dq_send)
    dkv_send = call(
        functools.partial(grad_key_kernel, cfg),
        [piece] * G,
        [meta, kv[0]] + q_plane + go_plane,
        scratch=[tiles(cfg.QH), tiles(cfg.KT), tiles(cfg.KT)]
        + [pltpu.VMEM((cfg.NT, 16, cfg.KT), F32)],
        us=16,
        name="grad_key",
    )
    got_f, *both = after(permute(cfg, sum_f, far), *dq, *dkv_send)
    dq, dkv_send = both[:G], both[G:]
    sum_f = add([sum_f, got_f])
    dkv = to_heads(dkv_send)
    pieces_f = to_plane(sum_f)

    qpart, bgrad_q, akeep_q, asend_q = call(
        functools.partial(query_back_kernel, cfg),
        [((T, D), F32), ((S, QW), BF), ((S, D // 2), BF), ((S, D // 2), BF)],
        [meta]
        + dq
        + [
            normed, qraw, sides, cos, sin, qg, query_weight, query_adapt_in, query_adapt_out,
        ],
        scratch=[pltpu.VMEM((T, QW), BF), pltpu.VMEM((S, D), F32)],
        us=3.5,
        name="query_back",
    )
    dnormed, bgrad_kv, akeep_kv, asend_kv = call(
        functools.partial(key_value_back_kernel, cfg),
        [((T, D), BF), ((S, 2 * KW), BF), ((2 * S, D // 2), BF), ((2 * S, D // 2), BF)],
        [meta]
        + dkv
        + [
            normed, kraw, sides, cos, sin, kg, key_weight, value_weight, key_adapt_in,
            value_adapt_in, key_adapt_out, value_adapt_out, qpart,
        ],
        scratch=[pltpu.VMEM((T, 2 * KW), BF), pltpu.VMEM((2 * S, D), F32)],
        us=4.5,
        name="key_value_back",
    )
    (input_rows,) = call(
        functools.partial(input_grad_kernel, cfg),
        [((T, D), BF)],
        [meta, x, gain_a, grad_mixed, dnormed, swap_cores(dnormed)],
        us=3,
        name="input_grad",
    )

    def expand(units, pieces, plan, halves, outs, name):
        theirs = swap_cores(jnp.stack([value[: units.us] for value in pieces]))
        return call(
            functools.partial(expand_kernel, cfg, units, plan, halves),
            outs,
            [meta] + pieces + [theirs],
            scratch=[pltpu.VMEM((units.n, units.u, 16, 128), BF)],
            us=4,
            name=name,
        )

    units_q = Units(cfg, lo, [D // 2] * 4, [QW, QW, KW, KW])
    dnormed, bgrad_kv, *pieces_f = after(dnormed, bgrad_kv, *pieces_f)
    parts_q = call(
        functools.partial(pack_qkv_kernel, cfg, units_q),
        [((units_q.u, 16, 128), BF)] * lo,
        [meta, akeep_q, swap_cores(asend_q), akeep_kv, swap_cores(asend_kv), ograds, bgrad_q]
        + [bgrad_kv],
        scratch=[pltpu.VMEM((lo, units_q.u, 16, 128), BF)],
        us=2,
        name="pack_qkv",
    )
    sum_q = add([parts_q[0]] + [permute(cfg, parts_q[j], j) for j in range(1, lo)])
    for bit in upper_bits(cfg):
        sum_q = add([sum_q, permute(cfg, sum_q, bit)])
    pieces_q = to_plane(sum_q)
    gate_in, up_in, down_out, gate_out, up_out, down_in = expand(
        units_f,
        pieces_f,
        [(0, 0, True), (0, 1, True), (0, 2, False), (1, 0, False), (1, 1, False), (1, 2, True)],
        False,
        [((D, AW), F32), ((D, AW), F32), ((AW, D), F32)]
        + [((AW, cfg.F), F32), ((AW, cfg.F), F32), ((cfg.F, AW), F32)],
        "expand_ffn",
    )
    query_in, key_in, value_in, out_out, out_in, query_out, key_out, value_out = expand(
        units_q,
        pieces_q,
        [(0, 0, True), (0, 1, True), (0, 2, True), (0, 3, False)]
        + [(1, 0, True), (1, 1, False), (1, 2, False), (1, 3, False)],
        True,
        [((D, AW), F32)] * 3
        + [((AW, D), F32), ((QW, AW), F32), ((AW, QW), F32), ((AW, KW), F32), ((AW, KW), F32)],
        "expand_qkv",
    )
    return (
        out_rows.reshape(T, 1, D),
        input_rows.reshape(T, 1, D),
        query_in,
        query_out,
        key_in,
        key_out,
        value_in,
        value_out,
        out_in,
        out_out,
        gate_in,
        gate_out,
        up_in,
        up_out,
        down_in,
        down_out,
    )


def solution(mesh):
    return jax.shard_map(
        per_device,
        mesh=mesh,
        in_specs=(
            P(None, "ctx", None), P(), P(None, "wa"), P(None, "wa"), P(None, "wa"), P(), P(),
            P("wa", None), P(), P(None, "wa"), P(None, "wa"), P("wa", None), P(), P(None, "wa"),
            P(), P(None, "wa"), P(), P(None, "wa"), P("wa", None), P(), P(), P(None, "wa"), P(),
            P(None, "wa"), P("wa", None), P(), P(), P(), P(None, "ctx", None),
        ),
        out_specs=(
            P(None, "ctx", None), P(None, "ctx", None), P(), P(None, "wa"), P(), P(None, "wa"), P(),
            P(None, "wa"), P("wa", None), P(), P(), P(None, "wa"), P(), P(None, "wa"),
            P("wa", None), P(),
        ),
        check_vma=False,
    )
```

```python
import functools
import math

import jax
import jax.numpy as jnp
import numpy as np
from jax import lax
from jax.experimental import pallas as pl
from jax.experimental.pallas import tpu as pltpu
from jax.sharding import PartitionSpec as P

RANK = 16
DOC_MIN = 200

norm_eps = 1e-05
theta_base = 1000000.0
BF = jnp.bfloat16
F32 = jnp.float32
LOG2E = 1.4426950408889634
STEP = 3
VMEM_SMALL = 28 * 1024 * 1024
VMEM_LARGE = 56 * 1024 * 1024


def mm(left, right):
    return jnp.dot(left, right, preferred_element_type=F32)


def mm_nt(left, right):
    return lax.dot_general(left, right, (((1,), (1,)), ((), ())), preferred_element_type=F32)


def mm_tn(left, right):
    return lax.dot_general(left, right, (((0,), (0,)), ((), ())), preferred_element_type=F32)


def iota(shape, dim):
    return lax.broadcasted_iota(jnp.int32, shape, dim)


class Cfg:
    def __init__(self, tokens, n_ctx, heads_kv, groups, head_dim, docs, adapt_width, width, hidden):
        self.T = tokens
        self.n = n_ctx
        self.G = heads_kv
        self.lo = n_ctx // heads_kv
        self.groups = groups
        self.hd = head_dim
        self.docs = docs
        self.AW = adapt_width
        self.slots = min(docs, adapt_width // RANK)
        self.S = self.slots * RANK
        self.D = width
        self.F = hidden
        self.R = max(16, min(tokens, 512 // n_ctx))
        self.NT = tokens // self.R
        self.span = self.R * n_ctx
        self.QH = self.G * self.R
        self.KT = n_ctx * self.R


class Meta:
    def __init__(self, extra, adapter):
        self.refs, self.docs = (extra, adapter), extra.shape[0]

    def __getitem__(self, i):
        if i < 2:
            return lax.axis_index(("ctx", "wa")[i])
        return self.refs[(i - 2) // self.docs][(i - 2) % self.docs]


def with_meta(kernel):
    return lambda extra, adapter, *refs: kernel(Meta(extra, adapter), *refs)


def doc_starts(cfg, meta):
    out = [jnp.int32(0)]
    for j in range(cfg.docs):
        out.append(out[-1] + meta[2 + j] + (DOC_MIN - 1))
    return out


def start_of(starts, token):
    out = jnp.zeros_like(token)
    for s in starts[1:-1]:
        out = jnp.where(token >= s, s, out)
    return out


def end_of(starts, token):
    out = starts[1]
    for j in range(1, len(starts) - 1):
        out = jnp.where(token >= starts[j], starts[j + 1], out)
    return out


def adapter_mask(cfg, meta):
    token = iota((cfg.T, cfg.AW), 0) * cfg.n + meta[0]
    starts = doc_starts(cfg, meta)
    adapter = jnp.full((cfg.T, cfg.AW), meta[2 + cfg.docs], jnp.int32)
    for j in range(1, cfg.docs):
        adapter = jnp.where(token >= starts[j], meta[2 + cfg.docs + j], adapter)
    return (adapter == iota((cfg.T, cfg.AW), 1) // RANK).astype(F32)


def slot_select(cfg, meta):
    row = iota((cfg.AW, cfg.S), 0)
    col = iota((cfg.AW, cfg.S), 1)
    if cfg.S == cfg.AW:
        return (row == col).astype(BF)
    target = jnp.full((cfg.AW, cfg.S), -1, jnp.int32)
    for s in range(cfg.slots):
        mine = meta[2 + cfg.docs + s]
        again = jnp.int32(0)
        for e in range(s):
            again = jnp.where(meta[2 + cfg.docs + e] == mine, 1, again)
        base = jnp.where(again == 1, -4 * cfg.AW, mine * RANK)
        target = jnp.where(col // RANK == s, base + col % RANK, target)
    return (row == target).astype(BF)


def block_mean(values, hd):
    width = values.shape[1]
    ones = (iota((width, width), 0) // hd == iota((width, width), 1) // hd).astype(BF)
    high = values.astype(BF)
    low = (values - high.astype(F32)).astype(BF)
    return (mm(high, ones) + mm(low, ones)) * (1.0 / hd)


def swap_halves(values, hd):
    width = values.shape[1]
    half = hd // 2
    first = iota(values.shape, 1) % hd < half
    return jnp.where(first, pltpu.roll(values, width - half, 1), pltpu.roll(values, half, 1))


def lanes(values, copies):
    return jnp.concatenate([values] * copies, axis=1) if copies > 1 else values


def params(large=False, **kw):
    limit = VMEM_SMALL if lax.axis_size("ctx") <= 16 and not large else VMEM_LARGE
    return pltpu.CompilerParams(vmem_limit_bytes=limit, **kw)


SMEM = pl.BlockSpec(memory_space=pltpu.SMEM)


def cost(us):
    return pl.CostEstimate(flops=int(us * 1.15e9), bytes_accessed=0, transcendentals=0)


def call(kernel, outs, ins, scratch=(), us=1.0, name=None, large=False):
    ins = [*ins[0], *ins[1:]]
    return pl.pallas_call(
        with_meta(kernel),
        out_shape=[jax.ShapeDtypeStruct(s, d) for s, d in outs],
        in_specs=[SMEM] * 2 + [pl.BlockSpec(memory_space=pltpu.VMEM)] * (len(ins) - 2),
        out_specs=[pl.BlockSpec(memory_space=pltpu.VMEM)] * len(outs),
        scratch_shapes=list(scratch),
        compiler_params=params(large),
        cost_estimate=cost(us),
        name=name,
    )(*ins)


def pre_kernel(
    cfg, meta, x_ref, gain, wq, wk, wv, aq, ak, av, bq, bk, bv, qg, kg, inverse, *refs
):
    G, hd = cfg.G, cfg.hd
    kv_out, q_out = refs[:G], refs[G : 2 * G]
    qraw_ref, kraw_ref, sides_ref, normed_ref, cos, sin, kv_scr, q_scr = refs[2 * G :]
    hi = meta[0] // cfg.lo
    shape = cos.shape
    token = iota(shape, 0) * cfg.n + meta[0]
    angle = (token - start_of(doc_starts(cfg, meta), token)).astype(F32) * inverse[...]
    cos[...] = jnp.cos(angle)
    sin[...] = jnp.sin(angle) * jnp.where(iota(shape, 1) % hd < hd // 2, -1.0, 1.0)
    x = x_ref[...].astype(F32)
    rr = lax.rsqrt(jnp.mean(x * x, axis=-1, keepdims=True) + norm_eps)
    normed = (x * rr * gain[...]).astype(BF)
    normed_ref[...] = normed
    mask = adapter_mask(cfg, meta)
    select = slot_select(cfg, meta)
    raws = []
    for i, (w, a, b) in enumerate(((wq, aq, bq), (wk, ak, bk), (wv, av, bv))):
        side = (mask * mm(normed, a[...])).astype(BF)
        sides_ref[i] = mm(side, select).astype(BF)
        raws.append(mm(normed, w[...]) + mm(side, b[...]))
    qraw, kraw, vraw = raws
    qraw_ref[...] = qraw
    kraw_ref[...] = kraw

    def prep(raw, g):
        copies = raw.shape[1] // hd
        scaled = raw * lax.rsqrt(block_mean(raw * raw, hd) + norm_eps) * lanes(g[...], copies)
        per = raw.shape[1] // cos.shape[1]
        return scaled * lanes(cos[...], per) + swap_halves(scaled, hd) * lanes(sin[...], per)

    query = prep(qraw, qg).astype(BF)
    key = prep(kraw, kg).astype(BF)
    value = vraw.astype(BF)
    gw = cfg.groups * hd
    for h in range(G):
        q_scr[h] = query[:, h * gw : (h + 1) * gw]
        kv_scr[h] = jnp.concatenate(
            [key[:, h * hd : (h + 1) * hd], value[:, h * hd : (h + 1) * hd]], axis=1
        )
    for k in range(G):
        kv_out[k][...] = kv_scr[hi ^ k]
        q_out[k][...] = q_scr[hi ^ k]


def tile_of(cfg, pieces, t):
    rows = pl.ds(pl.multiple_of(t * cfg.R, cfg.R), cfg.R)
    return jnp.concatenate([piece[rows, :] for piece in pieces], axis=0)


def list_items(cfg, starts, items):
    def per_query(qt, count):
        def one(s, at):
            items[0, at] = qt
            items[1, at] = s
            return at + 1

        return lax.fori_loop(start_of(starts, qt * cfg.span) // cfg.span, qt + 1, one, count)

    count = lax.fori_loop(0, cfg.NT, per_query, 0)
    for i in range(STEP - 1):
        items[0, count + i] = 0
        items[1, count + i] = cfg.NT - 1
    return (count + STEP - 1) // STEP


def items_scratch(cfg):
    return pltpu.SMEM((2, cfg.NT * (cfg.NT + 1) // 2 + STEP), jnp.int32)


def split_pieces(ref, count):
    return [ref.at[i] for i in range(count)]


def message_pieces(cfg, ref):
    return [ref.at[pl.ds(k * cfg.T, cfg.T)] for k in range(cfg.G)]


def token_in_span(cfg, meta, index):
    hi, lo = meta[0] // cfg.lo, meta[0] % cfg.lo
    piece, row = index // cfg.R, index % cfg.R
    j, k = piece // cfg.G, piece % cfg.G
    return row * cfg.n + (hi ^ k) * cfg.lo + (lo ^ j)


def pad_queries(cfg, qq, side):
    hd = cfg.hd
    wide = qq.astype(F32)
    first = iota(wide.shape, 1) < hd
    rolled = pltpu.roll(wide, hd, 1)
    if side == 0:
        parts = [jnp.where(first, wide, 0.0), jnp.where(first, rolled, 0.0)]
    else:
        parts = [jnp.where(first, 0.0, rolled), jnp.where(first, 0.0, wide)]
    return jnp.concatenate(parts, axis=0).astype(BF)


def attend_kernel(cfg, meta, *refs):
    G, R, hd, QH = cfg.G, cfg.R, cfg.hd, cfg.QH
    q_in, own, others = refs[:G], refs[G], refs[G + 1 : G + cfg.lo]
    rest = refs[G + cfg.lo :]
    o_out, o_all, linv, q_scr, acc_scr, items = rest[:G], *rest[G:]
    kv_pieces = split_pieces(own, G)
    for ref in others:
        kv_pieces = kv_pieces + split_pieces(ref, G)
    starts = doc_starts(cfg, meta)
    steps = list_items(cfg, starts, items)
    scale = hd ** (-0.5) * LOG2E
    key_off = token_in_span(cfg, meta, iota((1, cfg.KT), 1))
    row_off = token_in_span(cfg, meta, iota((2 * QH, 1), 0) % QH)
    key_lanes = iota((cfg.KT, 2 * hd), 1) < hd
    for t in range(cfg.NT):
        q_scr[t] = pad_queries(cfg, tile_of(cfg, q_in, t), 0)
        acc_scr[t] = jnp.zeros((2 * QH, 2 * hd), F32)

    def step(i, carry):
        parts = []
        for u in range(STEP):
            qt, s = items[0, i * STEP + u], items[1, i * STEP + u]
            kv = tile_of(cfg, kv_pieces, s)
            token = row_off + qt * cfg.span
            key_token = key_off + s * cfg.span
            e = jnp.exp2(mm_nt(q_scr[qt], kv) * scale)
            e = jnp.where((key_token <= token) & (key_token >= start_of(starts, token)), e, 0.0)
            parts.append((qt, mm(e.astype(BF), jnp.where(key_lanes, jnp.ones_like(kv), kv))))
        for qt, part in parts:
            acc_scr[qt] += part
        return carry

    lax.fori_loop(0, steps, step, 0)
    half = iota((QH, 2 * hd), 1) < hd
    for t in range(cfg.NT):
        acc = acc_scr[t]
        inv0 = 1.0 / acc[:QH]
        inv1 = 1.0 / acc[QH:]
        out0 = pltpu.roll(acc[:QH], hd, 1) * inv0
        out1 = acc[QH:] * pltpu.roll(inv1, hd, 1)
        out = jnp.where(half, out0, out1).astype(BF)
        inv = jnp.where(half, inv0, pltpu.roll(inv1, hd, 1))
        rows = slice(t * R, (t + 1) * R)
        for k in range(G):
            o_out[k][rows, :] = out[k * R : (k + 1) * R]
            o_all[k, rows, :] = out[k * R : (k + 1) * R]
            linv[k, rows, :] = inv[k * R : (k + 1) * R]


def head_sums(cfg, prod):
    pick = (iota((16, prod.shape[1]), 1) // cfg.hd == iota((16, prod.shape[1]), 0)).astype(BF)
    high = prod.astype(BF)
    low = (prod - high.astype(F32)).astype(BF)
    return mm_nt(pick, high) + mm_nt(pick, low)


def scale_kernel(cfg, meta, *refs):
    G, T, R, NT, QH = cfg.G, cfg.T, cfg.R, cfg.NT, cfg.QH
    go, linv, o_all, out, scr, delta = refs[:G], refs[G], refs[G + 1], refs[G + 2], *refs[G + 3 :]
    delta[...] = jnp.zeros_like(delta)
    for k in range(G):
        scaled = (go[k][...].astype(F32) * linv[k]).astype(BF)
        out[k * T : (k + 1) * T, :] = scaled
        prod = scaled.astype(F32) * o_all[k].astype(F32)
        for t in range(NT):
            scr[t, k * R : (k + 1) * R, :] = prod[t * R : (t + 1) * R]
    for t in range(NT):
        sums = head_sums(cfg, scr[t])
        for h in range(cfg.groups):
            delta[h * NT + t : h * NT + t + 1, :QH] = sums[h : h + 1]
    high = delta[...].astype(BF)
    at = G * T
    rows = cfg.groups * NT
    out[at : at + rows, :] = high
    out[at + rows : at + 2 * rows, :] = (delta[...] - high.astype(F32)).astype(BF)


def grad_query_kernel(cfg, meta, *refs):
    G, R, hd, QH = cfg.G, cfg.R, cfg.hd, cfg.QH
    q_in, own, others = refs[:G], refs[G], refs[G + 1 : G + cfg.lo]
    go_ref, o_ref = refs[G + cfg.lo : G + cfg.lo + 2]
    rest = refs[G + cfg.lo + 2 :]
    dq_out, q_scr, go_scr, delta_scr, acc_scr, items = rest[:G], *rest[G:]
    kv_pieces = split_pieces(own, G)
    for ref in others:
        kv_pieces = kv_pieces + split_pieces(ref, G)
    starts = doc_starts(cfg, meta)
    steps = list_items(cfg, starts, items)
    scale = hd ** (-0.5) * LOG2E
    key_off = token_in_span(cfg, meta, iota((1, cfg.KT), 1))
    row_off = token_in_span(cfg, meta, iota((2 * QH, 1), 0) % QH)
    half = iota((QH, 2 * hd), 1) < hd
    for t in range(cfg.NT):
        go = tile_of(cfg, message_pieces(cfg, go_ref), t)
        prod = go.astype(F32) * tile_of(cfg, split_pieces(o_ref, G), t).astype(F32)
        q_scr[t] = pad_queries(cfg, tile_of(cfg, q_in, t), 0)
        go_scr[t] = pad_queries(cfg, go, 1)
        delta_scr[t, :QH] = jnp.sum(jnp.where(half, prod, 0.0), axis=1, keepdims=True)
        delta_scr[t, QH:] = jnp.sum(jnp.where(half, 0.0, prod), axis=1, keepdims=True)
        acc_scr[t] = jnp.zeros((2 * QH, 2 * hd), F32)

    def step(i, carry):
        parts = []
        for u in range(STEP):
            qt, s = items[0, i * STEP + u], items[1, i * STEP + u]
            kv = tile_of(cfg, kv_pieces, s)
            token = row_off + qt * cfg.span
            key_token = key_off + s * cfg.span
            e = jnp.exp2(mm_nt(q_scr[qt], kv) * scale)
            ds = e * (mm_nt(go_scr[qt], kv) - delta_scr[qt])
            ds = jnp.where((key_token <= token) & (key_token >= start_of(starts, token)), ds, 0.0)
            parts.append((qt, mm(ds.astype(BF), kv)))
        for qt, part in parts:
            acc_scr[qt] += part
        return carry

    lax.fori_loop(0, steps, step, 0)
    for t in range(cfg.NT):
        acc = acc_scr[t]
        out = jnp.where(half, acc[:QH], pltpu.roll(acc[QH:], hd, 1)) * hd ** (-0.5)
        out = out.astype(BF)
        for k in range(G):
            dq_out[k][t * R : (t + 1) * R, :] = out[k * R : (k + 1) * R]


def grad_key_kernel(cfg, meta, *refs):
    G, T, R, hd, lo, QH, NT = cfg.G, cfg.T, cfg.R, cfg.hd, cfg.lo, cfg.QH, cfg.NT
    own = refs[0]
    q_refs, go_refs = (refs[1 + i * lo : 1 + (i + 1) * lo] for i in range(2))
    rest = refs[1 + 2 * lo :]
    dkv_out, key_scr, value_scr, delta_scr, gk_scr, gv_scr, items = rest[:G], *rest[G:]
    q_pieces = [piece for ref in q_refs for piece in split_pieces(ref, G)]
    go_pieces = [piece for ref in go_refs for piece in message_pieces(cfg, ref)]
    starts = doc_starts(cfg, meta)
    steps = list_items(cfg, starts, items)
    scale = hd ** (-0.5) * LOG2E
    rows = cfg.groups * NT
    for j in range(lo):
        sums = go_refs[j][G * T : G * T + 2 * rows, :].astype(F32)
        sums = sums[:rows] + sums[rows:]
        for t in range(NT):
            for h in range(cfg.groups):
                at = h * NT + t
                delta_scr[t, h : h + 1, j * QH : (j + 1) * QH] = sums[at : at + 1, :QH]
    query_off = token_in_span(cfg, meta, iota((1, cfg.KT), 1))
    row_off = token_in_span(cfg, meta, iota((2 * QH, 1), 0) % QH)
    first = iota((QH, 2 * hd), 1) < hd
    for t in range(NT):
        kv = tile_of(cfg, split_pieces(own, G), t).astype(F32)
        rolled = pltpu.roll(kv, hd, 1)
        keys = [jnp.where(first, kv, 0.0), jnp.where(first, 0.0, rolled)]
        values = [jnp.where(first, rolled, 0.0), jnp.where(first, 0.0, kv)]
        key_scr[t] = jnp.concatenate(keys, axis=0).astype(BF)
        value_scr[t] = jnp.concatenate(values, axis=0).astype(BF)
        gk_scr[t] = jnp.zeros((2 * QH, 2 * hd), F32)
        gv_scr[t] = jnp.zeros((2 * QH, 2 * hd), F32)

    def step(i, carry):
        parts = []
        for u in range(STEP):
            t, kt = items[0, i * STEP + u], items[1, i * STEP + u]
            queries, grads = tile_of(cfg, q_pieces, t), tile_of(cfg, go_pieces, t)
            key_token = row_off + kt * cfg.span
            token = query_off + t * cfg.span
            e = jnp.exp2(mm_nt(key_scr[kt], queries) * scale)
            e = jnp.where((key_token <= token) & (key_token >= start_of(starts, token)), e, 0.0)
            dp = mm_nt(value_scr[kt], grads)
            delta = delta_scr[t]
            ds = [
                (e[:QH] * (dp[:QH] - delta[0:1])).astype(BF),
                (e[QH:] * (dp[QH:] - delta[1:2])).astype(BF),
            ]
            ds = jnp.concatenate(ds, axis=0)
            parts.append((kt, mm(ds, queries), mm(e.astype(BF), grads)))
        for kt, gk, gv in parts:
            gk_scr[kt] += gk
            gv_scr[kt] += gv
        return carry

    lax.fori_loop(0, steps, step, 0)
    for t in range(NT):
        gk, gv = gk_scr[t], gv_scr[t]
        gk = (gk[:QH] + pltpu.roll(gk[QH:], hd, 1)) * hd ** (-0.5)
        gv = pltpu.roll(gv[:QH], hd, 1) + gv[QH:]
        out = jnp.where(first, gk, gv).astype(BF)
        for k in range(G):
            dkv_out[k][t * R : (t + 1) * R, :] = out[k * R : (k + 1) * R]


def place_pieces(cfg, hi, scr, pieces):
    w = pieces[0].shape[1]
    for k in range(cfg.G):
        at = pl.multiple_of((hi ^ k) * w, w)
        scr[:, pl.ds(at, w)] = pieces[k][...]


def out_kernel(cfg, meta, *refs):
    G = cfg.G
    wo, ao, part, attn = refs[G:]
    place_pieces(cfg, meta[0] // cfg.lo, attn, refs[:G])
    rows = attn[...]
    part[:, : cfg.D] = mm(rows, wo[...]).astype(BF)
    part[:, cfg.D :] = mm(rows, ao[...]).astype(BF)


def hidden_grad_kernel(cfg, meta, cot_ref, wd, bd, ad, out, turned):
    cot = cot_ref[...]
    side = (adapter_mask(cfg, meta) * mm_nt(cot, bd[...])).astype(BF)
    turned[...] = mm(side, slot_select(cfg, meta)).T.astype(BF)
    tile = 256
    for f in range(0, cfg.F, tile):
        at = slice(f, f + tile)
        out[:, at] = mm_nt(cot, wd[at, :]) + mm_nt(side, ad[at, :])


def ffn_kernel(
    cfg, units, meta, x_ref, own, other, bo, gain, wg, wu, wd, bg, bu, ag, au, ad, cot_ref, gh, gst,
    mixed_ref, dfn_ref, part_ref, oside, *refs,
):
    D, F = cfg.D, cfg.F
    chunks, (hidden_scr, gg_scr, gu_scr, grads) = refs[: units.n], refs[units.n :]
    flip = meta[0] % cfg.lo
    mask = adapter_mask(cfg, meta)
    select = slot_select(cfg, meta)
    compact = lambda side: mm(side, select).T.astype(BF)
    total = own[...].astype(F32) + other[...].astype(F32)
    out_side = (mask * total[:, D:]).astype(BF)
    oside[...] = mm(out_side, select).astype(BF)
    mixed = x_ref[...].astype(F32) + total[:, :D] + mm(out_side, bo[...])
    mixed_ref[...] = mixed
    rr = lax.rsqrt(jnp.mean(mixed * mixed, axis=-1, keepdims=True) + norm_eps)
    normed = (mixed * rr * gain[...]).astype(BF)
    side_g = (mask * mm(normed, ag[...])).astype(BF)
    side_u = (mask * mm(normed, au[...])).astype(BF)
    turned = compact(side_g), compact(side_u), gst[...]
    tile = 256
    for f in range(0, F, tile):
        at = slice(f, f + tile)
        grad_hidden = gh[:, at]
        gate = mm(normed, wg[:, at]) + mm(side_g, bg[:, at])
        upper = mm(normed, wu[:, at]) + mm(side_u, bu[:, at])
        sigma = 1.0 / (1.0 + jnp.exp(-gate))
        silu = gate * sigma
        hidden = (silu * upper).astype(BF)
        grad_gate = (grad_hidden * upper * (sigma + silu * (1.0 - sigma))).astype(BF)
        grad_upper = (grad_hidden * silu).astype(BF)
        hidden_scr[:, at] = hidden
        gg_scr[:, at] = grad_gate
        gu_scr[:, at] = grad_upper
    side_g = (mask * mm_nt(gg_scr[...], bg[...])).astype(BF)
    side_u = (mask * mm_nt(gu_scr[...], bu[...])).astype(BF)
    side_sum = mm(hidden_scr[...], ad[...])
    for d in range(0, D, tile):
        at = slice(d, d + tile)
        dfn = mm_nt(gg_scr[...], wg[at, :]) + mm_nt(gu_scr[...], wu[at, :])
        dfn_ref[:, at] = (dfn + mm_nt(side_g, ag[at, :]) + mm_nt(side_u, au[at, :])).astype(BF)
    for d in range(0, D, tile):
        at = slice(d, d + tile)
        part_ref[:, at] = mm(hidden_scr[...], wd[:, at]).astype(BF)
    part_ref[:, D:] = side_sum.astype(BF)
    side_d = (mask * side_sum).astype(BF)
    for i, (side, right) in enumerate(((side_g, normed), (side_u, normed), (side_d, cot_ref[...]))):
        units.store(grads, 0, i, mm(compact(side), right).astype(BF))
    for i, right in enumerate((gg_scr, gu_scr, hidden_scr)):
        units.store(grads, 1, i, mm(turned[i], right[...]).astype(BF))
    units.clear_spare(grads)
    for j, chunk in enumerate(chunks):
        chunk[...] = grads[j ^ flip]


def ffn_call(cfg, units, meta, *ins):
    T, D, F, AW, S = cfg.T, cfg.D, cfg.F, cfg.AW, cfg.S
    return call(
        functools.partial(ffn_kernel, cfg, units),
        [((T, D), F32), ((T, D), BF), ((T, D + AW), BF), ((T, S), BF)]
        + [((units.u, 16, 128), BF)] * units.n,
        [meta, *ins],
        scratch=[pltpu.VMEM((T, F), BF)] * 3 + [pltpu.VMEM((units.n, units.u, 16, 128), BF)],
        us=14,
        name="ffn",
    )


def mixed_grad_kernel(cfg, meta, *refs):
    G, D = cfg.G, cfg.D
    mixed_ref, own, other, cot, gain = refs[:5]
    o_in = refs[5 : 5 + G]
    wo, ao, bo, oside = refs[5 + G : 9 + G]
    rest = refs[9 + G :]
    gm_ref, ograds, go_out, attn, go_scr, gm_scr = rest[0], rest[1], rest[2 : 2 + G], *rest[2 + G :]
    hi = meta[0] // cfg.lo
    mixed = mixed_ref[...]
    w = (own[...].astype(F32) + other[...].astype(F32)) * gain[...]
    rr = lax.rsqrt(jnp.mean(mixed * mixed, axis=-1, keepdims=True) + norm_eps)
    inner = jnp.mean(w * mixed, axis=-1, keepdims=True)
    gm = cot[...].astype(F32) + rr * w - (rr * rr * rr * inner) * mixed
    gm_ref[...] = gm
    gmb = gm.astype(BF)
    gm_scr[...] = gmb
    mask = adapter_mask(cfg, meta)
    select = slot_select(cfg, meta)
    grad_side = (mask * mm_nt(gmb, bo[...])).astype(BF)
    go = (mm_nt(gmb, wo[...]) + mm_nt(grad_side, ao[...])).astype(BF)
    w = cfg.groups * cfg.hd
    for h in range(G):
        go_scr[h] = go[:, h * w : (h + 1) * w]
    for k in range(G):
        go_out[k][...] = go_scr[hi ^ k]
    place_pieces(cfg, hi, attn, o_in)
    ograds[0] = mm(mm(grad_side, select).T.astype(BF), attn[...]).astype(BF)
    half = D // 2
    mine = gm_scr[:, pl.ds(pl.multiple_of(meta[1] * half, half), half)]
    ograds[1] = mm(oside[...].astype(F32).T.astype(BF), mine).astype(BF)


def output_kernel(cfg, meta, mixed, own, other, bd, out_ref):
    D = cfg.D
    total = own[...].astype(F32) + other[...].astype(F32)
    side = (adapter_mask(cfg, meta) * total[:, D:]).astype(BF)
    out_ref[...] = (mixed[...] + total[:, :D] + mm(side, bd[...])).astype(BF)


def head_back(cfg, cos, sin, grad, raw, g):
    hd = cfg.hd
    copies = raw.shape[1] // hd
    per = raw.shape[1] // cos.shape[1]
    un = grad * lanes(cos[...], per) - swap_halves(grad, hd) * lanes(sin[...], per)
    w = un * lanes(g[...], copies)
    rr = lax.rsqrt(block_mean(raw * raw, hd) + norm_eps)
    return rr * w - rr * rr * rr * raw * block_mean(w * raw, hd)


def half_lanes(cfg, meta):
    half = cfg.D // 2
    keep = pl.ds(pl.multiple_of(meta[1] * half, half), half)
    send = pl.ds(pl.multiple_of((1 - meta[1]) * half, half), half)
    return keep, send


def query_back_kernel(cfg, meta, *refs):
    G, S = cfg.G, cfg.S
    normed, raw, sides, cos, sin, gain, w, a, b, part, bgrad, akeep, asend, dq_scr, a_scr = refs[G:]
    place_pieces(cfg, meta[0] // cfg.lo, dq_scr, refs[:G])
    g = head_back(cfg, cos, sin, dq_scr[...].astype(F32), raw[...], gain).astype(BF)
    select = slot_select(cfg, meta)
    grad_side = (adapter_mask(cfg, meta) * mm_nt(g, b[...])).astype(BF)
    part[...] = mm_nt(g, w[...]) + mm_nt(grad_side, a[...])
    a_scr[...] = mm(mm(grad_side, select).T.astype(BF), normed[...])
    bgrad[...] = mm(sides[0].astype(F32).T.astype(BF), g).astype(BF)
    keep, send = half_lanes(cfg, meta)
    akeep[...] = a_scr[:, keep].astype(BF)
    asend[...] = a_scr[:, send].astype(BF)


def key_value_back_kernel(cfg, meta, *refs):
    G, S, hd = cfg.G, cfg.S, cfg.hd
    (
        normed, raw, sides, cos, sin, gain, wk, wv, ak, av, bk, bv, qpart,
        part, bgrad, akeep, asend, dkv_scr, a_scr,
    ) = refs[G:]
    place_pieces(cfg, meta[0] // cfg.lo, dkv_scr, refs[:G])
    mask = adapter_mask(cfg, meta)
    select = slot_select(cfg, meta)
    dkv = dkv_scr[...]
    dk = jnp.concatenate([dkv[:, 2 * h * hd : (2 * h + 1) * hd] for h in range(G)], axis=1)
    dv = jnp.concatenate([dkv[:, (2 * h + 1) * hd : (2 * h + 2) * hd] for h in range(G)], axis=1)
    gk = head_back(cfg, cos, sin, dk.astype(F32), raw[...], gain).astype(BF)
    total = qpart[...]
    width = gk.shape[1]
    for i, (g, w, a, b) in enumerate(((gk, wk, ak, bk), (dv, wv, av, bv))):
        grad_side = (mask * mm_nt(g, b[...])).astype(BF)
        total = total + mm_nt(g, w[...]) + mm_nt(grad_side, a[...])
        a_scr[i * S : (i + 1) * S, :] = mm(mm(grad_side, select).T.astype(BF), normed[...])
        bgrad[:, i * width : (i + 1) * width] = mm(
            sides[i + 1].astype(F32).T.astype(BF), g
        ).astype(BF)
    part[...] = total.astype(BF)
    keep, send = half_lanes(cfg, meta)
    akeep[...] = a_scr[:, keep].astype(BF)
    asend[...] = a_scr[:, send].astype(BF)


def input_grad_kernel(cfg, meta, x_ref, gain, gm, own, other, out):
    x = x_ref[...].astype(F32)
    w = (own[...].astype(F32) + other[...].astype(F32)) * gain[...]
    rr = lax.rsqrt(jnp.mean(x * x, axis=-1, keepdims=True) + norm_eps)
    inner = jnp.mean(w * x, axis=-1, keepdims=True)
    out[...] = (gm[...] + rr * w - (rr * rr * rr * inner) * x).astype(BF)


class Units:
    def __init__(self, cfg, n, shared, private):
        self.n = n
        self.high = cfg.S // 16
        self.shared, self.private = shared, private
        self.us, self.up = self.per_chunk(shared), self.per_chunk(private)
        self.u = self.us + self.up

    def per_chunk(self, widths):
        return -(-sum(w // 128 for w in widths) * self.high // self.n)

    def places(self, which):
        widths, per, base = (
            (self.shared, self.us, 0) if which == 0 else (self.private, self.up, self.us)
        )
        at, out = 0, []
        for w in widths:
            spots = []
            for c in range(w // 128):
                for a in range(self.high):
                    spots.append((at // per, base + at % per, a, c))
                    at += 1
            out.append(spots)
        return out

    def spare(self):
        out = []
        for widths, per, base in ((self.shared, self.us, 0), (self.private, self.up, self.us)):
            count = sum(w // 128 for w in widths) * self.high
            out += [(i // per, base + i % per) for i in range(count, per * self.n)]
        return out

    def store(self, out, which, array, values, first=0):
        widths, per, base = (
            (self.shared, self.us, 0) if which == 0 else (self.private, self.up, self.us)
        )
        at = sum(w // 128 for w in widths[:array]) * self.high + first * self.high
        for c in range(values.shape[1] // 128):
            for a in range(self.high):
                unit = at + c * self.high + a
                out[unit // per, base + unit % per] = values[
                    a * 16 : a * 16 + 16, c * 128 : c * 128 + 128
                ]

    def clear_spare(self, out):
        for chunk, off in self.spare():
            out[chunk, off] = jnp.zeros((16, 128), BF)


def pack(units, scr, flip, outs, arrays):
    for i, values in enumerate(arrays):
        which = int(i >= len(units.shared))
        units.store(scr, which, i - which * len(units.shared), values)
    units.clear_spare(scr)
    for j, out in enumerate(outs):
        out[...] = scr[j ^ flip]


def add_halves(keep, got, count):
    total = (keep[...].astype(F32) + got[...].astype(F32)).astype(BF)
    rows = total.shape[0] // count
    return [total[i * rows : (i + 1) * rows] for i in range(count)]


def pack_qkv_kernel(cfg, units, meta, keep_q, got_q, keep, got, ograds, bq, bkv, *outs):
    scr, outs = outs[-1], outs[:-1]
    kw = bkv.shape[1] // 2
    shared = add_halves(keep_q, got_q, 1) + add_halves(keep, got, 2) + [ograds[1]]
    private = [ograds[0], bq[...], bkv[:, :kw], bkv[:, kw:]]
    pack(units, scr, meta[0] % cfg.lo, outs, shared + private)


def unpack(ref, spots):
    cols = {}
    for chunk, off, a, c in spots:
        cols.setdefault(c, []).append(ref[chunk, off])
    return jnp.concatenate([jnp.concatenate(cols[c], axis=0) for c in sorted(cols)], axis=1)


def expand_kernel(cfg, units, plan, halves, meta, *refs):
    own_in, other_in, outs = refs[: cfg.lo], refs[cfg.lo], refs[cfg.lo + 1 : -2]
    own, other = refs[-2:]
    flip = meta[0] % cfg.lo
    for j in range(cfg.lo):
        own[j ^ flip] = own_in[j][...]
        other[j ^ flip] = other_in[j]
    wa = meta[1]
    select = slot_select(cfg, meta)

    def write(out, values, transposed, at):
        full = mm(select, values)
        if transposed:
            out[at : at + full.shape[1], :] = full.T
        else:
            out[:, at : at + full.shape[1]] = full

    for (which, i, transposed), out in zip(plan, outs):
        spots = units.places(which)[i]
        mine = unpack(own, spots)
        if which == 1:
            write(out, mine, transposed, 0)
        else:
            theirs = unpack(other, spots)
            if not halves:
                total = mine.astype(F32) + theirs.astype(F32)
                write(out, total.astype(BF), transposed, 0)
                continue
            width = mine.shape[1]
            write(out, jnp.where(wa == 0, mine, theirs), transposed, 0)
            write(out, jnp.where(wa == 0, theirs, mine), transposed, width)


def upper_bits(cfg):
    bits, bit = [], cfg.n // 2
    while bit >= cfg.lo:
        bits.append(bit)
        bit //= 2
    return bits


def after(*values):
    return lax.optimization_barrier(values)


def swap_cores(value):
    return lax.ppermute(value, "wa", [(0, 1), (1, 0)])


def permute(cfg, value, bits):
    return lax.ppermute(value, "ctx", [(i, i ^ bits) for i in range(cfg.n)])


def per_device(
    hidden_in, attn_gain, query_weight, key_weight, value_weight, query_gain, key_gain, out_weight,
    ffn_gain, gate_weight, up_weight, down_weight, query_adapt_in, query_adapt_out, key_adapt_in,
    key_adapt_out, value_adapt_in, value_adapt_out, out_adapt_in, out_adapt_out, gate_adapt_in,
    gate_adapt_out, up_adapt_in, up_adapt_out, down_adapt_in, down_adapt_out, document_extra,
    document_adapter, cotangent,
):
    head_dim = query_gain.shape[0]
    cfg = Cfg(
        tokens=hidden_in.shape[0],
        n_ctx=lax.axis_size("ctx"),
        heads_kv=key_weight.shape[1] // head_dim,
        groups=query_weight.shape[1] // key_weight.shape[1],
        head_dim=head_dim,
        docs=document_extra.shape[0],
        adapt_width=query_adapt_in.shape[1],
        width=hidden_in.shape[2],
        hidden=gate_weight.shape[1],
    )
    T, D, G, S, AW, n, lo = cfg.T, cfg.D, cfg.G, cfg.S, cfg.AW, cfg.n, cfg.lo
    gw = cfg.groups * head_dim
    QW, KW = query_weight.shape[1], key_weight.shape[1]
    meta = (document_extra, document_adapter)
    x = hidden_in.reshape(T, D)
    cot = cotangent.reshape(T, D)
    gain_a = attn_gain.reshape(1, D)
    gain_f = ffn_gain.reshape(1, D)
    qg = query_gain.reshape(1, head_dim)
    kg = key_gain.reshape(1, head_dim)

    lane = np.arange(2 * head_dim) % (head_dim // 2)
    inverse = np.exp(lane * (-2.0 * math.log(theta_base) / head_dim)).astype(np.float32)[None, :]

    piece = ((T, gw), BF)
    pre = call(
        functools.partial(pre_kernel, cfg),
        [piece] * (2 * G)
        + [((T, QW), F32), ((T, KW), F32), ((3, T, S), BF), ((T, D), BF)]
        + [((T, 2 * head_dim), F32)] * 2,
        [
            meta, x, gain_a, query_weight, key_weight, value_weight, query_adapt_in, key_adapt_in,
            value_adapt_in, query_adapt_out, key_adapt_out, value_adapt_out, qg, kg, inverse,
        ],
        scratch=[pltpu.VMEM((G, T, gw), BF), pltpu.VMEM((G, T, gw), BF)],
        us=6,
        name="pre",
        large=True,
    )
    kv_send, q_send = pre[:G], pre[G : 2 * G]
    qraw, kraw, sides, normed, cos, sin = pre[2 * G :]

    def to_heads(pieces):
        return [pieces[0]] + [permute(cfg, pieces[k], k * lo) for k in range(1, G)]

    def add(values):
        return sum(value.astype(F32) for value in values).astype(BF)

    def to_plane(value):
        return [value] + [permute(cfg, value, j) for j in range(1, lo)]

    kv = to_plane(jnp.stack(to_heads(kv_send)))
    q = to_heads(q_send)
    grad_hidden, gst = call(
        functools.partial(hidden_grad_kernel, cfg),
        [((T, cfg.F), F32), ((S, T), BF)],
        [meta, cot, down_weight, down_adapt_out, down_adapt_in],
        us=3,
        name="hidden_grad",
    )
    grad_hidden, *both = after(grad_hidden, *kv, *q)
    kv, q = both[:lo], both[lo:]
    tiles = lambda dtype, width=gw: pltpu.VMEM((cfg.NT, 2 * cfg.QH, width), dtype)
    attn = call(
        functools.partial(attend_kernel, cfg),
        [piece] * G + [((G, T, gw), BF), ((G, T, gw), F32)],
        [meta] + q + kv,
        scratch=[tiles(BF), tiles(F32), items_scratch(cfg)],
        us=12,
        name="attend",
    )
    o_send, o_all, linv = attn[:G], attn[G], attn[G + 1]
    o = to_heads(o_send)
    q_stack, _ = after(jnp.stack(q), o_send[0])
    q_plane = to_plane(q_stack)
    (opart,) = call(
        functools.partial(out_kernel, cfg),
        [((T, D + AW), BF)],
        [meta] + o + [out_weight, out_adapt_in],
        scratch=[pltpu.VMEM((T, QW), BF)],
        us=3,
        name="out_proj",
    )
    units_f = Units(cfg, lo, [D] * 3, [cfg.F] * 3)
    ffn = ffn_call(
        cfg, units_f, meta, x, opart, swap_cores(opart), out_adapt_out, gain_f, gate_weight, up_weight,
        down_weight, gate_adapt_out, up_adapt_out, gate_adapt_in, up_adapt_in, down_adapt_in,
        cot, grad_hidden, gst,
    )
    mixed, dfn, dpart, oside, *parts_f = ffn
    dfn, *q_plane = after(dfn, *q_plane)
    mg = call(
        functools.partial(mixed_grad_kernel, cfg),
        [((T, D), F32), ((2, S, D // 2), BF)] + [piece] * G,
        [meta, mixed, dfn, swap_cores(dfn), cot, gain_f]
        + o
        + [out_weight, out_adapt_in, out_adapt_out, oside],
        scratch=[pltpu.VMEM((T, QW), BF), pltpu.VMEM((G, T, gw), BF), pltpu.VMEM((T, D), BF)],
        us=0.01,
        name="mixed_grad",
    )
    grad_mixed, ograds, go_send = mg[0], mg[1], mg[2:]
    go_heads = to_heads(go_send)
    parts_f = [parts_f[0]] + [permute(cfg, parts_f[j], j) for j in range(1, lo)]
    message = G * T + -(-2 * cfg.groups * cfg.NT // 16) * 16
    (go_all,) = call(
        functools.partial(scale_kernel, cfg),
        [((message, gw), BF)],
        [meta] + go_heads + [linv, o_all],
        scratch=[
            pltpu.VMEM((cfg.NT, cfg.QH, gw), F32),
            pltpu.VMEM((cfg.groups * cfg.NT, gw), F32),
        ],
        us=0.01,
        name="scale",
    )
    go_all, *parts_f = after(go_all, *parts_f)
    sum_f = add(parts_f)
    go_plane = to_plane(go_all)
    dq_send = call(
        functools.partial(grad_query_kernel, cfg),
        [piece] * G,
        [meta] + q + kv + [go_all, o_all],
        scratch=[tiles(BF), tiles(BF), tiles(F32, 1), tiles(F32), items_scratch(cfg)],
        us=13.5,
        name="grad_query",
    )
    near, far = upper_bits(cfg)[1], upper_bits(cfg)[0]
    got_f, *dq_send = after(permute(cfg, sum_f, near), *dq_send)
    sum_f = add([sum_f, got_f])
    dq = to_heads(dq_send)
    dkv_send = call(
        functools.partial(grad_key_kernel, cfg),
        [piece] * G,
        [meta, kv[0]] + q_plane + go_plane,
        scratch=[tiles(BF), tiles(BF), pltpu.VMEM((cfg.NT, 16, cfg.KT), F32), tiles(F32)]
        + [tiles(F32), items_scratch(cfg)],
        us=16,
        name="grad_key",
    )
    got_f, *both = after(permute(cfg, sum_f, far), *dq, *dkv_send)
    dq, dkv_send = both[:G], both[G:]
    sum_f = add([sum_f, got_f])
    dkv = to_heads(dkv_send)
    all_f = [sum_f] + [permute(cfg, sum_f, j) for j in range(1, lo - 1)]
    dpart, _ = after(dpart, dkv_send[0])
    (out_rows,) = call(
        functools.partial(output_kernel, cfg),
        [((T, D), BF)],
        [meta, mixed, dpart, swap_cores(dpart), down_adapt_out],
        us=0.01,
        name="output",
    )
    out_rows, *dkv = after(out_rows, *dkv)

    qpart, bgrad_q, akeep_q, asend_q = call(
        functools.partial(query_back_kernel, cfg),
        [((T, D), F32), ((S, QW), BF), ((S, D // 2), BF), ((S, D // 2), BF)],
        [meta]
        + dq
        + [
            normed, qraw, sides, cos, sin, qg, query_weight, query_adapt_in, query_adapt_out,
        ],
        scratch=[pltpu.VMEM((T, QW), BF), pltpu.VMEM((S, D), F32)],
        us=0.01,
        name="query_back",
    )
    dnormed, bgrad_kv, akeep_kv, asend_kv = call(
        functools.partial(key_value_back_kernel, cfg),
        [((T, D), BF), ((S, 2 * KW), BF), ((2 * S, D // 2), BF), ((2 * S, D // 2), BF)],
        [meta]
        + dkv
        + [
            normed, kraw, sides, cos, sin, kg, key_weight, value_weight, key_adapt_in,
            value_adapt_in, key_adapt_out, value_adapt_out, qpart,
        ],
        scratch=[pltpu.VMEM((T, 2 * KW), BF), pltpu.VMEM((2 * S, D), F32)],
        us=0.01,
        name="key_value_back",
    )
    def expand(units, chunks, plan, halves, outs, name):
        theirs = swap_cores(jnp.stack([chunk[: units.us] for chunk in chunks]))
        return call(
            functools.partial(expand_kernel, cfg, units, plan, halves),
            outs,
            [meta, *chunks, theirs],
            scratch=[
                pltpu.VMEM((units.n, units.u, 16, 128), BF),
                pltpu.VMEM((units.n, units.us, 16, 128), BF),
            ],
            us=4,
            name=name,
        )

    dnormed, *all_f = after(dnormed, *all_f)
    units_q = Units(cfg, lo, [D // 2] * 4, [QW, QW, KW, KW])
    dn_other = swap_cores(dnormed)
    parts_q = call(
        functools.partial(pack_qkv_kernel, cfg, units_q),
        [((units_q.u, 16, 128), BF)] * lo,
        [meta, akeep_q, swap_cores(asend_q), akeep_kv, swap_cores(asend_kv), ograds, bgrad_q]
        + [bgrad_kv],
        scratch=[pltpu.VMEM((lo, units_q.u, 16, 128), BF)],
        us=0.01,
        name="pack_qkv",
    )
    sum_q = add([parts_q[0]] + [permute(cfg, parts_q[j], j) for j in range(1, lo)])
    sum_q, dn_other, sum_f = after(sum_q, dn_other, sum_f)
    all_f = all_f + [permute(cfg, sum_f, lo - 1)]
    (input_rows,) = call(
        functools.partial(input_grad_kernel, cfg),
        [((T, D), BF)],
        [meta, x, gain_a, grad_mixed, dnormed, dn_other],
        us=0.01,
        name="input_grad",
    )
    got_q, input_rows = after(permute(cfg, sum_q, near), input_rows)
    sum_q = add([sum_q, got_q])
    got_q, all_f[-1] = after(permute(cfg, sum_q, far), all_f[-1])
    pieces_q = to_plane(add([sum_q, got_q]))
    gate_in, up_in, down_out, gate_out, up_out, down_in = expand(
        units_f,
        all_f,
        [(0, 0, True), (0, 1, True), (0, 2, False), (1, 0, False), (1, 1, False), (1, 2, True)],
        False,
        [((D, AW), F32), ((D, AW), F32), ((AW, D), F32)]
        + [((AW, cfg.F), F32), ((AW, cfg.F), F32), ((cfg.F, AW), F32)],
        "expand_ffn",
    )
    down_out, *pieces_q = after(down_out, *pieces_q)
    query_in, key_in, value_in, out_out, out_in, query_out, key_out, value_out = expand(
        units_q,
        pieces_q,
        [(0, 0, True), (0, 1, True), (0, 2, True), (0, 3, False)]
        + [(1, 0, True), (1, 1, False), (1, 2, False), (1, 3, False)],
        True,
        [((D, AW), F32)] * 3
        + [((AW, D), F32), ((QW, AW), F32), ((AW, QW), F32), ((AW, KW), F32), ((AW, KW), F32)],
        "expand_qkv",
    )
    return (
        out_rows.reshape(T, 1, D),
        input_rows.reshape(T, 1, D),
        query_in,
        query_out,
        key_in,
        key_out,
        value_in,
        value_out,
        out_in,
        out_out,
        gate_in,
        gate_out,
        up_in,
        up_out,
        down_in,
        down_out,
    )


def solution(mesh):
    return jax.shard_map(
        per_device,
        mesh=mesh,
        in_specs=(
            P(None, "ctx", None), P(), P(None, "wa"), P(None, "wa"), P(None, "wa"), P(), P(),
            P("wa", None), P(), P(None, "wa"), P(None, "wa"), P("wa", None), P(), P(None, "wa"),
            P(), P(None, "wa"), P(), P(None, "wa"), P("wa", None), P(), P(), P(None, "wa"), P(),
            P(None, "wa"), P("wa", None), P(), P(), P(), P(None, "ctx", None),
        ),
        out_specs=(
            P(None, "ctx", None), P(None, "ctx", None), P(), P(None, "wa"), P(), P(None, "wa"), P(),
            P(None, "wa"), P("wa", None), P(), P(), P(None, "wa"), P(), P(None, "wa"),
            P("wa", None), P(),
        ),
        check_vma=False,
    )
```

```python
import functools
import math

import jax
import jax.numpy as jnp
import numpy as np
from jax import lax
from jax.experimental import pallas as pl
from jax.experimental.pallas import tpu as pltpu
from jax.sharding import PartitionSpec as P

RANK = 16
DOC_MIN = 200

norm_eps = 1e-05
theta_base = 1000000.0
BF = jnp.bfloat16
F32 = jnp.float32
LOG2E = 1.4426950408889634
STEP = 11
VMEM_SMALL = 28 * 1024 * 1024
VMEM_LARGE = 56 * 1024 * 1024


def mm(left, right):
    return jnp.dot(left, right, preferred_element_type=F32)


def mm_nt(left, right):
    return lax.dot_general(left, right, (((1,), (1,)), ((), ())), preferred_element_type=F32)


def mm_tn(left, right):
    return lax.dot_general(left, right, (((0,), (0,)), ((), ())), preferred_element_type=F32)


def iota(shape, dim):
    return lax.broadcasted_iota(jnp.int32, shape, dim)


class Cfg:
    def __init__(self, tokens, n_ctx, heads_kv, groups, head_dim, docs, adapt_width, width, hidden):
        self.T = tokens
        self.n = n_ctx
        self.G = heads_kv
        self.lo = n_ctx // heads_kv
        self.groups = groups
        self.hd = head_dim
        self.docs = docs
        self.AW = adapt_width
        self.slots = min(docs, adapt_width // RANK)
        self.S = self.slots * RANK
        self.D = width
        self.F = hidden
        self.R = max(16, min(tokens, 512 // n_ctx))
        self.NT = tokens // self.R
        self.span = self.R * n_ctx
        self.QH = self.G * self.R
        self.KT = n_ctx * self.R


class Meta:
    def __init__(self, extra, adapter, items=None):
        self.refs, self.docs, self.items = (extra, adapter), extra.shape[0], items

    def __getitem__(self, i):
        if i < 2:
            return lax.axis_index(("ctx", "wa")[i])
        return self.refs[(i - 2) // self.docs][(i - 2) % self.docs]


def with_meta(kernel, count):
    return lambda *refs: kernel(Meta(*refs[:count]), *refs[count:])


def doc_starts(cfg, meta):
    out = [jnp.int32(0)]
    for j in range(cfg.docs):
        out.append(out[-1] + meta[2 + j] + (DOC_MIN - 1))
    return out


def start_of(starts, token):
    out = jnp.zeros_like(token)
    for s in starts[1:-1]:
        out = jnp.where(token >= s, s, out)
    return out


def end_of(starts, token):
    out = starts[1]
    for j in range(1, len(starts) - 1):
        out = jnp.where(token >= starts[j], starts[j + 1], out)
    return out


def adapter_mask(cfg, meta):
    token = iota((cfg.T, cfg.AW), 0) * cfg.n + meta[0]
    starts = doc_starts(cfg, meta)
    adapter = jnp.full((cfg.T, cfg.AW), meta[2 + cfg.docs], jnp.int32)
    for j in range(1, cfg.docs):
        adapter = jnp.where(token >= starts[j], meta[2 + cfg.docs + j], adapter)
    return (adapter == iota((cfg.T, cfg.AW), 1) // RANK).astype(F32)


def slot_select(cfg, meta):
    row = iota((cfg.AW, cfg.S), 0)
    col = iota((cfg.AW, cfg.S), 1)
    if cfg.S == cfg.AW:
        return (row == col).astype(BF)
    target = jnp.full((cfg.AW, cfg.S), -1, jnp.int32)
    for s in range(cfg.slots):
        mine = meta[2 + cfg.docs + s]
        again = jnp.int32(0)
        for e in range(s):
            again = jnp.where(meta[2 + cfg.docs + e] == mine, 1, again)
        base = jnp.where(again == 1, -4 * cfg.AW, mine * RANK)
        target = jnp.where(col // RANK == s, base + col % RANK, target)
    return (row == target).astype(BF)


def block_mean(values, hd):
    width = values.shape[1]
    ones = (iota((width, width), 0) // hd == iota((width, width), 1) // hd).astype(BF)
    high = values.astype(BF)
    low = (values - high.astype(F32)).astype(BF)
    return (mm(high, ones) + mm(low, ones)) * (1.0 / hd)


def swap_halves(values, hd):
    width = values.shape[1]
    half = hd // 2
    first = iota(values.shape, 1) % hd < half
    return jnp.where(first, pltpu.roll(values, width - half, 1), pltpu.roll(values, half, 1))


def lanes(values, copies):
    return jnp.concatenate([values] * copies, axis=1) if copies > 1 else values


def params(large=False, **kw):
    limit = VMEM_SMALL if lax.axis_size("ctx") <= 16 and not large else VMEM_LARGE
    return pltpu.CompilerParams(vmem_limit_bytes=limit, **kw)


SMEM = pl.BlockSpec(memory_space=pltpu.SMEM)


def cost(us):
    return pl.CostEstimate(flops=int(us * 1.15e9), bytes_accessed=0, transcendentals=0)


def call(kernel, outs, ins, scratch=(), us=1.0, name=None, large=False, in_place=0, lists=0):
    count = len(ins[0])
    ins = [*ins[0], *ins[1:]]
    return pl.pallas_call(
        with_meta(kernel, count),
        out_shape=[jax.ShapeDtypeStruct(s, d) for s, d in outs],
        in_specs=[SMEM] * count
        + [pl.BlockSpec(memory_space=pl.ANY)] * in_place
        + [pl.BlockSpec(memory_space=pltpu.VMEM)] * (len(ins) - count - in_place),
        out_specs=[pl.BlockSpec(memory_space=pltpu.VMEM)] * (len(outs) - lists) + [SMEM] * lists,
        scratch_shapes=list(scratch),
        compiler_params=params(large),
        cost_estimate=cost(us),
        name=name,
    )(*ins)


def head_prep(cfg, cos, sin, raw, g):
    hd = cfg.hd
    copies = raw.shape[1] // hd
    scaled = raw * lax.rsqrt(block_mean(raw * raw, hd) + norm_eps) * lanes(g[...], copies)
    per = raw.shape[1] // cos.shape[1]
    return scaled * lanes(cos[...], per) + swap_halves(scaled, hd) * lanes(sin[...], per)


def key_value_kernel(cfg, meta, *refs):
    G, hd = cfg.G, cfg.hd
    sources, (gain, kg, inverse), refs = refs[:7], refs[7:10], refs[10:]
    kv_out, refs = refs[:G], refs[G:]
    raw_ref, sides_ref, normed_ref, cos, sin, *scratch = refs
    buffers, sems, kv_scr = scratch[:7], scratch[7], scratch[8]
    copies = [
        pltpu.make_async_copy(source, buffer, sems.at[i])
        for i, (source, buffer) in enumerate(zip(sources, buffers))
    ]
    for copy in copies:
        copy.start()
    x_buf, ak, av, wk, bk, wv, bv = buffers
    shape = cos.shape
    token = iota(shape, 0) * cfg.n + meta[0]
    angle = (token - start_of(doc_starts(cfg, meta), token)).astype(F32) * inverse[...]
    cos[...] = jnp.cos(angle)
    sin[...] = jnp.sin(angle) * jnp.where(iota(shape, 1) % hd < hd // 2, -1.0, 1.0)
    mask = adapter_mask(cfg, meta)
    select = slot_select(cfg, meta)
    copies[0].wait()
    x = x_buf[...].astype(F32)
    rr = lax.rsqrt(jnp.mean(x * x, axis=-1, keepdims=True) + norm_eps)
    normed = (x * rr * gain[...]).astype(BF)
    normed_ref[...] = normed
    for copy in copies[1:]:
        copy.wait()
    raws = []
    for i, (w, a, b) in enumerate(((wk, ak, bk), (wv, av, bv))):
        side = (mask * mm(normed, a[...])).astype(BF)
        sides_ref[i] = mm(side, select).astype(BF)
        raws.append(mm(normed, w[...]) + mm(side, b[...]))
    kraw, vraw = raws
    raw_ref[...] = kraw
    key = head_prep(cfg, cos, sin, kraw, kg).astype(BF)
    value = vraw.astype(BF)
    for h in range(G):
        at = slice(h * hd, (h + 1) * hd)
        kv_scr[h] = jnp.concatenate([key[:, at], value[:, at]], axis=1)
    hi = meta[0] // cfg.lo
    for k in range(G):
        kv_out[k][...] = kv_scr[hi ^ k]


def query_kernel(cfg, meta, normed_ref, cos, sin, w, a, b, g, *refs):
    G = cfg.G
    q_out, raw_ref, side_ref, items, q_scr = refs[:G], *refs[G:]
    list_items(cfg, doc_starts(cfg, meta), items)
    normed = normed_ref[...]
    side = (adapter_mask(cfg, meta) * mm(normed, a[...])).astype(BF)
    side_ref[0] = mm(side, slot_select(cfg, meta)).astype(BF)
    raw = mm(normed, w[...]) + mm(side, b[...])
    raw_ref[...] = raw
    query = head_prep(cfg, cos, sin, raw, g).astype(BF)
    gw = cfg.groups * cfg.hd
    for h in range(G):
        q_scr[h] = query[:, h * gw : (h + 1) * gw]
    hi = meta[0] // cfg.lo
    for k in range(G):
        q_out[k][...] = q_scr[hi ^ k]


def tile_of(cfg, pieces, t):
    rows = pl.ds(pl.multiple_of(t * cfg.R, cfg.R), cfg.R)
    return jnp.concatenate([piece[rows, :] for piece in pieces], axis=0)


def list_items(cfg, starts, items):
    def per_query(qt, count):
        def one(s, at):
            items[0, at] = qt
            items[1, at] = s
            return at + 1

        return lax.fori_loop(start_of(starts, qt * cfg.span) // cfg.span, qt + 1, one, count)

    count = lax.fori_loop(0, cfg.NT, per_query, 0)
    for i in range(STEP - 1):
        items[0, count + i] = 0
        items[1, count + i] = cfg.NT - 1
    items[0, items.shape[1] - 1] = (count + STEP - 1) // STEP


def items_shape(cfg):
    return ((2, cfg.NT * (cfg.NT + 1) // 2 + STEP), jnp.int32)


def split_pieces(ref, count):
    return [ref.at[i] for i in range(count)]


def message_pieces(cfg, ref):
    return [ref.at[pl.ds(k * cfg.T, cfg.T)] for k in range(cfg.G)]


def token_in_span(cfg, meta, index):
    hi, lo = meta[0] // cfg.lo, meta[0] % cfg.lo
    piece, row = index // cfg.R, index % cfg.R
    j, k = piece // cfg.G, piece % cfg.G
    return row * cfg.n + (hi ^ k) * cfg.lo + (lo ^ j)


def pad_queries(cfg, qq, side):
    hd = cfg.hd
    wide = qq.astype(F32)
    first = iota(wide.shape, 1) < hd
    rolled = pltpu.roll(wide, hd, 1)
    if side == 0:
        parts = [jnp.where(first, wide, 0.0), jnp.where(first, rolled, 0.0)]
    else:
        parts = [jnp.where(first, 0.0, rolled), jnp.where(first, 0.0, wide)]
    return jnp.concatenate(parts, axis=0).astype(BF)


def attend_kernel(cfg, meta, *refs):
    G, R, hd, QH = cfg.G, cfg.R, cfg.hd, cfg.QH
    q_in, own, others = refs[:G], refs[G], refs[G + 1 : G + cfg.lo]
    rest = refs[G + cfg.lo :]
    o_out, o_all, linv, q_scr, acc_scr = rest[:G], *rest[G:]
    kv_pieces = split_pieces(own, G)
    for ref in others:
        kv_pieces = kv_pieces + split_pieces(ref, G)
    starts = doc_starts(cfg, meta)
    items = meta.items
    scale = hd ** (-0.5) * LOG2E
    key_off = token_in_span(cfg, meta, iota((1, cfg.KT), 1))
    row_off = token_in_span(cfg, meta, iota((2 * QH, 1), 0) % QH)
    key_lanes = iota((cfg.KT, 2 * hd), 1) < hd
    for t in range(cfg.NT):
        q_scr[t] = pad_queries(cfg, tile_of(cfg, q_in, t), 0)
        acc_scr[t] = jnp.zeros((2 * QH, 2 * hd), F32)

    def step(i, carry):
        parts = []
        for u in range(STEP):
            qt, s = items[0, i * STEP + u], items[1, i * STEP + u]
            kv = tile_of(cfg, kv_pieces, s)
            token = row_off + qt * cfg.span
            key_token = key_off + s * cfg.span
            e = jnp.exp2(mm_nt(q_scr[qt], kv) * scale)
            e = jnp.where((key_token <= token) & (key_token >= start_of(starts, token)), e, 0.0)
            parts.append((qt, mm(e.astype(BF), jnp.where(key_lanes, jnp.ones_like(kv), kv))))
        for qt, part in parts:
            acc_scr[qt] += part
        return carry

    lax.fori_loop(0, items[0, items.shape[1] - 1], step, 0)
    half = iota((QH, 2 * hd), 1) < hd
    for t in range(cfg.NT):
        acc = acc_scr[t]
        inv0 = 1.0 / acc[:QH]
        inv1 = 1.0 / acc[QH:]
        out0 = pltpu.roll(acc[:QH], hd, 1) * inv0
        out1 = acc[QH:] * pltpu.roll(inv1, hd, 1)
        out = jnp.where(half, out0, out1).astype(BF)
        inv = jnp.where(half, inv0, pltpu.roll(inv1, hd, 1))
        rows = slice(t * R, (t + 1) * R)
        for k in range(G):
            o_out[k][rows, :] = out[k * R : (k + 1) * R]
            o_all[k, rows, :] = out[k * R : (k + 1) * R]
            linv[k, rows, :] = inv[k * R : (k + 1) * R]


def head_sums(cfg, prod):
    pick = (iota((16, prod.shape[1]), 1) // cfg.hd == iota((16, prod.shape[1]), 0)).astype(BF)
    high = prod.astype(BF)
    low = (prod - high.astype(F32)).astype(BF)
    return mm_nt(pick, high) + mm_nt(pick, low)


def scale_kernel(cfg, meta, *refs):
    G, T, R, NT, QH = cfg.G, cfg.T, cfg.R, cfg.NT, cfg.QH
    go, linv, o_all, out, scr, delta = refs[:G], refs[G], refs[G + 1], refs[G + 2], *refs[G + 3 :]
    delta[...] = jnp.zeros_like(delta)
    for k in range(G):
        scaled = (go[k][...].astype(F32) * linv[k]).astype(BF)
        out[k * T : (k + 1) * T, :] = scaled
        prod = scaled.astype(F32) * o_all[k].astype(F32)
        for t in range(NT):
            scr[t, k * R : (k + 1) * R, :] = prod[t * R : (t + 1) * R]
    for t in range(NT):
        sums = head_sums(cfg, scr[t])
        for h in range(cfg.groups):
            delta[h * NT + t : h * NT + t + 1, :QH] = sums[h : h + 1]
    high = delta[...].astype(BF)
    at = G * T
    rows = cfg.groups * NT
    out[at : at + rows, :] = high
    out[at + rows : at + 2 * rows, :] = (delta[...] - high.astype(F32)).astype(BF)


def grad_query_kernel(cfg, meta, *refs):
    G, R, hd, QH = cfg.G, cfg.R, cfg.hd, cfg.QH
    q_in, own, others = refs[:G], refs[G], refs[G + 1 : G + cfg.lo]
    go_ref, o_ref = refs[G + cfg.lo : G + cfg.lo + 2]
    rest = refs[G + cfg.lo + 2 :]
    dq_out, q_scr, go_scr, delta_scr, acc_scr = rest[:G], *rest[G:]
    kv_pieces = split_pieces(own, G)
    for ref in others:
        kv_pieces = kv_pieces + split_pieces(ref, G)
    starts = doc_starts(cfg, meta)
    items = meta.items
    scale = hd ** (-0.5) * LOG2E
    key_off = token_in_span(cfg, meta, iota((1, cfg.KT), 1))
    row_off = token_in_span(cfg, meta, iota((2 * QH, 1), 0) % QH)
    half = iota((QH, 2 * hd), 1) < hd
    for t in range(cfg.NT):
        go = tile_of(cfg, message_pieces(cfg, go_ref), t)
        prod = go.astype(F32) * tile_of(cfg, split_pieces(o_ref, G), t).astype(F32)
        q_scr[t] = pad_queries(cfg, tile_of(cfg, q_in, t), 0)
        go_scr[t] = pad_queries(cfg, go, 1)
        delta_scr[t, :QH] = jnp.sum(jnp.where(half, prod, 0.0), axis=1, keepdims=True)
        delta_scr[t, QH:] = jnp.sum(jnp.where(half, 0.0, prod), axis=1, keepdims=True)
        acc_scr[t] = jnp.zeros((2 * QH, 2 * hd), F32)

    def step(i, carry):
        parts = []
        for u in range(STEP):
            qt, s = items[0, i * STEP + u], items[1, i * STEP + u]
            kv = tile_of(cfg, kv_pieces, s)
            token = row_off + qt * cfg.span
            key_token = key_off + s * cfg.span
            e = jnp.exp2(mm_nt(q_scr[qt], kv) * scale)
            ds = e * (mm_nt(go_scr[qt], kv) - delta_scr[qt])
            ds = jnp.where((key_token <= token) & (key_token >= start_of(starts, token)), ds, 0.0)
            parts.append((qt, mm(ds.astype(BF), kv)))
        for qt, part in parts:
            acc_scr[qt] += part
        return carry

    lax.fori_loop(0, items[0, items.shape[1] - 1], step, 0)
    for t in range(cfg.NT):
        acc = acc_scr[t]
        out = jnp.where(half, acc[:QH], pltpu.roll(acc[QH:], hd, 1)) * hd ** (-0.5)
        out = out.astype(BF)
        for k in range(G):
            dq_out[k][t * R : (t + 1) * R, :] = out[k * R : (k + 1) * R]


def grad_key_kernel(cfg, meta, *refs):
    G, T, R, hd, lo, QH, NT = cfg.G, cfg.T, cfg.R, cfg.hd, cfg.lo, cfg.QH, cfg.NT
    own = refs[0]
    q_refs, go_refs = (refs[1 + i * lo : 1 + (i + 1) * lo] for i in range(2))
    rest = refs[1 + 2 * lo :]
    dkv_out, key_scr, value_scr, delta_scr, gk_scr, gv_scr = rest[:G], *rest[G:]
    q_pieces = [piece for ref in q_refs for piece in split_pieces(ref, G)]
    go_pieces = [piece for ref in go_refs for piece in message_pieces(cfg, ref)]
    starts = doc_starts(cfg, meta)
    items = meta.items
    scale = hd ** (-0.5) * LOG2E
    rows = cfg.groups * NT
    for j in range(lo):
        sums = go_refs[j][G * T : G * T + 2 * rows, :].astype(F32)
        sums = sums[:rows] + sums[rows:]
        for t in range(NT):
            for h in range(cfg.groups):
                at = h * NT + t
                delta_scr[t, h : h + 1, j * QH : (j + 1) * QH] = sums[at : at + 1, :QH]
    query_off = token_in_span(cfg, meta, iota((1, cfg.KT), 1))
    row_off = token_in_span(cfg, meta, iota((2 * QH, 1), 0) % QH)
    first = iota((QH, 2 * hd), 1) < hd
    for t in range(NT):
        kv = tile_of(cfg, split_pieces(own, G), t).astype(F32)
        rolled = pltpu.roll(kv, hd, 1)
        keys = [jnp.where(first, kv, 0.0), jnp.where(first, 0.0, rolled)]
        values = [jnp.where(first, rolled, 0.0), jnp.where(first, 0.0, kv)]
        key_scr[t] = jnp.concatenate(keys, axis=0).astype(BF)
        value_scr[t] = jnp.concatenate(values, axis=0).astype(BF)
        gk_scr[t] = jnp.zeros((2 * QH, 2 * hd), F32)
        gv_scr[t] = jnp.zeros((2 * QH, 2 * hd), F32)

    def step(i, carry):
        parts = []
        for u in range(STEP):
            t, kt = items[0, i * STEP + u], items[1, i * STEP + u]
            queries, grads = tile_of(cfg, q_pieces, t), tile_of(cfg, go_pieces, t)
            key_token = row_off + kt * cfg.span
            token = query_off + t * cfg.span
            e = jnp.exp2(mm_nt(key_scr[kt], queries) * scale)
            e = jnp.where((key_token <= token) & (key_token >= start_of(starts, token)), e, 0.0)
            dp = mm_nt(value_scr[kt], grads)
            delta = delta_scr[t]
            ds = [
                (e[:QH] * (dp[:QH] - delta[0:1])).astype(BF),
                (e[QH:] * (dp[QH:] - delta[1:2])).astype(BF),
            ]
            ds = jnp.concatenate(ds, axis=0)
            parts.append((kt, mm(ds, queries), mm(e.astype(BF), grads)))
        for kt, gk, gv in parts:
            gk_scr[kt] += gk
            gv_scr[kt] += gv
        return carry

    lax.fori_loop(0, items[0, items.shape[1] - 1], step, 0)
    for t in range(NT):
        gk, gv = gk_scr[t], gv_scr[t]
        gk = (gk[:QH] + pltpu.roll(gk[QH:], hd, 1)) * hd ** (-0.5)
        gv = pltpu.roll(gv[:QH], hd, 1) + gv[QH:]
        out = jnp.where(first, gk, gv).astype(BF)
        for k in range(G):
            dkv_out[k][t * R : (t + 1) * R, :] = out[k * R : (k + 1) * R]


def place_pieces(cfg, hi, scr, pieces):
    w = pieces[0].shape[1]
    for k in range(cfg.G):
        at = pl.multiple_of((hi ^ k) * w, w)
        scr[:, pl.ds(at, w)] = pieces[k][...]


def out_kernel(cfg, meta, *refs):
    G = cfg.G
    wo, ao, part, attn = refs[G:]
    place_pieces(cfg, meta[0] // cfg.lo, attn, refs[:G])
    rows = attn[...]
    part[:, : cfg.D] = mm(rows, wo[...]).astype(BF)
    part[:, cfg.D :] = mm(rows, ao[...]).astype(BF)


def hidden_grad_kernel(cfg, meta, cot_ref, wd, bd, ad, out, turned):
    cot = cot_ref[...]
    side = (adapter_mask(cfg, meta) * mm_nt(cot, bd[...])).astype(BF)
    turned[...] = mm(side, slot_select(cfg, meta)).T.astype(BF)
    tile = 256
    for f in range(0, cfg.F, tile):
        at = slice(f, f + tile)
        out[:, at] = mm_nt(cot, wd[at, :]) + mm_nt(side, ad[at, :])


def ffn_kernel(
    cfg, units, meta, x_ref, own, other, bo, gain, wg, wu, wd, bg, bu, ag, au, ad, cot_ref, gh, gst,
    mixed_ref, dfn_ref, part_ref, oside, *refs,
):
    D, F = cfg.D, cfg.F
    chunks, (hidden_scr, gg_scr, gu_scr, grads) = refs[: cfg.lo], refs[cfg.lo :]
    flip = meta[0] % cfg.lo
    mask = adapter_mask(cfg, meta)
    select = slot_select(cfg, meta)
    compact = lambda side: mm(side, select).T.astype(BF)
    total = own[...].astype(F32) + other[...].astype(F32)
    out_side = (mask * total[:, D:]).astype(BF)
    oside[...] = mm(out_side, select).astype(BF)
    mixed = x_ref[...].astype(F32) + total[:, :D] + mm(out_side, bo[...])
    mixed_ref[...] = mixed
    rr = lax.rsqrt(jnp.mean(mixed * mixed, axis=-1, keepdims=True) + norm_eps)
    normed = (mixed * rr * gain[...]).astype(BF)
    side_g = (mask * mm(normed, ag[...])).astype(BF)
    side_u = (mask * mm(normed, au[...])).astype(BF)
    turned = compact(side_g), compact(side_u), gst[...]
    tile = 256
    for f in range(0, F, tile):
        at = slice(f, f + tile)
        grad_hidden = gh[:, at]
        gate = mm(normed, wg[:, at]) + mm(side_g, bg[:, at])
        upper = mm(normed, wu[:, at]) + mm(side_u, bu[:, at])
        sigma = 1.0 / (1.0 + jnp.exp(-gate))
        silu = gate * sigma
        hidden = (silu * upper).astype(BF)
        grad_gate = (grad_hidden * upper * (sigma + silu * (1.0 - sigma))).astype(BF)
        grad_upper = (grad_hidden * silu).astype(BF)
        hidden_scr[:, at] = hidden
        gg_scr[:, at] = grad_gate
        gu_scr[:, at] = grad_upper
    side_g = (mask * mm_nt(gg_scr[...], bg[...])).astype(BF)
    side_u = (mask * mm_nt(gu_scr[...], bu[...])).astype(BF)
    side_sum = mm(hidden_scr[...], ad[...])
    for d in range(0, D, tile):
        at = slice(d, d + tile)
        dfn = mm_nt(gg_scr[...], wg[at, :]) + mm_nt(gu_scr[...], wu[at, :])
        dfn_ref[:, at] = (dfn + mm_nt(side_g, ag[at, :]) + mm_nt(side_u, au[at, :])).astype(BF)
    for d in range(0, D, tile):
        at = slice(d, d + tile)
        part_ref[:, at] = mm(hidden_scr[...], wd[:, at]).astype(BF)
    part_ref[:, D:] = side_sum.astype(BF)
    side_d = (mask * side_sum).astype(BF)
    for i, (side, right) in enumerate(((side_g, normed), (side_u, normed), (side_d, cot_ref[...]))):
        units.store(grads, 0, i, mm(compact(side), right).astype(BF))
    for i, right in enumerate((gg_scr, gu_scr, hidden_scr)):
        units.store(grads, 1, i, mm(turned[i], right[...]).astype(BF))
    units.clear_spare(grads)
    for j, chunk in enumerate(chunks):
        for half in range(2):
            chunk[half] = grads[2 * (j ^ flip) + half]


def ffn_call(cfg, units, meta, *ins):
    T, D, F, AW, S = cfg.T, cfg.D, cfg.F, cfg.AW, cfg.S
    return call(
        functools.partial(ffn_kernel, cfg, units),
        [((T, D), F32), ((T, D), BF), ((T, D + AW), BF), ((T, S), BF)]
        + [((2, units.u, 16, 128), BF)] * cfg.lo,
        [meta, *ins],
        scratch=[pltpu.VMEM((T, F), BF)] * 3 + [pltpu.VMEM((units.n, units.u, 16, 128), BF)],
        us=14,
        name="ffn",
    )


def mixed_grad_kernel(cfg, meta, *refs):
    G, D = cfg.G, cfg.D
    mixed_ref, own, other, cot, gain = refs[:5]
    o_in = refs[5 : 5 + G]
    wo, ao, bo, oside = refs[5 + G : 9 + G]
    rest = refs[9 + G :]
    gm_ref, ograds, go_out, attn, go_scr, gm_scr = rest[0], rest[1], rest[2 : 2 + G], *rest[2 + G :]
    hi = meta[0] // cfg.lo
    mixed = mixed_ref[...]
    w = (own[...].astype(F32) + other[...].astype(F32)) * gain[...]
    rr = lax.rsqrt(jnp.mean(mixed * mixed, axis=-1, keepdims=True) + norm_eps)
    inner = jnp.mean(w * mixed, axis=-1, keepdims=True)
    gm = cot[...].astype(F32) + rr * w - (rr * rr * rr * inner) * mixed
    gm_ref[...] = gm
    gmb = gm.astype(BF)
    gm_scr[...] = gmb
    mask = adapter_mask(cfg, meta)
    select = slot_select(cfg, meta)
    grad_side = (mask * mm_nt(gmb, bo[...])).astype(BF)
    go = (mm_nt(gmb, wo[...]) + mm_nt(grad_side, ao[...])).astype(BF)
    w = cfg.groups * cfg.hd
    for h in range(G):
        go_scr[h] = go[:, h * w : (h + 1) * w]
    for k in range(G):
        go_out[k][...] = go_scr[hi ^ k]
    place_pieces(cfg, hi, attn, o_in)
    ograds[0] = mm(mm(grad_side, select).T.astype(BF), attn[...]).astype(BF)
    half = D // 2
    mine = gm_scr[:, pl.ds(pl.multiple_of(meta[1] * half, half), half)]
    ograds[1] = mm(oside[...].astype(F32).T.astype(BF), mine).astype(BF)


def output_kernel(cfg, meta, mixed, own, other, bd, out_ref):
    D = cfg.D
    total = own[...].astype(F32) + other[...].astype(F32)
    side = (adapter_mask(cfg, meta) * total[:, D:]).astype(BF)
    out_ref[...] = (mixed[...] + total[:, :D] + mm(side, bd[...])).astype(BF)


def head_back(cfg, cos, sin, grad, raw, g):
    hd = cfg.hd
    copies = raw.shape[1] // hd
    per = raw.shape[1] // cos.shape[1]
    un = grad * lanes(cos[...], per) - swap_halves(grad, hd) * lanes(sin[...], per)
    w = un * lanes(g[...], copies)
    rr = lax.rsqrt(block_mean(raw * raw, hd) + norm_eps)
    return rr * w - rr * rr * rr * raw * block_mean(w * raw, hd)


def half_lanes(cfg, meta):
    half = cfg.D // 2
    keep = pl.ds(pl.multiple_of(meta[1] * half, half), half)
    send = pl.ds(pl.multiple_of((1 - meta[1]) * half, half), half)
    return keep, send


def query_back_kernel(cfg, meta, *refs):
    G, S = cfg.G, cfg.S
    normed, raw, sides, cos, sin, gain, w, a, b, part, bgrad, akeep, asend, dq_scr, a_scr = refs[G:]
    place_pieces(cfg, meta[0] // cfg.lo, dq_scr, refs[:G])
    g = head_back(cfg, cos, sin, dq_scr[...].astype(F32), raw[...], gain).astype(BF)
    select = slot_select(cfg, meta)
    grad_side = (adapter_mask(cfg, meta) * mm_nt(g, b[...])).astype(BF)
    part[...] = mm_nt(g, w[...]) + mm_nt(grad_side, a[...])
    a_scr[...] = mm(mm(grad_side, select).T.astype(BF), normed[...])
    bgrad[...] = mm(sides[0].astype(F32).T.astype(BF), g).astype(BF)
    keep, send = half_lanes(cfg, meta)
    akeep[...] = a_scr[:, keep].astype(BF)
    asend[...] = a_scr[:, send].astype(BF)


def key_value_side_kernel(cfg, meta, *refs):
    G, S, hd = cfg.G, cfg.S, cfg.hd
    normed, raw, cos, sin, gain, bk, bv, grads, out_sides, akeep, asend, dkv_scr, a_scr = refs[G:]
    place_pieces(cfg, meta[0] // cfg.lo, dkv_scr, refs[:G])
    mask = adapter_mask(cfg, meta)
    select = slot_select(cfg, meta)
    dkv = dkv_scr[...]
    dk = jnp.concatenate([dkv[:, 2 * h * hd : (2 * h + 1) * hd] for h in range(G)], axis=1)
    dv = jnp.concatenate([dkv[:, (2 * h + 1) * hd : (2 * h + 2) * hd] for h in range(G)], axis=1)
    gk = head_back(cfg, cos, sin, dk.astype(F32), raw[...], gain).astype(BF)
    for i, (g, b) in enumerate(((gk, bk), (dv, bv))):
        grad_side = (mask * mm_nt(g, b[...])).astype(BF)
        grads[i] = g
        out_sides[i] = grad_side
        a_scr[i * S : (i + 1) * S, :] = mm(mm(grad_side, select).T.astype(BF), normed[...])
    keep, send = half_lanes(cfg, meta)
    akeep[...] = a_scr[:, keep].astype(BF)
    asend[...] = a_scr[:, send].astype(BF)


def key_value_back_kernel(cfg, meta, grads, grad_sides, sides, wk, wv, ak, av, qpart, part, bgrad):
    total = qpart[...]
    width = grads.shape[2]
    for i, (w, a) in enumerate(((wk, ak), (wv, av))):
        total = total + mm_nt(grads[i], w[...]) + mm_nt(grad_sides[i], a[...])
        bgrad[:, i * width : (i + 1) * width] = mm(
            sides[i].astype(F32).T.astype(BF), grads[i]
        ).astype(BF)
    part[...] = total.astype(BF)


def input_grad_kernel(cfg, meta, x_ref, gain, gm, own, other, out):
    x = x_ref[...].astype(F32)
    w = (own[...].astype(F32) + other[...].astype(F32)) * gain[...]
    rr = lax.rsqrt(jnp.mean(x * x, axis=-1, keepdims=True) + norm_eps)
    inner = jnp.mean(w * x, axis=-1, keepdims=True)
    out[...] = (gm[...] + rr * w - (rr * rr * rr * inner) * x).astype(BF)


class Units:
    def __init__(self, cfg, n, shared, private):
        self.n = n
        self.high = cfg.S // 16
        self.shared, self.private = shared, private
        self.us, self.up = self.per_chunk(shared), self.per_chunk(private)
        self.u = self.us + self.up

    def per_chunk(self, widths):
        return -(-sum(w // 128 for w in widths) * self.high // self.n)

    def places(self, which):
        widths, per, base = (
            (self.shared, self.us, 0) if which == 0 else (self.private, self.up, self.us)
        )
        at, out = 0, []
        for w in widths:
            spots = []
            for c in range(w // 128):
                for a in range(self.high):
                    spots.append((at // per, base + at % per, a, c))
                    at += 1
            out.append(spots)
        return out

    def spare(self):
        out = []
        for widths, per, base in ((self.shared, self.us, 0), (self.private, self.up, self.us)):
            count = sum(w // 128 for w in widths) * self.high
            out += [(i // per, base + i % per) for i in range(count, per * self.n)]
        return out

    def store(self, out, which, array, values, first=0):
        widths, per, base = (
            (self.shared, self.us, 0) if which == 0 else (self.private, self.up, self.us)
        )
        at = sum(w // 128 for w in widths[:array]) * self.high + first * self.high
        for c in range(values.shape[1] // 128):
            for a in range(self.high):
                unit = at + c * self.high + a
                out[unit // per, base + unit % per] = values[
                    a * 16 : a * 16 + 16, c * 128 : c * 128 + 128
                ]

    def clear_spare(self, out):
        for chunk, off in self.spare():
            out[chunk, off] = jnp.zeros((16, 128), BF)


def pack(units, scr, flip, outs, arrays):
    for i, values in enumerate(arrays):
        which = int(i >= len(units.shared))
        units.store(scr, which, i - which * len(units.shared), values)
    units.clear_spare(scr)
    for j, out in enumerate(outs):
        out[...] = scr[j ^ flip]


def add_halves(keep, got, count):
    total = (keep[...].astype(F32) + got[...].astype(F32)).astype(BF)
    rows = total.shape[0] // count
    return [total[i * rows : (i + 1) * rows] for i in range(count)]


def pack_qkv_kernel(cfg, units, meta, keep_q, got_q, keep, got, ograds, bq, bkv, *outs):
    scr, outs = outs[-1], outs[:-1]
    kw = bkv.shape[1] // 2
    shared = add_halves(keep_q, got_q, 1) + add_halves(keep, got, 2) + [ograds[1]]
    private = [ograds[0], bq[...], bkv[:, :kw], bkv[:, kw:]]
    pack(units, scr, meta[0] % cfg.lo, outs, shared + private)


def split_sum_kernel(cfg, meta, *refs):
    *terms, keep, send = refs
    bit = (meta[0] // cfg.lo) % 2
    for out, half in ((keep, bit), (send, 1 - bit)):
        total = terms[0][half].astype(F32)
        for term in terms[1:]:
            total = total + term[half].astype(F32)
        out[...] = total.astype(BF)


def sum_shared_kernel(meta, mine, got, out, shared):
    total = (mine[...].astype(F32) + got[...].astype(F32)).astype(BF)
    out[...] = total
    shared[...] = total[: shared.shape[0]]


def half_shared_kernel(meta, mine, got, out):
    count = got.shape[0]
    at = pl.ds(meta[1] * (count // 2), count // 2)
    out[: count // 2] = (mine[at].astype(F32) + got[at].astype(F32)).astype(BF)
    out[count // 2 :] = mine[count:]


def unpack(read, spots):
    cols = {}
    for chunk, off, a, c in spots:
        cols.setdefault(c, []).append(read(chunk, off))
    return jnp.concatenate([jnp.concatenate(cols[c], axis=0) for c in sorted(cols)], axis=1)


def expand_kernel(cfg, units, plan, halves, meta, *refs):
    own_in, other_in, outs = refs[: cfg.lo], refs[cfg.lo], refs[cfg.lo + 1 : -2]
    own, shared = refs[-2:]
    flip = meta[0] % cfg.lo
    wa = meta[1]
    count = shared.shape[2]
    for j in range(cfg.lo):
        if halves:
            own[j ^ flip] = own_in[j][...]
            shared[wa, j ^ flip] = own_in[j][:count]
            shared[1 - wa, j ^ flip] = other_in[j]
            continue
        for r in range(2):
            at = 2 * (j ^ flip) + (r ^ ((meta[0] // cfg.lo) % 2))
            own[at] = own_in[j][r]
            shared[wa, at] = own_in[j][r, :count]
            shared[1 - wa, at] = other_in[j, r]
    select = slot_select(cfg, meta)

    def write(out, values, transposed, at):
        full = mm(select, values)
        if transposed:
            out[at : at + full.shape[1], :] = full.T
        else:
            out[:, at : at + full.shape[1]] = full

    for (which, i, transposed), out in zip(plan, outs):
        spots = units.places(which)[i]
        if which == 1:
            shift = 0 if halves else count
            write(out, unpack(lambda chunk, off: own[chunk, off - shift], spots), transposed, 0)
        elif halves:
            for w in range(2):
                values = unpack(lambda chunk, off: shared[w, chunk, off], spots)
                write(out, values, transposed, w * values.shape[1])
        else:
            values = unpack(lambda chunk, off: shared[off // count, chunk, off % count], spots)
            write(out, values, transposed, 0)


def upper_bits(cfg):
    bits, bit = [], cfg.n // 2
    while bit >= cfg.lo:
        bits.append(bit)
        bit //= 2
    return bits


def after(*values):
    return lax.optimization_barrier(values)


def swap_cores(value):
    return lax.ppermute(value, "wa", [(0, 1), (1, 0)])


def permute(cfg, value, bits):
    return lax.ppermute(value, "ctx", [(i, i ^ bits) for i in range(cfg.n)])


def per_device(
    hidden_in, attn_gain, query_weight, key_weight, value_weight, query_gain, key_gain, out_weight,
    ffn_gain, gate_weight, up_weight, down_weight, query_adapt_in, query_adapt_out, key_adapt_in,
    key_adapt_out, value_adapt_in, value_adapt_out, out_adapt_in, out_adapt_out, gate_adapt_in,
    gate_adapt_out, up_adapt_in, up_adapt_out, down_adapt_in, down_adapt_out, document_extra,
    document_adapter, cotangent,
):
    head_dim = query_gain.shape[0]
    cfg = Cfg(
        tokens=hidden_in.shape[0],
        n_ctx=lax.axis_size("ctx"),
        heads_kv=key_weight.shape[1] // head_dim,
        groups=query_weight.shape[1] // key_weight.shape[1],
        head_dim=head_dim,
        docs=document_extra.shape[0],
        adapt_width=query_adapt_in.shape[1],
        width=hidden_in.shape[2],
        hidden=gate_weight.shape[1],
    )
    T, D, G, S, AW, n, lo = cfg.T, cfg.D, cfg.G, cfg.S, cfg.AW, cfg.n, cfg.lo
    gw = cfg.groups * head_dim
    QW, KW = query_weight.shape[1], key_weight.shape[1]
    meta = (document_extra, document_adapter)
    x = hidden_in.reshape(T, D)
    cot = cotangent.reshape(T, D)
    gain_a = attn_gain.reshape(1, D)
    gain_f = ffn_gain.reshape(1, D)
    qg = query_gain.reshape(1, head_dim)
    kg = key_gain.reshape(1, head_dim)

    lane = np.arange(2 * head_dim) % (head_dim // 2)
    inverse = np.exp(lane * (-2.0 * math.log(theta_base) / head_dim)).astype(np.float32)[None, :]

    piece = ((T, gw), BF)
    fetched = [
        x, key_adapt_in, value_adapt_in, key_weight, key_adapt_out, value_weight, value_adapt_out,
    ]
    first = call(
        functools.partial(key_value_kernel, cfg),
        [piece] * G
        + [((T, KW), F32), ((2, T, S), BF), ((T, D), BF)]
        + [((T, 2 * head_dim), F32)] * 2,
        [meta, *fetched, gain_a, kg, inverse],
        scratch=[pltpu.VMEM(value.shape, value.dtype) for value in fetched]
        + [pltpu.SemaphoreType.DMA((len(fetched),)), pltpu.VMEM((G, T, 2 * head_dim), BF)],
        us=4,
        name="key_value",
        in_place=len(fetched),
        large=True,
    )
    kv_send = first[:G]
    kraw, sides, normed, cos, sin = first[G:]

    def to_heads(pieces):
        return [pieces[0]] + [permute(cfg, pieces[k], k * lo) for k in range(1, G)]

    def add(values):
        return sum(value.astype(F32) for value in values).astype(BF)

    def to_plane(value):
        return [value] + [permute(cfg, value, j) for j in range(1, lo)]

    kv_heads = to_heads(kv_send)
    second = call(
        functools.partial(query_kernel, cfg),
        [piece] * G + [((T, QW), F32), ((1, T, S), BF), items_shape(cfg)],
        [meta, normed, cos, sin, query_weight, query_adapt_in, query_adapt_out, qg],
        scratch=[pltpu.VMEM((G, T, gw), BF)],
        us=3,
        name="query",
        lists=1,
    )
    q_send, (qraw, side_q, items) = second[:G], second[G:]
    listed = (*meta, items)
    both = list(after(*kv_heads, *q_send))
    kv_heads, q_send = both[:G], both[G:]
    kv = to_plane(jnp.stack(kv_heads))
    q = to_heads(q_send)
    grad_hidden, gst = call(
        functools.partial(hidden_grad_kernel, cfg),
        [((T, cfg.F), F32), ((S, T), BF)],
        [meta, cot, down_weight, down_adapt_out, down_adapt_in],
        us=3,
        name="hidden_grad",
    )
    grad_hidden, *both = after(grad_hidden, *kv, *q)
    kv, q = both[:lo], both[lo:]
    tiles = lambda dtype, width=gw: pltpu.VMEM((cfg.NT, 2 * cfg.QH, width), dtype)
    attn = call(
        functools.partial(attend_kernel, cfg),
        [piece] * G + [((G, T, gw), BF), ((G, T, gw), F32)],
        [listed] + q + kv,
        scratch=[tiles(BF), tiles(F32)],
        us=12,
        name="attend",
    )
    o_send, o_all, linv = attn[:G], attn[G], attn[G + 1]
    o = to_heads(o_send)
    q_stack, _ = after(jnp.stack(q), o_send[0])
    q_plane = to_plane(q_stack)
    (opart,) = call(
        functools.partial(out_kernel, cfg),
        [((T, D + AW), BF)],
        [meta] + o + [out_weight, out_adapt_in],
        scratch=[pltpu.VMEM((T, QW), BF)],
        us=3,
        name="out_proj",
    )
    units_f = Units(cfg, 2 * lo, [D] * 3, [cfg.F] * 3)
    ffn = ffn_call(
        cfg, units_f, meta, x, opart, swap_cores(opart), out_adapt_out, gain_f, gate_weight, up_weight,
        down_weight, gate_adapt_out, up_adapt_out, gate_adapt_in, up_adapt_in, down_adapt_in,
        cot, grad_hidden, gst,
    )
    mixed, dfn, dpart, oside, *parts_f = ffn
    dfn, *q_plane = after(dfn, *q_plane)
    mg = call(
        functools.partial(mixed_grad_kernel, cfg),
        [((T, D), F32), ((2, S, D // 2), BF)] + [piece] * G,
        [meta, mixed, dfn, swap_cores(dfn), cot, gain_f]
        + o
        + [out_weight, out_adapt_in, out_adapt_out, oside],
        scratch=[pltpu.VMEM((T, QW), BF), pltpu.VMEM((G, T, gw), BF), pltpu.VMEM((T, D), BF)],
        us=0.01,
        name="mixed_grad",
    )
    grad_mixed, ograds, go_send = mg[0], mg[1], mg[2:]
    go_heads = to_heads(go_send)
    parts_f = [parts_f[0]] + [permute(cfg, parts_f[j], j) for j in range(1, lo)]
    message = G * T + -(-2 * cfg.groups * cfg.NT // 16) * 16
    (go_all,) = call(
        functools.partial(scale_kernel, cfg),
        [((message, gw), BF)],
        [meta] + go_heads + [linv, o_all],
        scratch=[
            pltpu.VMEM((cfg.NT, cfg.QH, gw), F32),
            pltpu.VMEM((cfg.groups * cfg.NT, gw), F32),
        ],
        us=0.01,
        name="scale",
    )
    go_all, *parts_f = after(go_all, *parts_f)
    sum_f, send_f = call(
        functools.partial(split_sum_kernel, cfg),
        [((units_f.u, 16, 128), BF)] * 2,
        [meta, *parts_f],
        us=0.01,
        name="split_sum",
    )
    go_plane = to_plane(go_all)
    dq_send = call(
        functools.partial(grad_query_kernel, cfg),
        [piece] * G,
        [listed] + q + kv + [go_all, o_all],
        scratch=[tiles(BF), tiles(BF), tiles(F32, 1), tiles(F32)],
        us=13.5,
        name="grad_query",
    )
    near, far = upper_bits(cfg)[1], upper_bits(cfg)[0]
    got_f, *dq_send = after(permute(cfg, send_f, near), *dq_send)
    sum_f = add([sum_f, got_f])
    dq = to_heads(dq_send)
    dkv_send = call(
        functools.partial(grad_key_kernel, cfg),
        [piece] * G,
        [listed, kv[0]] + q_plane + go_plane,
        scratch=[tiles(BF), tiles(BF), pltpu.VMEM((cfg.NT, 16, cfg.KT), F32), tiles(F32)]
        + [tiles(F32)],
        us=16,
        name="grad_key",
    )
    both = list(after(*dq, *dkv_send))
    dq, dkv_send = both[:G], both[G:]
    dkv = to_heads(dkv_send)
    qpart, bgrad_q, akeep_q, asend_q = call(
        functools.partial(query_back_kernel, cfg),
        [((T, D), F32), ((S, QW), BF), ((S, D // 2), BF), ((S, D // 2), BF)],
        [meta]
        + dq
        + [
            normed, qraw, side_q, cos, sin, qg, query_weight, query_adapt_in, query_adapt_out,
        ],
        scratch=[pltpu.VMEM((T, QW), BF), pltpu.VMEM((S, D), F32)],
        us=0.01,
        name="query_back",
    )
    got_f, qpart = after(permute(cfg, sum_f, far), qpart)
    sum_f, shared_f = call(
        sum_shared_kernel,
        [((units_f.u, 16, 128), BF), ((units_f.us, 16, 128), BF)],
        [meta, sum_f, got_f],
        us=0.01,
        name="sum_shared",
    )
    shared_f, qpart, *dkv = after(shared_f, qpart, *dkv)
    kv_grads, kv_sides, akeep_kv, asend_kv = call(
        functools.partial(key_value_side_kernel, cfg),
        [((2, T, KW), BF), ((2, T, AW), BF), ((2 * S, D // 2), BF), ((2 * S, D // 2), BF)],
        [meta] + dkv + [normed, kraw, cos, sin, kg, key_adapt_out, value_adapt_out],
        scratch=[pltpu.VMEM((T, 2 * KW), BF), pltpu.VMEM((2 * S, D), F32)],
        us=0.01,
        name="key_value_side",
    )
    dnormed, bgrad_kv = call(
        functools.partial(key_value_back_kernel, cfg),
        [((T, D), BF), ((S, 2 * KW), BF)],
        [meta, kv_grads, kv_sides, sides, key_weight, value_weight, key_adapt_in, value_adapt_in]
        + [qpart],
        us=0.01,
        name="key_value_back",
    )

    def expand(units, chunks, plan, halves, outs, name):
        shared = units.us if halves else units.us // 2
        theirs = swap_cores(jnp.stack([chunk[..., :shared, :, :] for chunk in chunks]))
        per = chunks[0].shape[-3]
        return call(
            functools.partial(expand_kernel, cfg, units, plan, halves),
            outs,
            [meta, *chunks, theirs],
            scratch=[
                pltpu.VMEM((units.n, per, 16, 128), BF),
                pltpu.VMEM((2, units.n, shared, 16, 128), BF),
            ],
            us=4,
            name=name,
        )

    units_q = Units(cfg, lo, [D // 2] * 4, [QW, QW, KW, KW])
    parts_q = call(
        functools.partial(pack_qkv_kernel, cfg, units_q),
        [((units_q.u, 16, 128), BF)] * lo,
        [meta, akeep_q, swap_cores(asend_q), akeep_kv, swap_cores(asend_kv), ograds, bgrad_q]
        + [bgrad_kv],
        scratch=[pltpu.VMEM((lo, units_q.u, 16, 128), BF)],
        us=0.01,
        name="pack_qkv",
    )
    (sum_f,) = call(
        half_shared_kernel,
        [((units_f.u - units_f.us // 2, 16, 128), BF)],
        [meta, sum_f, swap_cores(shared_f)],
        us=0.01,
        name="half_shared",
    )
    sum_f, dnormed, *parts_q = after(sum_f, dnormed, *parts_q)
    dn_other = swap_cores(dnormed)
    near_f = permute(cfg, sum_f, near)
    sum_q = add([parts_q[0]] + [permute(cfg, parts_q[j], j) for j in range(1, lo)])
    sum_q, dn_other, sum_f, near_f = after(sum_q, dn_other, sum_f, near_f)
    all_f = to_plane(jnp.stack([sum_f, near_f]))
    (input_rows,) = call(
        functools.partial(input_grad_kernel, cfg),
        [((T, D), BF)],
        [meta, x, gain_a, grad_mixed, dnormed, dn_other],
        us=0.01,
        name="input_grad",
    )
    got_q, input_rows = after(permute(cfg, sum_q, near), input_rows)
    sum_q = add([sum_q, got_q])
    got_q, *all_f = after(permute(cfg, sum_q, far), *all_f)
    sum_q, dpart = after(add([sum_q, got_q]), dpart)
    pieces_q = to_plane(sum_q)
    (out_rows,) = call(
        functools.partial(output_kernel, cfg),
        [((T, D), BF)],
        [meta, mixed, dpart, swap_cores(dpart), down_adapt_out],
        us=0.01,
        name="output",
    )
    gate_in, up_in, down_out, gate_out, up_out, down_in = expand(
        units_f,
        all_f,
        [(0, 0, True), (0, 1, True), (0, 2, False), (1, 0, False), (1, 1, False), (1, 2, True)],
        False,
        [((D, AW), F32), ((D, AW), F32), ((AW, D), F32)]
        + [((AW, cfg.F), F32), ((AW, cfg.F), F32), ((cfg.F, AW), F32)],
        "expand_ffn",
    )
    down_out, out_rows, *pieces_q = after(down_out, out_rows, *pieces_q)
    query_in, key_in, value_in, out_out, out_in, query_out, key_out, value_out = expand(
        units_q,
        pieces_q,
        [(0, 0, True), (0, 1, True), (0, 2, True), (0, 3, False)]
        + [(1, 0, True), (1, 1, False), (1, 2, False), (1, 3, False)],
        True,
        [((D, AW), F32)] * 3
        + [((AW, D), F32), ((QW, AW), F32), ((AW, QW), F32), ((AW, KW), F32), ((AW, KW), F32)],
        "expand_qkv",
    )
    return (
        out_rows.reshape(T, 1, D),
        input_rows.reshape(T, 1, D),
        query_in,
        query_out,
        key_in,
        key_out,
        value_in,
        value_out,
        out_in,
        out_out,
        gate_in,
        gate_out,
        up_in,
        up_out,
        down_in,
        down_out,
    )


def solution(mesh):
    return jax.shard_map(
        per_device,
        mesh=mesh,
        in_specs=(
            P(None, "ctx", None), P(), P(None, "wa"), P(None, "wa"), P(None, "wa"), P(), P(),
            P("wa", None), P(), P(None, "wa"), P(None, "wa"), P("wa", None), P(), P(None, "wa"),
            P(), P(None, "wa"), P(), P(None, "wa"), P("wa", None), P(), P(), P(None, "wa"), P(),
            P(None, "wa"), P("wa", None), P(), P(), P(), P(None, "ctx", None),
        ),
        out_specs=(
            P(None, "ctx", None), P(None, "ctx", None), P(), P(None, "wa"), P(), P(None, "wa"), P(),
            P(None, "wa"), P("wa", None), P(), P(), P(None, "wa"), P(), P(None, "wa"),
            P("wa", None), P(),
        ),
        check_vma=False,
    )
```

```python
import functools
import math

import jax
import jax.numpy as jnp
import numpy as np
from jax import lax
from jax.experimental import pallas as pl
from jax.experimental.pallas import tpu as pltpu
from jax.sharding import PartitionSpec as P

RANK = 16
DOC_MIN = 200

norm_eps = 1e-05
theta_base = 1000000.0
BF = jnp.bfloat16
F32 = jnp.float32
LOG2E = 1.4426950408889634
STEP, STEP_QUERY = 11, 11
FFN_TILE, FFN_STEP = 256, 3
VMEM_SMALL = 28 * 1024 * 1024
VMEM_LARGE = 56 * 1024 * 1024


def mm(left, right):
    return jnp.dot(left, right, preferred_element_type=F32)


def mm_nt(left, right):
    return lax.dot_general(left, right, (((1,), (1,)), ((), ())), preferred_element_type=F32)


def mm_tn(left, right):
    return lax.dot_general(left, right, (((0,), (0,)), ((), ())), preferred_element_type=F32)


def iota(shape, dim):
    return lax.broadcasted_iota(jnp.int32, shape, dim)


class Cfg:
    def __init__(self, tokens, n_ctx, heads_kv, groups, head_dim, docs, adapt_width, width, hidden):
        self.T = tokens
        self.n = n_ctx
        self.G = heads_kv
        self.lo = n_ctx // heads_kv
        self.groups = groups
        self.hd = head_dim
        self.docs = docs
        self.AW = adapt_width
        self.slots = min(docs, adapt_width // RANK)
        self.S = self.slots * RANK
        self.D = width
        self.F = hidden
        self.R = max(16, min(tokens, 512 // n_ctx))
        self.NT = tokens // self.R
        self.span = self.R * n_ctx
        self.QH = self.G * self.R
        self.KT = n_ctx * self.R


class Meta:
    def __init__(self, extra, adapter, items=None):
        self.refs, self.docs, self.items = (extra, adapter), extra.shape[0], items

    def __getitem__(self, i):
        if i < 2:
            return lax.axis_index(("ctx", "wa")[i])
        return self.refs[(i - 2) // self.docs][(i - 2) % self.docs]


def with_meta(kernel, count):
    return lambda *refs: kernel(Meta(*refs[:count]), *refs[count:])


def doc_starts(cfg, meta):
    out = [jnp.int32(0)]
    for j in range(cfg.docs):
        out.append(out[-1] + meta[2 + j] + (DOC_MIN - 1))
    return out


def start_of(starts, token):
    out = jnp.zeros_like(token)
    for s in starts[1:-1]:
        out = jnp.where(token >= s, s, out)
    return out


def end_of(starts, token):
    out = starts[1]
    for j in range(1, len(starts) - 1):
        out = jnp.where(token >= starts[j], starts[j + 1], out)
    return out


def adapter_mask(cfg, meta):
    token = iota((cfg.T, cfg.AW), 0) * cfg.n + meta[0]
    starts = doc_starts(cfg, meta)
    adapter = jnp.full((cfg.T, cfg.AW), meta[2 + cfg.docs], jnp.int32)
    for j in range(1, cfg.docs):
        adapter = jnp.where(token >= starts[j], meta[2 + cfg.docs + j], adapter)
    return (adapter == iota((cfg.T, cfg.AW), 1) // RANK).astype(F32)


def slot_select(cfg, meta):
    row = iota((cfg.AW, cfg.S), 0)
    col = iota((cfg.AW, cfg.S), 1)
    if cfg.S == cfg.AW:
        return (row == col).astype(BF)
    target = jnp.full((cfg.AW, cfg.S), -1, jnp.int32)
    for s in range(cfg.slots):
        mine = meta[2 + cfg.docs + s]
        again = jnp.int32(0)
        for e in range(s):
            again = jnp.where(meta[2 + cfg.docs + e] == mine, 1, again)
        base = jnp.where(again == 1, -4 * cfg.AW, mine * RANK)
        target = jnp.where(col // RANK == s, base + col % RANK, target)
    return (row == target).astype(BF)


def block_mean(values, hd):
    part = min(values.shape[1], 256)
    ones = (iota((part, part), 0) // hd == iota((part, part), 1) // hd).astype(BF)
    out = []
    for at in range(0, values.shape[1], part):
        piece = values[:, at : at + part]
        high = piece.astype(BF)
        low = (piece - high.astype(F32)).astype(BF)
        out.append((mm(high, ones) + mm(low, ones)) * (1.0 / hd))
    return jnp.concatenate(out, axis=1)


def swap_halves(values, hd):
    width = values.shape[1]
    half = hd // 2
    first = iota(values.shape, 1) % hd < half
    return jnp.where(first, pltpu.roll(values, width - half, 1), pltpu.roll(values, half, 1))


def lanes(values, copies):
    return jnp.concatenate([values] * copies, axis=1) if copies > 1 else values


def params(large=False, **kw):
    limit = VMEM_SMALL if lax.axis_size("ctx") <= 16 and not large else VMEM_LARGE
    return pltpu.CompilerParams(vmem_limit_bytes=limit, **kw)


SMEM = pl.BlockSpec(memory_space=pltpu.SMEM)


def cost(us):
    return pl.CostEstimate(flops=int(us * 1.15e9), bytes_accessed=0, transcendentals=0)


def call(kernel, outs, ins, scratch=(), us=1.0, name=None, large=False, in_place=0, lists=0):
    count = len(ins[0])
    ins = [*ins[0], *ins[1:]]
    return pl.pallas_call(
        with_meta(kernel, count),
        out_shape=[jax.ShapeDtypeStruct(s, d) for s, d in outs],
        in_specs=[SMEM] * count
        + [pl.BlockSpec(memory_space=pl.ANY)] * in_place
        + [pl.BlockSpec(memory_space=pltpu.VMEM)] * (len(ins) - count - in_place),
        out_specs=[pl.BlockSpec(memory_space=pltpu.VMEM)] * (len(outs) - lists) + [SMEM] * lists,
        scratch_shapes=list(scratch),
        compiler_params=params(large),
        cost_estimate=cost(us),
        name=name,
    )(*ins)


def head_prep(cfg, cos, sin, raw, g):
    hd = cfg.hd
    copies = raw.shape[1] // hd
    scaled = raw * lax.rsqrt(block_mean(raw * raw, hd) + norm_eps) * lanes(g[...], copies)
    per = raw.shape[1] // cos.shape[1]
    return scaled * lanes(cos[...], per) + swap_halves(scaled, hd) * lanes(sin[...], per)


def rotation(cfg, meta, inverse, cos, sin):
    width, half = 2 * cfg.hd, cfg.hd // 2
    blocks = width // half
    rows = cfg.T // blocks
    lane = iota((rows, width), 1)
    token = ((lane // half) * rows + iota((rows, width), 0)) * cfg.n + meta[0]
    angle = (token - start_of(doc_starts(cfg, meta), token)).astype(F32) * inverse[...]
    sign = jnp.where(lane % cfg.hd < half, -1.0, 1.0)
    for out, values, scale in ((cos, jnp.cos(angle), None), (sin, jnp.sin(angle), sign)):
        for b in range(blocks):
            part = pltpu.roll(values, width - b * half, 1) if b else values
            part = jnp.where(lane < half, part, 0.0)
            size = half
            while size < width:
                part = part + pltpu.roll(part, size, 1)
                size *= 2
            out[b * rows : (b + 1) * rows, :] = part if scale is None else part * scale


def key_value_kernel(cfg, meta, *refs):
    G, hd = cfg.G, cfg.hd
    sources, (gain, kg, inverse), refs = refs[:7], refs[7:10], refs[10:]
    kv_out, refs = refs[:G], refs[G:]
    raw_ref, sides_ref, normed_ref, cos, sin, *scratch = refs
    buffers, sems, kv_scr = scratch[:7], scratch[7], scratch[8]
    copies = [
        pltpu.make_async_copy(source, buffer, sems.at[i])
        for i, (source, buffer) in enumerate(zip(sources, buffers))
    ]
    for copy in copies:
        copy.start()
    x_buf, ak, av, wk, bk, wv, bv = buffers
    rotation(cfg, meta, inverse, cos, sin)
    mask = adapter_mask(cfg, meta)
    select = slot_select(cfg, meta)
    copies[0].wait()
    x = x_buf[...].astype(F32)
    rr = lax.rsqrt(jnp.mean(x * x, axis=-1, keepdims=True) + norm_eps)
    normed = (x * rr * gain[...]).astype(BF)
    normed_ref[...] = normed
    for copy in copies[1:]:
        copy.wait()
    raws = []
    for i, (w, a, b) in enumerate(((wk, ak, bk), (wv, av, bv))):
        side = (mask * mm(normed, a[...])).astype(BF)
        sides_ref[i] = mm(side, select).astype(BF)
        raws.append(mm(normed, w[...]) + mm(side, b[...]))
    kraw, vraw = raws
    raw_ref[...] = kraw
    key = head_prep(cfg, cos, sin, kraw, kg).astype(BF)
    value = vraw.astype(BF)
    for h in range(G):
        at = slice(h * hd, (h + 1) * hd)
        kv_scr[h] = jnp.concatenate([key[:, at], value[:, at]], axis=1)
    hi = meta[0] // cfg.lo
    for k in range(G):
        kv_out[k][...] = kv_scr[hi ^ k]


def query_kernel(cfg, meta, normed_ref, cos, sin, w, a, b, g, *refs):
    G = cfg.G
    q_out, raw_ref, side_ref, items, q_scr = refs[:G], *refs[G:]
    list_items(cfg, doc_starts(cfg, meta), items)
    normed = normed_ref[...]
    side = (adapter_mask(cfg, meta) * mm(normed, a[...])).astype(BF)
    side_ref[0] = mm(side, slot_select(cfg, meta)).astype(BF)
    raw = mm(normed, w[...]) + mm(side, b[...])
    raw_ref[...] = raw
    query = head_prep(cfg, cos, sin, raw, g).astype(BF)
    gw = cfg.groups * cfg.hd
    for h in range(G):
        q_scr[h] = query[:, h * gw : (h + 1) * gw]
    hi = meta[0] // cfg.lo
    for k in range(G):
        q_out[k][...] = q_scr[hi ^ k]


def tile_of(cfg, pieces, t):
    rows = pl.ds(pl.multiple_of(t * cfg.R, cfg.R), cfg.R)
    return jnp.concatenate([piece[rows, :] for piece in pieces], axis=0)


def list_items(cfg, starts, items):
    def per_query(qt, count):
        def one(s, at):
            items[0, at] = qt
            items[1, at] = s
            return at + 1

        return lax.fori_loop(start_of(starts, qt * cfg.span) // cfg.span, qt + 1, one, count)

    count = lax.fori_loop(0, cfg.NT, per_query, 0)
    for i in range(STEP - 1):
        items[0, count + i] = 0
        items[1, count + i] = cfg.NT - 1
    items[0, items.shape[1] - 1] = count


def steps_of(items, step):
    return (items[0, items.shape[1] - 1] + step - 1) // step


def items_shape(cfg):
    return ((2, cfg.NT * (cfg.NT + 1) // 2 + STEP), jnp.int32)


def split_pieces(ref, count):
    return [ref.at[i] for i in range(count)]


def message_pieces(cfg, ref):
    return [ref.at[pl.ds(k * cfg.T, cfg.T)] for k in range(cfg.G)]


def token_in_span(cfg, meta, index):
    hi, lo = meta[0] // cfg.lo, meta[0] % cfg.lo
    piece, row = index // cfg.R, index % cfg.R
    j, k = piece // cfg.G, piece % cfg.G
    return row * cfg.n + (hi ^ k) * cfg.lo + (lo ^ j)


def pad_queries(cfg, qq, side):
    hd = cfg.hd
    wide = qq.astype(F32)
    first = iota(wide.shape, 1) < hd
    rolled = pltpu.roll(wide, hd, 1)
    if side == 0:
        parts = [jnp.where(first, wide, 0.0), jnp.where(first, rolled, 0.0)]
    else:
        parts = [jnp.where(first, 0.0, rolled), jnp.where(first, 0.0, wide)]
    return jnp.concatenate(parts, axis=0).astype(BF)


def attend_kernel(cfg, meta, *refs):
    G, R, hd, QH = cfg.G, cfg.R, cfg.hd, cfg.QH
    q_in, own, others = refs[:G], refs[G], refs[G + 1 : G + cfg.lo]
    rest = refs[G + cfg.lo :]
    o_out, o_all, linv, q_scr, acc_scr = rest[:G], *rest[G:]
    kv_pieces = split_pieces(own, G)
    for ref in others:
        kv_pieces = kv_pieces + split_pieces(ref, G)
    starts = doc_starts(cfg, meta)
    items = meta.items
    scale = hd ** (-0.5) * LOG2E
    key_off = token_in_span(cfg, meta, iota((1, cfg.KT), 1))
    row_off = token_in_span(cfg, meta, iota((2 * QH, 1), 0) % QH)
    key_lanes = iota((cfg.KT, 2 * hd), 1) < hd
    for t in range(cfg.NT):
        q_scr[t] = pad_queries(cfg, tile_of(cfg, q_in, t), 0)
        acc_scr[t] = jnp.zeros((2 * QH, 2 * hd), F32)

    def step(i, carry):
        parts = []
        for u in range(STEP):
            qt, s = items[0, i * STEP + u], items[1, i * STEP + u]
            kv = tile_of(cfg, kv_pieces, s)
            token = row_off + qt * cfg.span
            key_token = key_off + s * cfg.span
            e = jnp.exp2(mm_nt(q_scr[qt], kv) * scale)
            e = jnp.where((key_token <= token) & (key_token >= start_of(starts, token)), e, 0.0)
            parts.append((qt, mm(e.astype(BF), jnp.where(key_lanes, jnp.ones_like(kv), kv))))
        for qt, part in parts:
            acc_scr[qt] += part
        return carry

    lax.fori_loop(0, steps_of(items, STEP), step, 0)
    half = iota((QH, 2 * hd), 1) < hd
    for t in range(cfg.NT):
        acc = acc_scr[t]
        inv0 = 1.0 / acc[:QH]
        inv1 = 1.0 / acc[QH:]
        out0 = pltpu.roll(acc[:QH], hd, 1) * inv0
        out1 = acc[QH:] * pltpu.roll(inv1, hd, 1)
        out = jnp.where(half, out0, out1).astype(BF)
        inv = jnp.where(half, inv0, pltpu.roll(inv1, hd, 1))
        rows = slice(t * R, (t + 1) * R)
        for k in range(G):
            o_out[k][rows, :] = out[k * R : (k + 1) * R]
            o_all[k, rows, :] = out[k * R : (k + 1) * R]
            linv[k, rows, :] = inv[k * R : (k + 1) * R]


def head_sums(cfg, prod):
    pick = (iota((16, prod.shape[1]), 1) // cfg.hd == iota((16, prod.shape[1]), 0)).astype(BF)
    high = prod.astype(BF)
    low = (prod - high.astype(F32)).astype(BF)
    return mm_nt(pick, high) + mm_nt(pick, low)


def scale_kernel(cfg, meta, *refs):
    G, T, R, NT, QH = cfg.G, cfg.T, cfg.R, cfg.NT, cfg.QH
    go, linv, o_all, out, scr, delta = refs[:G], refs[G], refs[G + 1], refs[G + 2], *refs[G + 3 :]
    delta[...] = jnp.zeros_like(delta)
    for k in range(G):
        scaled = (go[k][...].astype(F32) * linv[k]).astype(BF)
        out[k * T : (k + 1) * T, :] = scaled
        prod = scaled.astype(F32) * o_all[k].astype(F32)
        for t in range(NT):
            scr[t, k * R : (k + 1) * R, :] = prod[t * R : (t + 1) * R]
    for t in range(NT):
        sums = head_sums(cfg, scr[t])
        for h in range(cfg.groups):
            delta[h * NT + t : h * NT + t + 1, :QH] = sums[h : h + 1]
    high = delta[...].astype(BF)
    at = G * T
    rows = cfg.groups * NT
    out[at : at + rows, :] = high
    out[at + rows : at + 2 * rows, :] = (delta[...] - high.astype(F32)).astype(BF)


def grad_query_kernel(cfg, meta, *refs):
    G, R, hd, QH = cfg.G, cfg.R, cfg.hd, cfg.QH
    q_in, own, others = refs[:G], refs[G], refs[G + 1 : G + cfg.lo]
    go_ref, o_ref = refs[G + cfg.lo : G + cfg.lo + 2]
    rest = refs[G + cfg.lo + 2 :]
    dq_out, q_scr, go_scr, delta_scr, acc_scr = rest[:G], *rest[G:]
    kv_pieces = split_pieces(own, G)
    for ref in others:
        kv_pieces = kv_pieces + split_pieces(ref, G)
    starts = doc_starts(cfg, meta)
    items = meta.items
    scale = hd ** (-0.5) * LOG2E
    key_off = token_in_span(cfg, meta, iota((1, cfg.KT), 1))
    row_off = token_in_span(cfg, meta, iota((2 * QH, 1), 0) % QH)
    half = iota((QH, 2 * hd), 1) < hd
    for t in range(cfg.NT):
        go = tile_of(cfg, message_pieces(cfg, go_ref), t)
        prod = go.astype(F32) * tile_of(cfg, split_pieces(o_ref, G), t).astype(F32)
        q_scr[t] = pad_queries(cfg, tile_of(cfg, q_in, t), 0)
        go_scr[t] = pad_queries(cfg, go, 1)
        delta_scr[t, :QH] = jnp.sum(jnp.where(half, prod, 0.0), axis=1, keepdims=True)
        delta_scr[t, QH:] = jnp.sum(jnp.where(half, 0.0, prod), axis=1, keepdims=True)
        acc_scr[t] = jnp.zeros((2 * QH, 2 * hd), F32)

    def step(i, carry):
        parts = []
        for u in range(STEP_QUERY):
            qt, s = items[0, i * STEP_QUERY + u], items[1, i * STEP_QUERY + u]
            kv = tile_of(cfg, kv_pieces, s)
            token = row_off + qt * cfg.span
            key_token = key_off + s * cfg.span
            e = jnp.exp2(mm_nt(q_scr[qt], kv) * scale)
            ds = e * (mm_nt(go_scr[qt], kv) - delta_scr[qt])
            ds = jnp.where((key_token <= token) & (key_token >= start_of(starts, token)), ds, 0.0)
            parts.append((qt, mm(ds.astype(BF), kv)))
        for qt, part in parts:
            acc_scr[qt] += part
        return carry

    lax.fori_loop(0, steps_of(items, STEP_QUERY), step, 0)
    for t in range(cfg.NT):
        acc = acc_scr[t]
        out = jnp.where(half, acc[:QH], pltpu.roll(acc[QH:], hd, 1)) * hd ** (-0.5)
        out = out.astype(BF)
        for k in range(G):
            dq_out[k][t * R : (t + 1) * R, :] = out[k * R : (k + 1) * R]


def grad_key_kernel(cfg, meta, *refs):
    G, T, R, hd, lo, QH, NT = cfg.G, cfg.T, cfg.R, cfg.hd, cfg.lo, cfg.QH, cfg.NT
    own = refs[0]
    q_refs, go_refs = (refs[1 + i * lo : 1 + (i + 1) * lo] for i in range(2))
    rest = refs[1 + 2 * lo :]
    dkv_out, key_scr, value_scr, delta_scr, gk_scr, gv_scr = rest[:G], *rest[G:]
    q_pieces = [piece for ref in q_refs for piece in split_pieces(ref, G)]
    go_pieces = [piece for ref in go_refs for piece in message_pieces(cfg, ref)]
    starts = doc_starts(cfg, meta)
    items = meta.items
    scale = hd ** (-0.5) * LOG2E
    rows = cfg.groups * NT
    for j in range(lo):
        sums = go_refs[j][G * T : G * T + 2 * rows, :].astype(F32)
        sums = sums[:rows] + sums[rows:]
        for t in range(NT):
            for h in range(cfg.groups):
                at = h * NT + t
                delta_scr[t, h : h + 1, j * QH : (j + 1) * QH] = sums[at : at + 1, :QH]
    query_off = token_in_span(cfg, meta, iota((1, cfg.KT), 1))
    row_off = token_in_span(cfg, meta, iota((2 * QH, 1), 0) % QH)
    first = iota((QH, 2 * hd), 1) < hd
    for t in range(NT):
        kv = tile_of(cfg, split_pieces(own, G), t).astype(F32)
        rolled = pltpu.roll(kv, hd, 1)
        keys = [jnp.where(first, kv, 0.0), jnp.where(first, 0.0, rolled)]
        values = [jnp.where(first, rolled, 0.0), jnp.where(first, 0.0, kv)]
        key_scr[t] = jnp.concatenate(keys, axis=0).astype(BF)
        value_scr[t] = jnp.concatenate(values, axis=0).astype(BF)
        gk_scr[t] = jnp.zeros((2 * QH, 2 * hd), F32)
        gv_scr[t] = jnp.zeros((2 * QH, 2 * hd), F32)

    def step(i, carry):
        parts = []
        for u in range(STEP):
            t, kt = items[0, i * STEP + u], items[1, i * STEP + u]
            queries, grads = tile_of(cfg, q_pieces, t), tile_of(cfg, go_pieces, t)
            key_token = row_off + kt * cfg.span
            token = query_off + t * cfg.span
            e = jnp.exp2(mm_nt(key_scr[kt], queries) * scale)
            e = jnp.where((key_token <= token) & (key_token >= start_of(starts, token)), e, 0.0)
            dp = mm_nt(value_scr[kt], grads)
            delta = delta_scr[t]
            ds = [
                (e[:QH] * (dp[:QH] - delta[0:1])).astype(BF),
                (e[QH:] * (dp[QH:] - delta[1:2])).astype(BF),
            ]
            ds = jnp.concatenate(ds, axis=0)
            parts.append((kt, mm(ds, queries), mm(e.astype(BF), grads)))
        for kt, gk, gv in parts:
            gk_scr[kt] += gk
            gv_scr[kt] += gv
        return carry

    lax.fori_loop(0, steps_of(items, STEP), step, 0)
    for t in range(NT):
        gk, gv = gk_scr[t], gv_scr[t]
        gk = (gk[:QH] + pltpu.roll(gk[QH:], hd, 1)) * hd ** (-0.5)
        gv = pltpu.roll(gv[:QH], hd, 1) + gv[QH:]
        out = jnp.where(first, gk, gv).astype(BF)
        for k in range(G):
            dkv_out[k][t * R : (t + 1) * R, :] = out[k * R : (k + 1) * R]


def place_pieces(cfg, hi, scr, pieces):
    w = pieces[0].shape[1]
    for k in range(cfg.G):
        at = pl.multiple_of((hi ^ k) * w, w)
        scr[:, pl.ds(at, w)] = pieces[k][...]


def out_kernel(cfg, meta, *refs):
    G = cfg.G
    wo, ao, part, attn = refs[G:]
    place_pieces(cfg, meta[0] // cfg.lo, attn, refs[:G])
    rows = attn[...]
    part[:, : cfg.D] = mm(rows, wo[...]).astype(BF)
    part[:, cfg.D :] = mm(rows, ao[...]).astype(BF)


def tiles_of(i, count):
    return [
        pl.ds(pl.multiple_of(i * (count * FFN_TILE) + j * FFN_TILE, FFN_TILE), FFN_TILE)
        for j in range(count)
    ]


def hidden_grad_kernel(cfg, meta, cot_ref, wd, bd, ad, out, turned):
    cot = cot_ref[...]
    side = (adapter_mask(cfg, meta) * mm_nt(cot, bd[...])).astype(BF)
    turned[...] = mm(side, slot_select(cfg, meta)).T.astype(BF)

    def part(i, carry):
        for at in tiles_of(i, FFN_STEP):
            out[:, at] = mm_nt(cot, wd[at, :]) + mm_nt(side, ad[at, :])
        return carry

    lax.fori_loop(0, cfg.F // (FFN_STEP * FFN_TILE), part, 0)


def ffn_kernel(
    cfg, units, meta, x_ref, own, other, bo, gain, wg, wu, wd, bg, bu, ag, au, ad, cot_ref, gh, gst,
    mixed_ref, dfn_ref, part_ref, oside, *refs,
):
    D, F = cfg.D, cfg.F
    chunks, (hidden_scr, gg_scr, gu_scr, grads) = refs[: cfg.lo], refs[cfg.lo :]
    flip = meta[0] % cfg.lo
    mask = adapter_mask(cfg, meta)
    select = slot_select(cfg, meta)
    compact = lambda side: mm(side, select).T.astype(BF)
    total = own[...].astype(F32) + other[...].astype(F32)
    out_side = (mask * total[:, D:]).astype(BF)
    oside[...] = mm(out_side, select).astype(BF)
    mixed = x_ref[...].astype(F32) + total[:, :D] + mm(out_side, bo[...])
    mixed_ref[...] = mixed
    rr = lax.rsqrt(jnp.mean(mixed * mixed, axis=-1, keepdims=True) + norm_eps)
    normed = (mixed * rr * gain[...]).astype(BF)
    side_g = (mask * mm(normed, ag[...])).astype(BF)
    side_u = (mask * mm(normed, au[...])).astype(BF)
    turned = compact(side_g), compact(side_u), gst[...]

    def part(i, carry):
        for at in tiles_of(i, FFN_STEP):
            grad_hidden = gh[:, at]
            gate = mm(normed, wg[:, at]) + mm(side_g, bg[:, at])
            upper = mm(normed, wu[:, at]) + mm(side_u, bu[:, at])
            sigma = 1.0 / (1.0 + jnp.exp(-gate))
            silu = gate * sigma
            hidden_scr[:, at] = (silu * upper).astype(BF)
            gg_scr[:, at] = (grad_hidden * upper * (sigma + silu * (1.0 - sigma))).astype(BF)
            gu_scr[:, at] = (grad_hidden * silu).astype(BF)
        return carry

    lax.fori_loop(0, F // (FFN_STEP * FFN_TILE), part, 0)
    tile = FFN_TILE
    side_g = (mask * mm_nt(gg_scr[...], bg[...])).astype(BF)
    side_u = (mask * mm_nt(gu_scr[...], bu[...])).astype(BF)
    side_sum = mm(hidden_scr[...], ad[...])
    for d in range(0, D, tile):
        at = slice(d, d + tile)
        dfn = mm_nt(gg_scr[...], wg[at, :]) + mm_nt(gu_scr[...], wu[at, :])
        dfn_ref[:, at] = (dfn + mm_nt(side_g, ag[at, :]) + mm_nt(side_u, au[at, :])).astype(BF)
    for d in range(0, D, tile):
        at = slice(d, d + tile)
        part_ref[:, at] = mm(hidden_scr[...], wd[:, at]).astype(BF)
    part_ref[:, D:] = side_sum.astype(BF)
    side_d = (mask * side_sum).astype(BF)
    for i, (side, right) in enumerate(((side_g, normed), (side_u, normed), (side_d, cot_ref[...]))):
        units.store(grads, 0, i, mm(compact(side), right).astype(BF))
    for i, right in enumerate((gg_scr, gu_scr, hidden_scr)):
        units.store(grads, 1, i, mm(turned[i], right[...]).astype(BF))
    units.clear_spare(grads)
    for j, chunk in enumerate(chunks):
        for half in range(2):
            chunk[half] = grads[2 * (j ^ flip) + half]


def ffn_call(cfg, units, meta, *ins):
    T, D, F, AW, S = cfg.T, cfg.D, cfg.F, cfg.AW, cfg.S
    return call(
        functools.partial(ffn_kernel, cfg, units),
        [((T, D), F32), ((T, D), BF), ((T, D + AW), BF), ((T, S), BF)]
        + [((2, units.u, 16, 128), BF)] * cfg.lo,
        [meta, *ins],
        scratch=[pltpu.VMEM((T, F), BF)] * 3 + [pltpu.VMEM((units.n, units.u, 16, 128), BF)],
        us=14,
        name="ffn",
    )


def mixed_grad_kernel(cfg, meta, *refs):
    G, D = cfg.G, cfg.D
    mixed_ref, own, other, cot, gain = refs[:5]
    o_in = refs[5 : 5 + G]
    wo, ao, bo, oside = refs[5 + G : 9 + G]
    rest = refs[9 + G :]
    gm_ref, ograds, go_out, attn, go_scr, gm_scr = rest[0], rest[1], rest[2 : 2 + G], *rest[2 + G :]
    hi = meta[0] // cfg.lo
    mixed = mixed_ref[...]
    w = (own[...].astype(F32) + other[...].astype(F32)) * gain[...]
    rr = lax.rsqrt(jnp.mean(mixed * mixed, axis=-1, keepdims=True) + norm_eps)
    inner = jnp.mean(w * mixed, axis=-1, keepdims=True)
    gm = cot[...].astype(F32) + rr * w - (rr * rr * rr * inner) * mixed
    gm_ref[...] = gm
    gmb = gm.astype(BF)
    gm_scr[...] = gmb
    mask = adapter_mask(cfg, meta)
    select = slot_select(cfg, meta)
    grad_side = (mask * mm_nt(gmb, bo[...])).astype(BF)
    go = (mm_nt(gmb, wo[...]) + mm_nt(grad_side, ao[...])).astype(BF)
    w = cfg.groups * cfg.hd
    for h in range(G):
        go_scr[h] = go[:, h * w : (h + 1) * w]
    for k in range(G):
        go_out[k][...] = go_scr[hi ^ k]
    place_pieces(cfg, hi, attn, o_in)
    ograds[0] = mm(mm(grad_side, select).T.astype(BF), attn[...]).astype(BF)
    half = D // 2
    mine = gm_scr[:, pl.ds(pl.multiple_of(meta[1] * half, half), half)]
    ograds[1] = mm(oside[...].astype(F32).T.astype(BF), mine).astype(BF)


def output_kernel(cfg, meta, mixed, own, other, bd, out_ref):
    D = cfg.D
    total = own[...].astype(F32) + other[...].astype(F32)
    side = (adapter_mask(cfg, meta) * total[:, D:]).astype(BF)
    out_ref[...] = (mixed[...] + total[:, :D] + mm(side, bd[...])).astype(BF)


def head_back(cfg, cos, sin, grad, raw, g):
    hd = cfg.hd
    copies = raw.shape[1] // hd
    per = raw.shape[1] // cos.shape[1]
    un = grad * lanes(cos[...], per) - swap_halves(grad, hd) * lanes(sin[...], per)
    w = un * lanes(g[...], copies)
    rr = lax.rsqrt(block_mean(raw * raw, hd) + norm_eps)
    return rr * w - rr * rr * rr * raw * block_mean(w * raw, hd)


def half_lanes(cfg, meta):
    half = cfg.D // 2
    keep = pl.ds(pl.multiple_of(meta[1] * half, half), half)
    send = pl.ds(pl.multiple_of((1 - meta[1]) * half, half), half)
    return keep, send


def query_back_kernel(cfg, meta, *refs):
    G, S = cfg.G, cfg.S
    normed, raw, sides, cos, sin, gain, w, a, b, part, bgrad, akeep, asend, dq_scr, a_scr = refs[G:]
    place_pieces(cfg, meta[0] // cfg.lo, dq_scr, refs[:G])
    g = head_back(cfg, cos, sin, dq_scr[...].astype(F32), raw[...], gain).astype(BF)
    select = slot_select(cfg, meta)
    grad_side = (adapter_mask(cfg, meta) * mm_nt(g, b[...])).astype(BF)
    part[...] = mm_nt(g, w[...]) + mm_nt(grad_side, a[...])
    a_scr[...] = mm(mm(grad_side, select).T.astype(BF), normed[...])
    bgrad[...] = mm(sides[0].astype(F32).T.astype(BF), g).astype(BF)
    keep, send = half_lanes(cfg, meta)
    akeep[...] = a_scr[:, keep].astype(BF)
    asend[...] = a_scr[:, send].astype(BF)


def key_value_side_kernel(cfg, meta, *refs):
    G, S, hd = cfg.G, cfg.S, cfg.hd
    normed, raw, cos, sin, gain, bk, bv, grads, out_sides, akeep, asend, dkv_scr, a_scr = refs[G:]
    place_pieces(cfg, meta[0] // cfg.lo, dkv_scr, refs[:G])
    mask = adapter_mask(cfg, meta)
    select = slot_select(cfg, meta)
    dkv = dkv_scr[...]
    dk = jnp.concatenate([dkv[:, 2 * h * hd : (2 * h + 1) * hd] for h in range(G)], axis=1)
    dv = jnp.concatenate([dkv[:, (2 * h + 1) * hd : (2 * h + 2) * hd] for h in range(G)], axis=1)
    gk = head_back(cfg, cos, sin, dk.astype(F32), raw[...], gain).astype(BF)
    for i, (g, b) in enumerate(((gk, bk), (dv, bv))):
        grad_side = (mask * mm_nt(g, b[...])).astype(BF)
        grads[i] = g
        out_sides[i] = grad_side
        a_scr[i * S : (i + 1) * S, :] = mm(mm(grad_side, select).T.astype(BF), normed[...])
    keep, send = half_lanes(cfg, meta)
    akeep[...] = a_scr[:, keep].astype(BF)
    asend[...] = a_scr[:, send].astype(BF)


def key_value_back_kernel(cfg, meta, grads, grad_sides, sides, wk, wv, ak, av, qpart, part, bgrad):
    total = qpart[...]
    width = grads.shape[2]
    for i, (w, a) in enumerate(((wk, ak), (wv, av))):
        total = total + mm_nt(grads[i], w[...]) + mm_nt(grad_sides[i], a[...])
        bgrad[:, i * width : (i + 1) * width] = mm(
            sides[i].astype(F32).T.astype(BF), grads[i]
        ).astype(BF)
    part[...] = total.astype(BF)


def input_grad_kernel(cfg, meta, x_ref, gain, gm, own, other, out):
    x = x_ref[...].astype(F32)
    w = (own[...].astype(F32) + other[...].astype(F32)) * gain[...]
    rr = lax.rsqrt(jnp.mean(x * x, axis=-1, keepdims=True) + norm_eps)
    inner = jnp.mean(w * x, axis=-1, keepdims=True)
    out[...] = (gm[...] + rr * w - (rr * rr * rr * inner) * x).astype(BF)


class Units:
    def __init__(self, cfg, n, shared, private):
        self.n = n
        self.high = cfg.S // 16
        self.shared, self.private = shared, private
        self.us, self.up = self.per_chunk(shared), self.per_chunk(private)
        self.u = self.us + self.up

    def per_chunk(self, widths):
        return -(-sum(w // 128 for w in widths) * self.high // self.n)

    def places(self, which):
        widths, per, base = (
            (self.shared, self.us, 0) if which == 0 else (self.private, self.up, self.us)
        )
        at, out = 0, []
        for w in widths:
            spots = []
            for c in range(w // 128):
                for a in range(self.high):
                    spots.append((at // per, base + at % per, a, c))
                    at += 1
            out.append(spots)
        return out

    def spare(self):
        out = []
        for widths, per, base in ((self.shared, self.us, 0), (self.private, self.up, self.us)):
            count = sum(w // 128 for w in widths) * self.high
            out += [(i // per, base + i % per) for i in range(count, per * self.n)]
        return out

    def store(self, out, which, array, values, first=0):
        widths, per, base = (
            (self.shared, self.us, 0) if which == 0 else (self.private, self.up, self.us)
        )
        at = sum(w // 128 for w in widths[:array]) * self.high + first * self.high
        for c in range(values.shape[1] // 128):
            for a in range(self.high):
                unit = at + c * self.high + a
                out[unit // per, base + unit % per] = values[
                    a * 16 : a * 16 + 16, c * 128 : c * 128 + 128
                ]

    def clear_spare(self, out):
        for chunk, off in self.spare():
            out[chunk, off] = jnp.zeros((16, 128), BF)


def pack(units, scr, flip, outs, arrays):
    for i, values in enumerate(arrays):
        which = int(i >= len(units.shared))
        units.store(scr, which, i - which * len(units.shared), values)
    units.clear_spare(scr)
    for j, out in enumerate(outs):
        out[...] = scr[j ^ flip]


def add_halves(keep, got, count):
    total = (keep[...].astype(F32) + got[...].astype(F32)).astype(BF)
    rows = total.shape[0] // count
    return [total[i * rows : (i + 1) * rows] for i in range(count)]


def pack_qkv_kernel(cfg, units, meta, keep_q, got_q, keep, got, ograds, bq, bkv, *outs):
    scr, outs = outs[-1], outs[:-1]
    kw = bkv.shape[1] // 2
    shared = add_halves(keep_q, got_q, 1) + add_halves(keep, got, 2) + [ograds[1]]
    private = [ograds[0], bq[...], bkv[:, :kw], bkv[:, kw:]]
    pack(units, scr, meta[0] % cfg.lo, outs, shared + private)


def split_sum_kernel(cfg, meta, *refs):
    *terms, keep, send = refs
    bit = (meta[0] // cfg.lo) % 2
    for out, half in ((keep, bit), (send, 1 - bit)):
        total = terms[0][half].astype(F32)
        for term in terms[1:]:
            total = total + term[half].astype(F32)
        out[...] = total.astype(BF)


def sum_shared_kernel(meta, mine, got, out, shared):
    total = (mine[...].astype(F32) + got[...].astype(F32)).astype(BF)
    out[...] = total
    shared[...] = total[: shared.shape[0]]


def half_shared_kernel(meta, mine, got, out):
    count = got.shape[0]
    at = pl.ds(meta[1] * (count // 2), count // 2)
    out[: count // 2] = (mine[at].astype(F32) + got[at].astype(F32)).astype(BF)
    out[count // 2 :] = mine[count:]


def unpack(read, spots):
    cols = {}
    for chunk, off, a, c in spots:
        cols.setdefault(c, []).append(read(chunk, off))
    return jnp.concatenate([jnp.concatenate(cols[c], axis=0) for c in sorted(cols)], axis=1)


def expand_kernel(cfg, units, plan, halves, meta, *refs):
    own_in, other_in, outs = refs[: cfg.lo], refs[cfg.lo], refs[cfg.lo + 1 : -2]
    own, shared = refs[-2:]
    flip = meta[0] % cfg.lo
    wa = meta[1]
    count = shared.shape[2]
    for j in range(cfg.lo):
        if halves:
            own[j ^ flip] = own_in[j][...]
            shared[wa, j ^ flip] = own_in[j][:count]
            shared[1 - wa, j ^ flip] = other_in[j]
            continue
        for r in range(2):
            at = 2 * (j ^ flip) + (r ^ ((meta[0] // cfg.lo) % 2))
            own[at] = own_in[j][r]
            shared[wa, at] = own_in[j][r, :count]
            shared[1 - wa, at] = other_in[j, r]
    select = slot_select(cfg, meta)

    def write(out, values, transposed, at):
        full = mm(select, values)
        if transposed:
            out[at : at + full.shape[1], :] = full.T
        else:
            out[:, at : at + full.shape[1]] = full

    for (which, i, transposed), out in zip(plan, outs):
        spots = units.places(which)[i]
        if which == 1:
            shift = 0 if halves else count
            write(out, unpack(lambda chunk, off: own[chunk, off - shift], spots), transposed, 0)
        elif halves:
            for w in range(2):
                values = unpack(lambda chunk, off: shared[w, chunk, off], spots)
                write(out, values, transposed, w * values.shape[1])
        else:
            values = unpack(lambda chunk, off: shared[off // count, chunk, off % count], spots)
            write(out, values, transposed, 0)


def upper_bits(cfg):
    bits, bit = [], cfg.n // 2
    while bit >= cfg.lo:
        bits.append(bit)
        bit //= 2
    return bits


def after(*values):
    return lax.optimization_barrier(values)


def swap_cores(value):
    return lax.ppermute(value, "wa", [(0, 1), (1, 0)])


def permute(cfg, value, bits):
    return lax.ppermute(value, "ctx", [(i, i ^ bits) for i in range(cfg.n)])


def per_device(
    hidden_in, attn_gain, query_weight, key_weight, value_weight, query_gain, key_gain, out_weight,
    ffn_gain, gate_weight, up_weight, down_weight, query_adapt_in, query_adapt_out, key_adapt_in,
    key_adapt_out, value_adapt_in, value_adapt_out, out_adapt_in, out_adapt_out, gate_adapt_in,
    gate_adapt_out, up_adapt_in, up_adapt_out, down_adapt_in, down_adapt_out, document_extra,
    document_adapter, cotangent,
):
    head_dim = query_gain.shape[0]
    cfg = Cfg(
        tokens=hidden_in.shape[0],
        n_ctx=lax.axis_size("ctx"),
        heads_kv=key_weight.shape[1] // head_dim,
        groups=query_weight.shape[1] // key_weight.shape[1],
        head_dim=head_dim,
        docs=document_extra.shape[0],
        adapt_width=query_adapt_in.shape[1],
        width=hidden_in.shape[2],
        hidden=gate_weight.shape[1],
    )
    T, D, G, S, AW, n, lo = cfg.T, cfg.D, cfg.G, cfg.S, cfg.AW, cfg.n, cfg.lo
    gw = cfg.groups * head_dim
    QW, KW = query_weight.shape[1], key_weight.shape[1]
    meta = (document_extra, document_adapter)
    x = hidden_in.reshape(T, D)
    cot = cotangent.reshape(T, D)
    gain_a = attn_gain.reshape(1, D)
    gain_f = ffn_gain.reshape(1, D)
    qg = query_gain.reshape(1, head_dim)
    kg = key_gain.reshape(1, head_dim)

    lane = np.arange(2 * head_dim) % (head_dim // 2)
    inverse = np.exp(lane * (-2.0 * math.log(theta_base) / head_dim)).astype(np.float32)[None, :]

    piece = ((T, gw), BF)
    fetched = [
        x, key_adapt_in, value_adapt_in, key_weight, key_adapt_out, value_weight, value_adapt_out,
    ]
    first = call(
        functools.partial(key_value_kernel, cfg),
        [piece] * G
        + [((T, KW), F32), ((2, T, S), BF), ((T, D), BF)]
        + [((T, 2 * head_dim), F32)] * 2,
        [meta, *fetched, gain_a, kg, inverse],
        scratch=[pltpu.VMEM(value.shape, value.dtype) for value in fetched]
        + [pltpu.SemaphoreType.DMA((len(fetched),)), pltpu.VMEM((G, T, 2 * head_dim), BF)],
        us=4,
        name="key_value",
        in_place=len(fetched),
        large=True,
    )
    kv_send = first[:G]
    kraw, sides, normed, cos, sin = first[G:]

    def to_heads(pieces):
        return [pieces[0]] + [permute(cfg, pieces[k], k * lo) for k in range(1, G)]

    def add(values):
        return sum(value.astype(F32) for value in values).astype(BF)

    def to_plane(value):
        return [value] + [permute(cfg, value, j) for j in range(1, lo)]

    kv_heads = to_heads(kv_send)
    second = call(
        functools.partial(query_kernel, cfg),
        [piece] * G + [((T, QW), F32), ((1, T, S), BF), items_shape(cfg)],
        [meta, normed, cos, sin, query_weight, query_adapt_in, query_adapt_out, qg],
        scratch=[pltpu.VMEM((G, T, gw), BF)],
        us=3,
        name="query",
        lists=1,
    )
    q_send, (qraw, side_q, items) = second[:G], second[G:]
    listed = (*meta, items)
    both = list(after(*kv_heads, *q_send))
    kv_heads, q_send = both[:G], both[G:]
    kv = to_plane(jnp.stack(kv_heads))
    q = to_heads(q_send)
    grad_hidden, gst = call(
        functools.partial(hidden_grad_kernel, cfg),
        [((T, cfg.F), F32), ((S, T), BF)],
        [meta, cot, down_weight, down_adapt_out, down_adapt_in],
        us=3,
        name="hidden_grad",
    )
    grad_hidden, *both = after(grad_hidden, *kv, *q)
    kv, q = both[:lo], both[lo:]
    tiles = lambda dtype, width=gw: pltpu.VMEM((cfg.NT, 2 * cfg.QH, width), dtype)
    attn = call(
        functools.partial(attend_kernel, cfg),
        [piece] * G + [((G, T, gw), BF), ((G, T, gw), F32)],
        [listed] + q + kv,
        scratch=[tiles(BF), tiles(F32)],
        us=12,
        name="attend",
    )
    o_send, o_all, linv = attn[:G], attn[G], attn[G + 1]
    o = to_heads(o_send)
    q_stack, _ = after(jnp.stack(q), o_send[0])
    q_plane = to_plane(q_stack)
    (opart,) = call(
        functools.partial(out_kernel, cfg),
        [((T, D + AW), BF)],
        [meta] + o + [out_weight, out_adapt_in],
        scratch=[pltpu.VMEM((T, QW), BF)],
        us=3,
        name="out_proj",
    )
    units_f = Units(cfg, 2 * lo, [D] * 3, [cfg.F] * 3)
    ffn = ffn_call(
        cfg, units_f, meta, x, opart, swap_cores(opart), out_adapt_out, gain_f, gate_weight, up_weight,
        down_weight, gate_adapt_out, up_adapt_out, gate_adapt_in, up_adapt_in, down_adapt_in,
        cot, grad_hidden, gst,
    )
    mixed, dfn, dpart, oside, *parts_f = ffn
    dfn, *q_plane = after(dfn, *q_plane)
    mg = call(
        functools.partial(mixed_grad_kernel, cfg),
        [((T, D), F32), ((2, S, D // 2), BF)] + [piece] * G,
        [meta, mixed, dfn, swap_cores(dfn), cot, gain_f]
        + o
        + [out_weight, out_adapt_in, out_adapt_out, oside],
        scratch=[pltpu.VMEM((T, QW), BF), pltpu.VMEM((G, T, gw), BF), pltpu.VMEM((T, D), BF)],
        us=0.01,
        name="mixed_grad",
    )
    grad_mixed, ograds, go_send = mg[0], mg[1], mg[2:]
    go_heads = to_heads(go_send)
    parts_f = [parts_f[0]] + [permute(cfg, parts_f[j], j) for j in range(1, lo)]
    message = G * T + -(-2 * cfg.groups * cfg.NT // 16) * 16
    (go_all,) = call(
        functools.partial(scale_kernel, cfg),
        [((message, gw), BF)],
        [meta] + go_heads + [linv, o_all],
        scratch=[
            pltpu.VMEM((cfg.NT, cfg.QH, gw), F32),
            pltpu.VMEM((cfg.groups * cfg.NT, gw), F32),
        ],
        us=0.01,
        name="scale",
    )
    go_all, *parts_f = after(go_all, *parts_f)
    sum_f, send_f = call(
        functools.partial(split_sum_kernel, cfg),
        [((units_f.u, 16, 128), BF)] * 2,
        [meta, *parts_f],
        us=0.01,
        name="split_sum",
    )
    go_plane = to_plane(go_all)
    dq_send = call(
        functools.partial(grad_query_kernel, cfg),
        [piece] * G,
        [listed] + q + kv + [go_all, o_all],
        scratch=[tiles(BF), tiles(BF), tiles(F32, 1), tiles(F32)],
        us=13.5,
        name="grad_query",
    )
    near, far = upper_bits(cfg)[1], upper_bits(cfg)[0]
    got_f, *dq_send = after(permute(cfg, send_f, near), *dq_send)
    sum_f = add([sum_f, got_f])
    dq = to_heads(dq_send)
    dkv_send = call(
        functools.partial(grad_key_kernel, cfg),
        [piece] * G,
        [listed, kv[0]] + q_plane + go_plane,
        scratch=[tiles(BF), tiles(BF), pltpu.VMEM((cfg.NT, 16, cfg.KT), F32), tiles(F32)]
        + [tiles(F32)],
        us=16,
        name="grad_key",
    )
    both = list(after(*dq, *dkv_send))
    dq, dkv_send = both[:G], both[G:]
    dkv = to_heads(dkv_send)
    qpart, bgrad_q, akeep_q, asend_q = call(
        functools.partial(query_back_kernel, cfg),
        [((T, D), F32), ((S, QW), BF), ((S, D // 2), BF), ((S, D // 2), BF)],
        [meta]
        + dq
        + [
            normed, qraw, side_q, cos, sin, qg, query_weight, query_adapt_in, query_adapt_out,
        ],
        scratch=[pltpu.VMEM((T, QW), BF), pltpu.VMEM((S, D), F32)],
        us=0.01,
        name="query_back",
    )
    got_f, qpart = after(permute(cfg, sum_f, far), qpart)
    sum_f, shared_f = call(
        sum_shared_kernel,
        [((units_f.u, 16, 128), BF), ((units_f.us, 16, 128), BF)],
        [meta, sum_f, got_f],
        us=0.01,
        name="sum_shared",
    )
    shared_f, qpart, *dkv = after(shared_f, qpart, *dkv)
    kv_grads, kv_sides, akeep_kv, asend_kv = call(
        functools.partial(key_value_side_kernel, cfg),
        [((2, T, KW), BF), ((2, T, AW), BF), ((2 * S, D // 2), BF), ((2 * S, D // 2), BF)],
        [meta] + dkv + [normed, kraw, cos, sin, kg, key_adapt_out, value_adapt_out],
        scratch=[pltpu.VMEM((T, 2 * KW), BF), pltpu.VMEM((2 * S, D), F32)],
        us=0.01,
        name="key_value_side",
    )
    dnormed, bgrad_kv = call(
        functools.partial(key_value_back_kernel, cfg),
        [((T, D), BF), ((S, 2 * KW), BF)],
        [meta, kv_grads, kv_sides, sides, key_weight, value_weight, key_adapt_in, value_adapt_in]
        + [qpart],
        us=0.01,
        name="key_value_back",
    )

    def expand(units, chunks, plan, halves, outs, name):
        shared = units.us if halves else units.us // 2
        theirs = swap_cores(jnp.stack([chunk[..., :shared, :, :] for chunk in chunks]))
        per = chunks[0].shape[-3]
        return call(
            functools.partial(expand_kernel, cfg, units, plan, halves),
            outs,
            [meta, *chunks, theirs],
            scratch=[
                pltpu.VMEM((units.n, per, 16, 128), BF),
                pltpu.VMEM((2, units.n, shared, 16, 128), BF),
            ],
            us=4,
            name=name,
        )

    units_q = Units(cfg, lo, [D // 2] * 4, [QW, QW, KW, KW])
    parts_q = call(
        functools.partial(pack_qkv_kernel, cfg, units_q),
        [((units_q.u, 16, 128), BF)] * lo,
        [meta, akeep_q, swap_cores(asend_q), akeep_kv, swap_cores(asend_kv), ograds, bgrad_q]
        + [bgrad_kv],
        scratch=[pltpu.VMEM((lo, units_q.u, 16, 128), BF)],
        us=0.01,
        name="pack_qkv",
    )
    (sum_f,) = call(
        half_shared_kernel,
        [((units_f.u - units_f.us // 2, 16, 128), BF)],
        [meta, sum_f, swap_cores(shared_f)],
        us=0.01,
        name="half_shared",
    )
    sum_f, dnormed, *parts_q = after(sum_f, dnormed, *parts_q)
    dn_other = swap_cores(dnormed)
    near_f = permute(cfg, sum_f, near)
    sum_q = add([parts_q[0]] + [permute(cfg, parts_q[j], j) for j in range(1, lo)])
    sum_q, dn_other, sum_f, near_f = after(sum_q, dn_other, sum_f, near_f)
    all_f = to_plane(jnp.stack([sum_f, near_f]))
    (input_rows,) = call(
        functools.partial(input_grad_kernel, cfg),
        [((T, D), BF)],
        [meta, x, gain_a, grad_mixed, dnormed, dn_other],
        us=0.01,
        name="input_grad",
    )
    got_q, input_rows = after(permute(cfg, sum_q, near), input_rows)
    sum_q = add([sum_q, got_q])
    got_q, *all_f = after(permute(cfg, sum_q, far), *all_f)
    sum_q, dpart = after(add([sum_q, got_q]), dpart)
    pieces_q = to_plane(sum_q)
    (out_rows,) = call(
        functools.partial(output_kernel, cfg),
        [((T, D), BF)],
        [meta, mixed, dpart, swap_cores(dpart), down_adapt_out],
        us=0.01,
        name="output",
    )
    gate_in, up_in, down_out, gate_out, up_out, down_in = expand(
        units_f,
        all_f,
        [(0, 0, True), (0, 1, True), (0, 2, False), (1, 0, False), (1, 1, False), (1, 2, True)],
        False,
        [((D, AW), F32), ((D, AW), F32), ((AW, D), F32)]
        + [((AW, cfg.F), F32), ((AW, cfg.F), F32), ((cfg.F, AW), F32)],
        "expand_ffn",
    )
    down_out, out_rows, *pieces_q = after(down_out, out_rows, *pieces_q)
    query_in, key_in, value_in, out_out, out_in, query_out, key_out, value_out = expand(
        units_q,
        pieces_q,
        [(0, 0, True), (0, 1, True), (0, 2, True), (0, 3, False)]
        + [(1, 0, True), (1, 1, False), (1, 2, False), (1, 3, False)],
        True,
        [((D, AW), F32)] * 3
        + [((AW, D), F32), ((QW, AW), F32), ((AW, QW), F32), ((AW, KW), F32), ((AW, KW), F32)],
        "expand_qkv",
    )
    return (
        out_rows.reshape(T, 1, D),
        input_rows.reshape(T, 1, D),
        query_in,
        query_out,
        key_in,
        key_out,
        value_in,
        value_out,
        out_in,
        out_out,
        gate_in,
        gate_out,
        up_in,
        up_out,
        down_in,
        down_out,
    )


def solution(mesh):
    return jax.shard_map(
        per_device,
        mesh=mesh,
        in_specs=(
            P(None, "ctx", None), P(), P(None, "wa"), P(None, "wa"), P(None, "wa"), P(), P(),
            P("wa", None), P(), P(None, "wa"), P(None, "wa"), P("wa", None), P(), P(None, "wa"),
            P(), P(None, "wa"), P(), P(None, "wa"), P("wa", None), P(), P(), P(None, "wa"), P(),
            P(None, "wa"), P("wa", None), P(), P(), P(), P(None, "ctx", None),
        ),
        out_specs=(
            P(None, "ctx", None), P(None, "ctx", None), P(), P(None, "wa"), P(), P(None, "wa"), P(),
            P(None, "wa"), P("wa", None), P(), P(), P(None, "wa"), P(), P(None, "wa"),
            P("wa", None), P(),
        ),
        check_vma=False,
    )
```

```python
import functools
import math

import jax
import jax.numpy as jnp
import numpy as np
from jax import lax
from jax.experimental import pallas as pl
from jax.experimental.pallas import tpu as pltpu
from jax.sharding import PartitionSpec as P

RANK = 16
DOC_MIN = 200

norm_eps = 1e-05
theta_base = 1000000.0
BF = jnp.bfloat16
F32 = jnp.float32
LOG2E = 1.4426950408889634
STEP, STEP_QUERY = 11, 11
FFN_TILE, FFN_STEP = 256, 3
VMEM_SMALL = 28 * 1024 * 1024
VMEM_LARGE = 56 * 1024 * 1024


def mm(left, right):
    return jnp.dot(left, right, preferred_element_type=F32)


def mm_nt(left, right):
    return lax.dot_general(left, right, (((1,), (1,)), ((), ())), preferred_element_type=F32)


def mm_tn(left, right):
    return lax.dot_general(left, right, (((0,), (0,)), ((), ())), preferred_element_type=F32)


def iota(shape, dim):
    return lax.broadcasted_iota(jnp.int32, shape, dim)


class Cfg:
    def __init__(self, tokens, n_ctx, heads_kv, groups, head_dim, docs, adapt_width, width, hidden):
        self.T = tokens
        self.n = n_ctx
        self.G = heads_kv
        self.lo = n_ctx // heads_kv
        self.groups = groups
        self.hd = head_dim
        self.docs = docs
        self.AW = adapt_width
        self.slots = min(docs, adapt_width // RANK)
        self.S = self.slots * RANK
        self.D = width
        self.F = hidden
        self.R = max(16, min(tokens, 512 // n_ctx))
        self.NT = tokens // self.R
        self.span = self.R * n_ctx
        self.QH = self.G * self.R
        self.KT = n_ctx * self.R


class Meta:
    def __init__(self, extra, adapter, items=None):
        self.refs, self.docs, self.items = (extra, adapter), extra.shape[0], items

    def __getitem__(self, i):
        if i < 2:
            return lax.axis_index(("ctx", "wa")[i])
        return self.refs[(i - 2) // self.docs][(i - 2) % self.docs]


def with_meta(kernel, count):
    return lambda *refs: kernel(Meta(*refs[:count]), *refs[count:])


def doc_starts(cfg, meta):
    out = [jnp.int32(0)]
    for j in range(cfg.docs):
        out.append(out[-1] + meta[2 + j] + (DOC_MIN - 1))
    return out


def start_of(starts, token):
    out = jnp.zeros_like(token)
    for s in starts[1:-1]:
        out = jnp.where(token >= s, s, out)
    return out


def end_of(starts, token):
    out = starts[1]
    for j in range(1, len(starts) - 1):
        out = jnp.where(token >= starts[j], starts[j + 1], out)
    return out


def adapter_mask(cfg, meta):
    token = iota((cfg.T, cfg.AW), 0) * cfg.n + meta[0]
    starts = doc_starts(cfg, meta)
    adapter = jnp.full((cfg.T, cfg.AW), meta[2 + cfg.docs], jnp.int32)
    for j in range(1, cfg.docs):
        adapter = jnp.where(token >= starts[j], meta[2 + cfg.docs + j], adapter)
    return (adapter == iota((cfg.T, cfg.AW), 1) // RANK).astype(F32)


def slot_select(cfg, meta):
    row = iota((cfg.AW, cfg.S), 0)
    col = iota((cfg.AW, cfg.S), 1)
    if cfg.S == cfg.AW:
        return (row == col).astype(BF)
    target = jnp.full((cfg.AW, cfg.S), -1, jnp.int32)
    for s in range(cfg.slots):
        mine = meta[2 + cfg.docs + s]
        again = jnp.int32(0)
        for e in range(s):
            again = jnp.where(meta[2 + cfg.docs + e] == mine, 1, again)
        base = jnp.where(again == 1, -4 * cfg.AW, mine * RANK)
        target = jnp.where(col // RANK == s, base + col % RANK, target)
    return (row == target).astype(BF)


def block_mean(values, hd):
    part = min(values.shape[1], 256)
    ones = (iota((part, part), 0) // hd == iota((part, part), 1) // hd).astype(BF)
    out = []
    for at in range(0, values.shape[1], part):
        piece = values[:, at : at + part]
        high = piece.astype(BF)
        low = (piece - high.astype(F32)).astype(BF)
        out.append((mm(high, ones) + mm(low, ones)) * (1.0 / hd))
    return jnp.concatenate(out, axis=1)


def swap_halves(values, hd):
    width = values.shape[1]
    half = hd // 2
    first = iota(values.shape, 1) % hd < half
    return jnp.where(first, pltpu.roll(values, width - half, 1), pltpu.roll(values, half, 1))


def lanes(values, copies):
    return jnp.concatenate([values] * copies, axis=1) if copies > 1 else values


def params(large=False, **kw):
    limit = VMEM_SMALL if lax.axis_size("ctx") <= 16 and not large else VMEM_LARGE
    return pltpu.CompilerParams(vmem_limit_bytes=limit, **kw)


SMEM = pl.BlockSpec(memory_space=pltpu.SMEM)


def cost(us):
    return pl.CostEstimate(flops=int(us * 1.15e9), bytes_accessed=0, transcendentals=0)


def call(kernel, outs, ins, scratch=(), us=1.0, name=None, large=False, in_place=0, lists=0):
    count = len(ins[0])
    ins = [*ins[0], *ins[1:]]
    return pl.pallas_call(
        with_meta(kernel, count),
        out_shape=[jax.ShapeDtypeStruct(s, d) for s, d in outs],
        in_specs=[SMEM] * count
        + [pl.BlockSpec(memory_space=pl.ANY)] * in_place
        + [pl.BlockSpec(memory_space=pltpu.VMEM)] * (len(ins) - count - in_place),
        out_specs=[pl.BlockSpec(memory_space=pltpu.VMEM)] * (len(outs) - lists) + [SMEM] * lists,
        scratch_shapes=list(scratch),
        compiler_params=params(large),
        cost_estimate=cost(us),
        name=name,
    )(*ins)


def head_prep(cfg, cos, sin, raw, g):
    hd = cfg.hd
    copies = raw.shape[1] // hd
    scaled = raw * lax.rsqrt(block_mean(raw * raw, hd) + norm_eps) * lanes(g[...], copies)
    per = raw.shape[1] // cos.shape[1]
    return scaled * lanes(cos[...], per) + swap_halves(scaled, hd) * lanes(sin[...], per)


def rotation(cfg, meta, inverse, cos, sin):
    width, half = 2 * cfg.hd, cfg.hd // 2
    blocks = width // half
    rows = cfg.T // blocks
    lane = iota((rows, width), 1)
    token = ((lane // half) * rows + iota((rows, width), 0)) * cfg.n + meta[0]
    angle = (token - start_of(doc_starts(cfg, meta), token)).astype(F32) * inverse[...]
    sign = jnp.where(lane % cfg.hd < half, -1.0, 1.0)
    for out, values, scale in ((cos, jnp.cos(angle), None), (sin, jnp.sin(angle), sign)):
        for b in range(blocks):
            part = pltpu.roll(values, width - b * half, 1) if b else values
            part = jnp.where(lane < half, part, 0.0)
            size = half
            while size < width:
                part = part + pltpu.roll(part, size, 1)
                size *= 2
            out[b * rows : (b + 1) * rows, :] = part if scale is None else part * scale


def key_value_kernel(cfg, meta, *refs):
    G, hd = cfg.G, cfg.hd
    sources, (gain, kg, inverse), refs = refs[:7], refs[7:10], refs[10:]
    kv_out, refs = refs[:G], refs[G:]
    raw_ref, sides_ref, normed_ref, cos, sin, *scratch = refs
    buffers, sems, kv_scr = scratch[:7], scratch[7], scratch[8]
    copies = [
        pltpu.make_async_copy(source, buffer, sems.at[i])
        for i, (source, buffer) in enumerate(zip(sources, buffers))
    ]
    for copy in copies:
        copy.start()
    x_buf, ak, av, wk, bk, wv, bv = buffers
    rotation(cfg, meta, inverse, cos, sin)
    mask = adapter_mask(cfg, meta)
    select = slot_select(cfg, meta)
    copies[0].wait()
    x = x_buf[...].astype(F32)
    rr = lax.rsqrt(jnp.mean(x * x, axis=-1, keepdims=True) + norm_eps)
    normed = (x * rr * gain[...]).astype(BF)
    normed_ref[...] = normed
    for copy in copies[1:]:
        copy.wait()
    raws = []
    for i, (w, a, b) in enumerate(((wk, ak, bk), (wv, av, bv))):
        side = (mask * mm(normed, a[...])).astype(BF)
        sides_ref[i] = mm(side, select).astype(BF)
        raws.append(mm(normed, w[...]) + mm(side, b[...]))
    kraw, vraw = raws
    raw_ref[...] = kraw
    key = head_prep(cfg, cos, sin, kraw, kg).astype(BF)
    value = vraw.astype(BF)
    for h in range(G):
        at = slice(h * hd, (h + 1) * hd)
        kv_scr[h] = jnp.concatenate([key[:, at], value[:, at]], axis=1)
    hi = meta[0] // cfg.lo
    for k in range(G):
        kv_out[k][...] = kv_scr[hi ^ k]


def query_kernel(cfg, meta, normed_ref, cos, sin, w, a, b, g, *refs):
    G = cfg.G
    q_out, raw_ref, side_ref, items, q_scr = refs[:G], *refs[G:]
    list_items(cfg, doc_starts(cfg, meta), items)
    normed = normed_ref[...]
    side = (adapter_mask(cfg, meta) * mm(normed, a[...])).astype(BF)
    side_ref[0] = mm(side, slot_select(cfg, meta)).astype(BF)
    raw = mm(normed, w[...]) + mm(side, b[...])
    raw_ref[...] = raw
    query = head_prep(cfg, cos, sin, raw, g).astype(BF)
    gw = cfg.groups * cfg.hd
    for h in range(G):
        q_scr[h] = query[:, h * gw : (h + 1) * gw]
    hi = meta[0] // cfg.lo
    for k in range(G):
        q_out[k][...] = q_scr[hi ^ k]


def tile_of(cfg, pieces, t):
    rows = pl.ds(pl.multiple_of(t * cfg.R, cfg.R), cfg.R)
    return jnp.concatenate([piece[rows, :] for piece in pieces], axis=0)


def list_items(cfg, starts, items):
    def per_query(qt, count):
        def one(s, at):
            items[0, at] = qt
            items[1, at] = s
            return at + 1

        return lax.fori_loop(start_of(starts, qt * cfg.span) // cfg.span, qt + 1, one, count)

    count = lax.fori_loop(0, cfg.NT, per_query, 0)
    for i in range(STEP - 1):
        items[0, count + i] = 0
        items[1, count + i] = cfg.NT - 1
    items[0, items.shape[1] - 1] = count


def steps_of(items, step):
    return (items[0, items.shape[1] - 1] + step - 1) // step


def items_shape(cfg):
    return ((2, cfg.NT * (cfg.NT + 1) // 2 + STEP), jnp.int32)


def split_pieces(ref, count):
    return [ref.at[i] for i in range(count)]


def message_pieces(cfg, ref):
    return [ref.at[pl.ds(k * cfg.T, cfg.T)] for k in range(cfg.G)]


def token_in_span(cfg, meta, index):
    hi, lo = meta[0] // cfg.lo, meta[0] % cfg.lo
    piece, row = index // cfg.R, index % cfg.R
    j, k = piece // cfg.G, piece % cfg.G
    return row * cfg.n + (hi ^ k) * cfg.lo + (lo ^ j)


def pad_queries(cfg, qq, side):
    hd = cfg.hd
    wide = qq.astype(F32)
    first = iota(wide.shape, 1) < hd
    rolled = pltpu.roll(wide, hd, 1)
    if side == 0:
        parts = [jnp.where(first, wide, 0.0), jnp.where(first, rolled, 0.0)]
    else:
        parts = [jnp.where(first, 0.0, rolled), jnp.where(first, 0.0, wide)]
    return jnp.concatenate(parts, axis=0).astype(BF)


def attend_kernel(cfg, meta, *refs):
    G, R, hd, QH = cfg.G, cfg.R, cfg.hd, cfg.QH
    q_in, own, others = refs[:G], refs[G], refs[G + 1 : G + cfg.lo]
    rest = refs[G + cfg.lo :]
    o_out, o_all, linv, q_scr, acc_scr = rest[:G], *rest[G:]
    kv_pieces = split_pieces(own, G)
    for ref in others:
        kv_pieces = kv_pieces + split_pieces(ref, G)
    starts = doc_starts(cfg, meta)
    items = meta.items
    scale = hd ** (-0.5) * LOG2E
    key_off = token_in_span(cfg, meta, iota((1, cfg.KT), 1))
    row_off = token_in_span(cfg, meta, iota((2 * QH, 1), 0) % QH)
    key_lanes = iota((cfg.KT, 2 * hd), 1) < hd
    for t in range(cfg.NT):
        q_scr[t] = pad_queries(cfg, tile_of(cfg, q_in, t), 0)
        acc_scr[t] = jnp.zeros((2 * QH, 2 * hd), F32)

    def step(i, carry):
        parts = []
        for u in range(STEP):
            qt, s = items[0, i * STEP + u], items[1, i * STEP + u]
            kv = tile_of(cfg, kv_pieces, s)
            token = row_off + qt * cfg.span
            key_token = key_off + s * cfg.span
            e = jnp.exp2(mm_nt(q_scr[qt], kv) * scale)
            e = jnp.where((key_token <= token) & (key_token >= start_of(starts, token)), e, 0.0)
            parts.append((qt, mm(e.astype(BF), jnp.where(key_lanes, jnp.ones_like(kv), kv))))
        for qt, part in parts:
            acc_scr[qt] += part
        return carry

    lax.fori_loop(0, steps_of(items, STEP), step, 0)
    half = iota((QH, 2 * hd), 1) < hd
    for t in range(cfg.NT):
        acc = acc_scr[t]
        inv0 = 1.0 / acc[:QH]
        inv1 = 1.0 / acc[QH:]
        out0 = pltpu.roll(acc[:QH], hd, 1) * inv0
        out1 = acc[QH:] * pltpu.roll(inv1, hd, 1)
        out = jnp.where(half, out0, out1).astype(BF)
        inv = jnp.where(half, inv0, pltpu.roll(inv1, hd, 1))
        rows = slice(t * R, (t + 1) * R)
        for k in range(G):
            o_out[k][rows, :] = out[k * R : (k + 1) * R]
            o_all[k, rows, :] = out[k * R : (k + 1) * R]
            linv[k, rows, :] = inv[k * R : (k + 1) * R]


def head_sums(cfg, prod):
    pick = (iota((16, prod.shape[1]), 1) // cfg.hd == iota((16, prod.shape[1]), 0)).astype(BF)
    high = prod.astype(BF)
    low = (prod - high.astype(F32)).astype(BF)
    return mm_nt(pick, high) + mm_nt(pick, low)


def scale_kernel(cfg, meta, *refs):
    G, T, R, NT, QH = cfg.G, cfg.T, cfg.R, cfg.NT, cfg.QH
    go, linv, o_all, out, scr, delta = refs[:G], refs[G], refs[G + 1], refs[G + 2], *refs[G + 3 :]
    delta[...] = jnp.zeros_like(delta)
    for k in range(G):
        scaled = (go[k][...].astype(F32) * linv[k]).astype(BF)
        out[k * T : (k + 1) * T, :] = scaled
        prod = scaled.astype(F32) * o_all[k].astype(F32)
        for t in range(NT):
            scr[t, k * R : (k + 1) * R, :] = prod[t * R : (t + 1) * R]
    for t in range(NT):
        sums = head_sums(cfg, scr[t])
        for h in range(cfg.groups):
            delta[h * NT + t : h * NT + t + 1, :QH] = sums[h : h + 1]
    high = delta[...].astype(BF)
    at = G * T
    rows = cfg.groups * NT
    out[at : at + rows, :] = high
    out[at + rows : at + 2 * rows, :] = (delta[...] - high.astype(F32)).astype(BF)


def grad_query_kernel(cfg, meta, *refs):
    G, R, hd, QH = cfg.G, cfg.R, cfg.hd, cfg.QH
    q_in, own, others = refs[:G], refs[G], refs[G + 1 : G + cfg.lo]
    go_ref, o_ref = refs[G + cfg.lo : G + cfg.lo + 2]
    rest = refs[G + cfg.lo + 2 :]
    dq_out, q_scr, go_scr, delta_scr, acc_scr = rest[:G], *rest[G:]
    kv_pieces = split_pieces(own, G)
    for ref in others:
        kv_pieces = kv_pieces + split_pieces(ref, G)
    starts = doc_starts(cfg, meta)
    items = meta.items
    scale = hd ** (-0.5) * LOG2E
    key_off = token_in_span(cfg, meta, iota((1, cfg.KT), 1))
    row_off = token_in_span(cfg, meta, iota((2 * QH, 1), 0) % QH)
    half = iota((QH, 2 * hd), 1) < hd
    for t in range(cfg.NT):
        go = tile_of(cfg, message_pieces(cfg, go_ref), t)
        prod = go.astype(F32) * tile_of(cfg, split_pieces(o_ref, G), t).astype(F32)
        q_scr[t] = pad_queries(cfg, tile_of(cfg, q_in, t), 0)
        go_scr[t] = pad_queries(cfg, go, 1)
        delta_scr[t, :QH] = jnp.sum(jnp.where(half, prod, 0.0), axis=1, keepdims=True)
        delta_scr[t, QH:] = jnp.sum(jnp.where(half, 0.0, prod), axis=1, keepdims=True)
        acc_scr[t] = jnp.zeros((2 * QH, 2 * hd), F32)

    def step(i, carry):
        parts = []
        for u in range(STEP_QUERY):
            qt, s = items[0, i * STEP_QUERY + u], items[1, i * STEP_QUERY + u]
            kv = tile_of(cfg, kv_pieces, s)
            token = row_off + qt * cfg.span
            key_token = key_off + s * cfg.span
            e = jnp.exp2(mm_nt(q_scr[qt], kv) * scale)
            ds = e * (mm_nt(go_scr[qt], kv) - delta_scr[qt])
            ds = jnp.where((key_token <= token) & (key_token >= start_of(starts, token)), ds, 0.0)
            parts.append((qt, mm(ds.astype(BF), kv)))
        for qt, part in parts:
            acc_scr[qt] += part
        return carry

    lax.fori_loop(0, steps_of(items, STEP_QUERY), step, 0)
    for t in range(cfg.NT):
        acc = acc_scr[t]
        out = jnp.where(half, acc[:QH], pltpu.roll(acc[QH:], hd, 1)) * hd ** (-0.5)
        out = out.astype(BF)
        for k in range(G):
            dq_out[k][t * R : (t + 1) * R, :] = out[k * R : (k + 1) * R]


def grad_key_kernel(cfg, meta, *refs):
    G, T, R, hd, lo, QH, NT = cfg.G, cfg.T, cfg.R, cfg.hd, cfg.lo, cfg.QH, cfg.NT
    own = refs[0]
    q_refs, go_refs = (refs[1 + i * lo : 1 + (i + 1) * lo] for i in range(2))
    rest = refs[1 + 2 * lo :]
    dkv_out, key_scr, value_scr, delta_scr, gk_scr, gv_scr = rest[:G], *rest[G:]
    q_pieces = [piece for ref in q_refs for piece in split_pieces(ref, G)]
    go_pieces = [piece for ref in go_refs for piece in message_pieces(cfg, ref)]
    starts = doc_starts(cfg, meta)
    items = meta.items
    scale = hd ** (-0.5) * LOG2E
    rows = cfg.groups * NT
    for j in range(lo):
        sums = go_refs[j][G * T : G * T + 2 * rows, :].astype(F32)
        sums = sums[:rows] + sums[rows:]
        for t in range(NT):
            for h in range(cfg.groups):
                at = h * NT + t
                delta_scr[t, h : h + 1, j * QH : (j + 1) * QH] = sums[at : at + 1, :QH]
    query_off = token_in_span(cfg, meta, iota((1, cfg.KT), 1))
    row_off = token_in_span(cfg, meta, iota((2 * QH, 1), 0) % QH)
    first = iota((QH, 2 * hd), 1) < hd
    for t in range(NT):
        kv = tile_of(cfg, split_pieces(own, G), t).astype(F32)
        rolled = pltpu.roll(kv, hd, 1)
        keys = [jnp.where(first, kv, 0.0), jnp.where(first, 0.0, rolled)]
        values = [jnp.where(first, rolled, 0.0), jnp.where(first, 0.0, kv)]
        key_scr[t] = jnp.concatenate(keys, axis=0).astype(BF)
        value_scr[t] = jnp.concatenate(values, axis=0).astype(BF)
        gk_scr[t] = jnp.zeros((2 * QH, 2 * hd), F32)
        gv_scr[t] = jnp.zeros((2 * QH, 2 * hd), F32)

    def step(i, carry):
        parts = []
        for u in range(STEP):
            t, kt = items[0, i * STEP + u], items[1, i * STEP + u]
            queries, grads = tile_of(cfg, q_pieces, t), tile_of(cfg, go_pieces, t)
            key_token = row_off + kt * cfg.span
            token = query_off + t * cfg.span
            e = jnp.exp2(mm_nt(key_scr[kt], queries) * scale)
            e = jnp.where((key_token <= token) & (key_token >= start_of(starts, token)), e, 0.0)
            dp = mm_nt(value_scr[kt], grads)
            delta = delta_scr[t]
            ds = [
                (e[:QH] * (dp[:QH] - delta[0:1])).astype(BF),
                (e[QH:] * (dp[QH:] - delta[1:2])).astype(BF),
            ]
            ds = jnp.concatenate(ds, axis=0)
            parts.append((kt, mm(ds, queries), mm(e.astype(BF), grads)))
        for kt, gk, gv in parts:
            gk_scr[kt] += gk
            gv_scr[kt] += gv
        return carry

    lax.fori_loop(0, steps_of(items, STEP), step, 0)
    for t in range(NT):
        gk, gv = gk_scr[t], gv_scr[t]
        gk = (gk[:QH] + pltpu.roll(gk[QH:], hd, 1)) * hd ** (-0.5)
        gv = pltpu.roll(gv[:QH], hd, 1) + gv[QH:]
        out = jnp.where(first, gk, gv).astype(BF)
        for k in range(G):
            dkv_out[k][t * R : (t + 1) * R, :] = out[k * R : (k + 1) * R]


def place_pieces(cfg, hi, scr, pieces):
    w = pieces[0].shape[1]
    for k in range(cfg.G):
        at = pl.multiple_of((hi ^ k) * w, w)
        scr[:, pl.ds(at, w)] = pieces[k][...]


def out_kernel(cfg, meta, *refs):
    G = cfg.G
    wo, ao, part, attn = refs[G:]
    place_pieces(cfg, meta[0] // cfg.lo, attn, refs[:G])
    rows = attn[...]
    part[:, : cfg.D] = mm(rows, wo[...]).astype(BF)
    part[:, cfg.D :] = mm(rows, ao[...]).astype(BF)


def tiles_of(i, count):
    return [
        pl.ds(pl.multiple_of(i * (count * FFN_TILE) + j * FFN_TILE, FFN_TILE), FFN_TILE)
        for j in range(count)
    ]


def hidden_grad_kernel(cfg, meta, cot_ref, wd, bd, ad, out, turned):
    cot = cot_ref[...]
    side = (adapter_mask(cfg, meta) * mm_nt(cot, bd[...])).astype(BF)
    turned[...] = mm(side, slot_select(cfg, meta)).T.astype(BF)

    def part(i, carry):
        for at in tiles_of(i, FFN_STEP):
            out[:, at] = mm_nt(cot, wd[at, :]) + mm_nt(side, ad[at, :])
        return carry

    lax.fori_loop(0, cfg.F // (FFN_STEP * FFN_TILE), part, 0)


def ffn_kernel(
    cfg, units, meta, x_ref, own, other, bo, gain, wg, wu, bg, bu, ag, au, ad, cot_ref, gh, gst,
    mixed_ref, dfn_ref, hidden_scr, side_ref, oside, *refs,
):
    D, F = cfg.D, cfg.F
    chunks, (gg_scr, gu_scr, grads) = refs[: cfg.lo], refs[cfg.lo :]
    flip = meta[0] % cfg.lo
    mask = adapter_mask(cfg, meta)
    select = slot_select(cfg, meta)
    compact = lambda side: mm(side, select).T.astype(BF)
    total = own[...].astype(F32) + other[...].astype(F32)
    out_side = (mask * total[:, D:]).astype(BF)
    oside[...] = mm(out_side, select).astype(BF)
    mixed = x_ref[...].astype(F32) + total[:, :D] + mm(out_side, bo[...])
    mixed_ref[...] = mixed
    rr = lax.rsqrt(jnp.mean(mixed * mixed, axis=-1, keepdims=True) + norm_eps)
    normed = (mixed * rr * gain[...]).astype(BF)
    side_g = (mask * mm(normed, ag[...])).astype(BF)
    side_u = (mask * mm(normed, au[...])).astype(BF)
    turned = compact(side_g), compact(side_u), gst[...]

    def part(i, carry):
        for at in tiles_of(i, FFN_STEP):
            grad_hidden = gh[:, at]
            gate = mm(normed, wg[:, at]) + mm(side_g, bg[:, at])
            upper = mm(normed, wu[:, at]) + mm(side_u, bu[:, at])
            sigma = 1.0 / (1.0 + jnp.exp(-gate))
            silu = gate * sigma
            hidden_scr[:, at] = (silu * upper).astype(BF)
            gg_scr[:, at] = (grad_hidden * upper * (sigma + silu * (1.0 - sigma))).astype(BF)
            gu_scr[:, at] = (grad_hidden * silu).astype(BF)
        return carry

    lax.fori_loop(0, F // (FFN_STEP * FFN_TILE), part, 0)
    tile = FFN_TILE
    side_g = (mask * mm_nt(gg_scr[...], bg[...])).astype(BF)
    side_u = (mask * mm_nt(gu_scr[...], bu[...])).astype(BF)
    side_sum = mm(hidden_scr[...], ad[...])
    for d in range(0, D, tile):
        at = slice(d, d + tile)
        dfn = mm_nt(gg_scr[...], wg[at, :]) + mm_nt(gu_scr[...], wu[at, :])
        dfn_ref[:, at] = (dfn + mm_nt(side_g, ag[at, :]) + mm_nt(side_u, au[at, :])).astype(BF)
    side_ref[...] = side_sum.astype(BF)
    side_d = (mask * side_sum).astype(BF)
    for i, (side, right) in enumerate(((side_g, normed), (side_u, normed), (side_d, cot_ref[...]))):
        units.store(grads, 0, i, mm(compact(side), right).astype(BF))
    for i, right in enumerate((gg_scr, gu_scr, hidden_scr)):
        units.store(grads, 1, i, mm(turned[i], right[...]).astype(BF))
    units.clear_spare(grads)
    for j, chunk in enumerate(chunks):
        for half in range(2):
            chunk[half] = grads[2 * (j ^ flip) + half]


def ffn_call(cfg, units, meta, *ins):
    T, D, F, AW, S = cfg.T, cfg.D, cfg.F, cfg.AW, cfg.S
    return call(
        functools.partial(ffn_kernel, cfg, units),
        [((T, D), F32), ((T, D), BF), ((T, F), BF), ((T, AW), BF), ((T, S), BF)]
        + [((2, units.u, 16, 128), BF)] * cfg.lo,
        [meta, *ins],
        scratch=[pltpu.VMEM((T, F), BF)] * 2 + [pltpu.VMEM((units.n, units.u, 16, 128), BF)],
        us=14,
        name="ffn",
    )


def mixed_grad_kernel(cfg, meta, *refs):
    G, D = cfg.G, cfg.D
    mixed_ref, own, other, cot, gain = refs[:5]
    o_in = refs[5 : 5 + G]
    wo, ao, bo, oside = refs[5 + G : 9 + G]
    rest = refs[9 + G :]
    gm_ref, ograds, go_out, attn, go_scr, gm_scr = rest[0], rest[1], rest[2 : 2 + G], *rest[2 + G :]
    hi = meta[0] // cfg.lo
    mixed = mixed_ref[...]
    w = (own[...].astype(F32) + other[...].astype(F32)) * gain[...]
    rr = lax.rsqrt(jnp.mean(mixed * mixed, axis=-1, keepdims=True) + norm_eps)
    inner = jnp.mean(w * mixed, axis=-1, keepdims=True)
    gm = cot[...].astype(F32) + rr * w - (rr * rr * rr * inner) * mixed
    gm_ref[...] = gm
    gmb = gm.astype(BF)
    gm_scr[...] = gmb
    mask = adapter_mask(cfg, meta)
    select = slot_select(cfg, meta)
    grad_side = (mask * mm_nt(gmb, bo[...])).astype(BF)
    go = (mm_nt(gmb, wo[...]) + mm_nt(grad_side, ao[...])).astype(BF)
    w = cfg.groups * cfg.hd
    for h in range(G):
        go_scr[h] = go[:, h * w : (h + 1) * w]
    for k in range(G):
        go_out[k][...] = go_scr[hi ^ k]
    place_pieces(cfg, hi, attn, o_in)
    ograds[0] = mm(mm(grad_side, select).T.astype(BF), attn[...]).astype(BF)
    half = D // 2
    mine = gm_scr[:, pl.ds(pl.multiple_of(meta[1] * half, half), half)]
    ograds[1] = mm(oside[...].astype(F32).T.astype(BF), mine).astype(BF)


def down_kernel(cfg, meta, hidden, wd, side, part):
    part[:, : cfg.D] = mm(hidden[...], wd[...]).astype(BF)
    part[:, cfg.D :] = side[...]


def output_kernel(cfg, meta, mixed, own, other, bd, out_ref):
    D = cfg.D
    total = own[...].astype(F32) + other[...].astype(F32)
    side = (adapter_mask(cfg, meta) * total[:, D:]).astype(BF)
    out_ref[...] = (mixed[...] + total[:, :D] + mm(side, bd[...])).astype(BF)


def head_back(cfg, cos, sin, grad, raw, g):
    hd = cfg.hd
    copies = raw.shape[1] // hd
    per = raw.shape[1] // cos.shape[1]
    un = grad * lanes(cos[...], per) - swap_halves(grad, hd) * lanes(sin[...], per)
    w = un * lanes(g[...], copies)
    rr = lax.rsqrt(block_mean(raw * raw, hd) + norm_eps)
    return rr * w - rr * rr * rr * raw * block_mean(w * raw, hd)


def half_lanes(cfg, meta):
    half = cfg.D // 2
    keep = pl.ds(pl.multiple_of(meta[1] * half, half), half)
    send = pl.ds(pl.multiple_of((1 - meta[1]) * half, half), half)
    return keep, send


def query_back_kernel(cfg, meta, *refs):
    G, S = cfg.G, cfg.S
    normed, raw, sides, cos, sin, gain, w, a, b, part, bgrad, akeep, asend, dq_scr, a_scr = refs[G:]
    place_pieces(cfg, meta[0] // cfg.lo, dq_scr, refs[:G])
    g = head_back(cfg, cos, sin, dq_scr[...].astype(F32), raw[...], gain).astype(BF)
    select = slot_select(cfg, meta)
    grad_side = (adapter_mask(cfg, meta) * mm_nt(g, b[...])).astype(BF)
    part[...] = mm_nt(g, w[...]) + mm_nt(grad_side, a[...])
    a_scr[...] = mm(mm(grad_side, select).T.astype(BF), normed[...])
    bgrad[...] = mm(sides[0].astype(F32).T.astype(BF), g).astype(BF)
    keep, send = half_lanes(cfg, meta)
    akeep[...] = a_scr[:, keep].astype(BF)
    asend[...] = a_scr[:, send].astype(BF)


def key_value_side_kernel(cfg, meta, *refs):
    G, S, hd = cfg.G, cfg.S, cfg.hd
    dkv_in = refs[:G]
    normed, raw, cos, sin, gain, bk, bv, mine, got, *refs = refs[G:]
    grads, out_sides, akeep, asend, chunk, dkv_scr, a_scr = refs
    half_shared(meta, mine, got, chunk)
    place_pieces(cfg, meta[0] // cfg.lo, dkv_scr, dkv_in)
    mask = adapter_mask(cfg, meta)
    select = slot_select(cfg, meta)
    dkv = dkv_scr[...]
    dk = jnp.concatenate([dkv[:, 2 * h * hd : (2 * h + 1) * hd] for h in range(G)], axis=1)
    dv = jnp.concatenate([dkv[:, (2 * h + 1) * hd : (2 * h + 2) * hd] for h in range(G)], axis=1)
    gk = head_back(cfg, cos, sin, dk.astype(F32), raw[...], gain).astype(BF)
    for i, (g, b) in enumerate(((gk, bk), (dv, bv))):
        grad_side = (mask * mm_nt(g, b[...])).astype(BF)
        grads[i] = g
        out_sides[i] = grad_side
        a_scr[i * S : (i + 1) * S, :] = mm(mm(grad_side, select).T.astype(BF), normed[...])
    keep, send = half_lanes(cfg, meta)
    akeep[...] = a_scr[:, keep].astype(BF)
    asend[...] = a_scr[:, send].astype(BF)


def key_value_back_kernel(
    cfg, meta, grads, grad_sides, sides, wk, wv, ak, av, qpart, part, bgrad
):
    total = qpart[...]
    width = grads.shape[2]
    for i, (w, a) in enumerate(((wk, ak), (wv, av))):
        total = total + mm_nt(grads[i], w[...]) + mm_nt(grad_sides[i], a[...])
        bgrad[:, i * width : (i + 1) * width] = mm(
            sides[i].astype(F32).T.astype(BF), grads[i]
        ).astype(BF)
    part[...] = total.astype(BF)


def input_grad_kernel(cfg, meta, x_ref, gain, gm, own, other, out):
    x = x_ref[...].astype(F32)
    w = (own[...].astype(F32) + other[...].astype(F32)) * gain[...]
    rr = lax.rsqrt(jnp.mean(x * x, axis=-1, keepdims=True) + norm_eps)
    inner = jnp.mean(w * x, axis=-1, keepdims=True)
    out[...] = (gm[...] + rr * w - (rr * rr * rr * inner) * x).astype(BF)


class Units:
    def __init__(self, cfg, n, shared, private):
        self.n = n
        self.high = cfg.S // 16
        self.shared, self.private = shared, private
        self.us, self.up = self.per_chunk(shared), self.per_chunk(private)
        self.u = self.us + self.up

    def per_chunk(self, widths):
        return -(-sum(w // 128 for w in widths) * self.high // self.n)

    def places(self, which):
        widths, per, base = (
            (self.shared, self.us, 0) if which == 0 else (self.private, self.up, self.us)
        )
        at, out = 0, []
        for w in widths:
            spots = []
            for c in range(w // 128):
                for a in range(self.high):
                    spots.append((at // per, base + at % per, a, c))
                    at += 1
            out.append(spots)
        return out

    def spare(self):
        out = []
        for widths, per, base in ((self.shared, self.us, 0), (self.private, self.up, self.us)):
            count = sum(w // 128 for w in widths) * self.high
            out += [(i // per, base + i % per) for i in range(count, per * self.n)]
        return out

    def store(self, out, which, array, values, first=0):
        widths, per, base = (
            (self.shared, self.us, 0) if which == 0 else (self.private, self.up, self.us)
        )
        at = sum(w // 128 for w in widths[:array]) * self.high + first * self.high
        for c in range(values.shape[1] // 128):
            for a in range(self.high):
                unit = at + c * self.high + a
                out[unit // per, base + unit % per] = values[
                    a * 16 : a * 16 + 16, c * 128 : c * 128 + 128
                ]

    def clear_spare(self, out):
        for chunk, off in self.spare():
            out[chunk, off] = jnp.zeros((16, 128), BF)


def pack(units, scr, flip, outs, arrays):
    for i, values in enumerate(arrays):
        which = int(i >= len(units.shared))
        units.store(scr, which, i - which * len(units.shared), values)
    units.clear_spare(scr)
    for j, out in enumerate(outs):
        out[...] = scr[j ^ flip]


def add_halves(keep, got, count):
    total = (keep[...].astype(F32) + got[...].astype(F32)).astype(BF)
    rows = total.shape[0] // count
    return [total[i * rows : (i + 1) * rows] for i in range(count)]


def pack_qkv_kernel(cfg, units, meta, keep_q, got_q, keep, got, ograds, bq, bkv, *outs):
    scr, outs = outs[-1], outs[:-1]
    kw = bkv.shape[1] // 2
    shared = add_halves(keep_q, got_q, 1) + add_halves(keep, got, 2) + [ograds[1]]
    private = [ograds[0], bq[...], bkv[:, :kw], bkv[:, kw:]]
    pack(units, scr, meta[0] % cfg.lo, outs, shared + private)


def split_sum_kernel(cfg, meta, *refs):
    *terms, keep, send = refs
    bit = (meta[0] // cfg.lo) % 2
    for out, half in ((keep, bit), (send, 1 - bit)):
        total = terms[0][half].astype(F32)
        for term in terms[1:]:
            total = total + term[half].astype(F32)
        out[...] = total.astype(BF)


def sum_shared_kernel(meta, mine, got, out, shared):
    total = (mine[...].astype(F32) + got[...].astype(F32)).astype(BF)
    out[...] = total
    shared[...] = total[: shared.shape[0]]


def half_shared(meta, mine, got, out):
    count = got.shape[0]
    at = pl.ds(meta[1] * (count // 2), count // 2)
    out[: count // 2] = (mine[at].astype(F32) + got[at].astype(F32)).astype(BF)
    out[count // 2 :] = mine[count:]


def unpack(read, spots):
    cols = {}
    for chunk, off, a, c in spots:
        cols.setdefault(c, []).append(read(chunk, off))
    return jnp.concatenate([jnp.concatenate(cols[c], axis=0) for c in sorted(cols)], axis=1)


def expand_kernel(cfg, units, plan, halves, meta, *refs):
    own_in, other_in, outs = refs[: cfg.lo], refs[cfg.lo], refs[cfg.lo + 1 : -2]
    own, shared = refs[-2:]
    flip = meta[0] % cfg.lo
    wa = meta[1]
    count = shared.shape[2]
    for j in range(cfg.lo):
        if halves:
            if any(which == 1 for which, _, _ in plan):
                own[j ^ flip] = own_in[j][...]
            if any(which == 0 for which, _, _ in plan):
                shared[wa, j ^ flip] = own_in[j][:count]
                shared[1 - wa, j ^ flip] = other_in[j]
            continue
        for r in range(2):
            at = 2 * (j ^ flip) + (r ^ ((meta[0] // cfg.lo) % 2))
            own[at] = own_in[j][r]
            shared[wa, at] = own_in[j][r, :count]
            shared[1 - wa, at] = other_in[j, r]
    select = slot_select(cfg, meta)

    def write(out, values, transposed, at):
        width = values.shape[1]
        if transposed:
            out[at : at + width, :] = lax.dot_general(
                values, select, (((0,), (1,)), ((), ())), preferred_element_type=F32
            )
        else:
            out[:, at : at + width] = mm(select, values)

    for (which, i, transposed), out in zip(plan, outs):
        spots = units.places(which)[i]
        if which == 1:
            shift = 0 if halves else count
            write(out, unpack(lambda chunk, off: own[chunk, off - shift], spots), transposed, 0)
        elif halves:
            for w in range(2):
                values = unpack(lambda chunk, off: shared[w, chunk, off], spots)
                write(out, values, transposed, w * values.shape[1])
        else:
            values = unpack(lambda chunk, off: shared[off // count, chunk, off % count], spots)
            write(out, values, transposed, 0)


def upper_bits(cfg):
    bits, bit = [], cfg.n // 2
    while bit >= cfg.lo:
        bits.append(bit)
        bit //= 2
    return bits


def after(*values):
    return lax.optimization_barrier(values)


def swap_cores(value):
    return lax.ppermute(value, "wa", [(0, 1), (1, 0)])


def permute(cfg, value, bits):
    return lax.ppermute(value, "ctx", [(i, i ^ bits) for i in range(cfg.n)])


def per_device(
    hidden_in, attn_gain, query_weight, key_weight, value_weight, query_gain, key_gain, out_weight,
    ffn_gain, gate_weight, up_weight, down_weight, query_adapt_in, query_adapt_out, key_adapt_in,
    key_adapt_out, value_adapt_in, value_adapt_out, out_adapt_in, out_adapt_out, gate_adapt_in,
    gate_adapt_out, up_adapt_in, up_adapt_out, down_adapt_in, down_adapt_out, document_extra,
    document_adapter, cotangent,
):
    head_dim = query_gain.shape[0]
    cfg = Cfg(
        tokens=hidden_in.shape[0],
        n_ctx=lax.axis_size("ctx"),
        heads_kv=key_weight.shape[1] // head_dim,
        groups=query_weight.shape[1] // key_weight.shape[1],
        head_dim=head_dim,
        docs=document_extra.shape[0],
        adapt_width=query_adapt_in.shape[1],
        width=hidden_in.shape[2],
        hidden=gate_weight.shape[1],
    )
    T, D, G, S, AW, n, lo = cfg.T, cfg.D, cfg.G, cfg.S, cfg.AW, cfg.n, cfg.lo
    gw = cfg.groups * head_dim
    QW, KW = query_weight.shape[1], key_weight.shape[1]
    meta = (document_extra, document_adapter)
    x = hidden_in.reshape(T, D)
    cot = cotangent.reshape(T, D)
    gain_a = attn_gain.reshape(1, D)
    gain_f = ffn_gain.reshape(1, D)
    qg = query_gain.reshape(1, head_dim)
    kg = key_gain.reshape(1, head_dim)

    lane = np.arange(2 * head_dim) % (head_dim // 2)
    inverse = np.exp(lane * (-2.0 * math.log(theta_base) / head_dim)).astype(np.float32)[None, :]

    piece = ((T, gw), BF)
    fetched = [
        x, key_adapt_in, value_adapt_in, key_weight, key_adapt_out, value_weight, value_adapt_out,
    ]
    first = call(
        functools.partial(key_value_kernel, cfg),
        [piece] * G
        + [((T, KW), F32), ((2, T, S), BF), ((T, D), BF)]
        + [((T, 2 * head_dim), F32)] * 2,
        [meta, *fetched, gain_a, kg, inverse],
        scratch=[pltpu.VMEM(value.shape, value.dtype) for value in fetched]
        + [pltpu.SemaphoreType.DMA((len(fetched),)), pltpu.VMEM((G, T, 2 * head_dim), BF)],
        us=4,
        name="key_value",
        in_place=len(fetched),
        large=True,
    )
    kv_send = first[:G]
    kraw, sides, normed, cos, sin = first[G:]

    def to_heads(pieces):
        return [pieces[0]] + [permute(cfg, pieces[k], k * lo) for k in range(1, G)]

    def add(values):
        return sum(value.astype(F32) for value in values).astype(BF)

    def to_plane(value):
        return [value] + [permute(cfg, value, j) for j in range(1, lo)]

    kv_heads = to_heads(kv_send)
    second = call(
        functools.partial(query_kernel, cfg),
        [piece] * G + [((T, QW), F32), ((1, T, S), BF), items_shape(cfg)],
        [meta, normed, cos, sin, query_weight, query_adapt_in, query_adapt_out, qg],
        scratch=[pltpu.VMEM((G, T, gw), BF)],
        us=3,
        name="query",
        lists=1,
        large=True,
    )
    q_send, (qraw, side_q, items) = second[:G], second[G:]
    listed = (*meta, items)
    both = list(after(*kv_heads, *q_send))
    kv_heads, q_send = both[:G], both[G:]
    kv = to_plane(jnp.stack(kv_heads))
    q = to_heads(q_send)
    grad_hidden, gst = call(
        functools.partial(hidden_grad_kernel, cfg),
        [((T, cfg.F), F32), ((S, T), BF)],
        [meta, cot, down_weight, down_adapt_out, down_adapt_in],
        us=3,
        name="hidden_grad",
    )
    grad_hidden, *both = after(grad_hidden, *kv, *q)
    kv, q = both[:lo], both[lo:]
    tiles = lambda dtype, width=gw: pltpu.VMEM((cfg.NT, 2 * cfg.QH, width), dtype)
    attn = call(
        functools.partial(attend_kernel, cfg),
        [piece] * G + [((G, T, gw), BF), ((G, T, gw), F32)],
        [listed] + q + kv,
        scratch=[tiles(BF), tiles(F32)],
        us=12,
        name="attend",
    )
    o_send, o_all, linv = attn[:G], attn[G], attn[G + 1]
    o = to_heads(o_send)
    q_stack, _ = after(jnp.stack(q), o_send[0])
    q_plane = to_plane(q_stack)
    (opart,) = call(
        functools.partial(out_kernel, cfg),
        [((T, D + AW), BF)],
        [meta] + o + [out_weight, out_adapt_in],
        scratch=[pltpu.VMEM((T, QW), BF)],
        us=3,
        name="out_proj",
    )
    units_f = Units(cfg, 2 * lo, [D] * 3, [cfg.F] * 3)
    ffn = ffn_call(
        cfg, units_f, meta, x, opart, swap_cores(opart), out_adapt_out, gain_f, gate_weight, up_weight,
        gate_adapt_out, up_adapt_out, gate_adapt_in, up_adapt_in, down_adapt_in,
        cot, grad_hidden, gst,
    )
    mixed, dfn, hidden, dside, oside, *parts_f = ffn
    dfn, *q_plane = after(dfn, *q_plane)
    mg = call(
        functools.partial(mixed_grad_kernel, cfg),
        [((T, D), F32), ((2, S, D // 2), BF)] + [piece] * G,
        [meta, mixed, dfn, swap_cores(dfn), cot, gain_f]
        + o
        + [out_weight, out_adapt_in, out_adapt_out, oside],
        scratch=[pltpu.VMEM((T, QW), BF), pltpu.VMEM((G, T, gw), BF), pltpu.VMEM((T, D), BF)],
        us=0.01,
        name="mixed_grad",
    )
    grad_mixed, ograds, go_send = mg[0], mg[1], mg[2:]
    go_heads = to_heads(go_send)
    parts_f = [parts_f[0]] + [permute(cfg, parts_f[j], j) for j in range(1, lo)]
    message = G * T + -(-2 * cfg.groups * cfg.NT // 16) * 16
    (go_all,) = call(
        functools.partial(scale_kernel, cfg),
        [((message, gw), BF)],
        [meta] + go_heads + [linv, o_all],
        scratch=[
            pltpu.VMEM((cfg.NT, cfg.QH, gw), F32),
            pltpu.VMEM((cfg.groups * cfg.NT, gw), F32),
        ],
        us=0.01,
        name="scale",
    )
    go_all, *parts_f = after(go_all, *parts_f)
    sum_f, send_f = call(
        functools.partial(split_sum_kernel, cfg),
        [((units_f.u, 16, 128), BF)] * 2,
        [meta, *parts_f],
        us=0.01,
        name="split_sum",
    )
    go_plane = to_plane(go_all)
    dq_send = call(
        functools.partial(grad_query_kernel, cfg),
        [piece] * G,
        [listed] + q + kv + [go_all, o_all],
        scratch=[tiles(BF), tiles(BF), tiles(F32, 1), tiles(F32)],
        us=13.5,
        name="grad_query",
    )
    near, far = upper_bits(cfg)[1], upper_bits(cfg)[0]
    got_f, *dq_send = after(permute(cfg, send_f, near), *dq_send)
    sum_f = add([sum_f, got_f])
    dq = to_heads(dq_send)
    dkv_send = call(
        functools.partial(grad_key_kernel, cfg),
        [piece] * G,
        [listed, kv[0]] + q_plane + go_plane,
        scratch=[tiles(BF), tiles(BF), pltpu.VMEM((cfg.NT, 16, cfg.KT), F32), tiles(F32)]
        + [tiles(F32)],
        us=16,
        name="grad_key",
    )
    both = list(after(*dq, *dkv_send))
    dq, dkv_send = both[:G], both[G:]
    dkv = to_heads(dkv_send)
    qpart, bgrad_q, akeep_q, asend_q = call(
        functools.partial(query_back_kernel, cfg),
        [((T, D), F32), ((S, QW), BF), ((S, D // 2), BF), ((S, D // 2), BF)],
        [meta]
        + dq
        + [
            normed, qraw, side_q, cos, sin, qg, query_weight, query_adapt_in, query_adapt_out,
        ],
        scratch=[pltpu.VMEM((T, QW), BF), pltpu.VMEM((S, D), F32)],
        us=0.01,
        name="query_back",
    )
    got_f, qpart = after(permute(cfg, sum_f, far), qpart)
    sum_f, shared_f = call(
        sum_shared_kernel,
        [((units_f.u, 16, 128), BF), ((units_f.us, 16, 128), BF)],
        [meta, sum_f, got_f],
        us=0.01,
        name="sum_shared",
    )
    shared_f, qpart, *dkv = after(swap_cores(shared_f), qpart, *dkv)
    kv_grads, kv_sides, akeep_kv, asend_kv, sum_f = call(
        functools.partial(key_value_side_kernel, cfg),
        [((2, T, KW), BF), ((2, T, AW), BF), ((2 * S, D // 2), BF), ((2 * S, D // 2), BF)]
        + [((units_f.u - units_f.us // 2, 16, 128), BF)],
        [meta]
        + dkv
        + [normed, kraw, cos, sin, kg, key_adapt_out, value_adapt_out, sum_f, shared_f],
        scratch=[pltpu.VMEM((T, 2 * KW), BF), pltpu.VMEM((2 * S, D), F32)],
        us=0.01,
        name="key_value_side",
    )
    dnormed, bgrad_kv = call(
        functools.partial(key_value_back_kernel, cfg),
        [((T, D), BF), ((S, 2 * KW), BF)],
        [meta, kv_grads, kv_sides, sides, key_weight, value_weight, key_adapt_in, value_adapt_in]
        + [qpart],
        us=0.01,
        name="key_value_back",
    )

    def other_core(units, chunks, halves):
        shared = units.us if halves else units.us // 2
        return swap_cores(jnp.stack([chunk[..., :shared, :, :] for chunk in chunks]))

    def expand(units, chunks, theirs, plan, halves, outs, name):
        shared = units.us if halves else units.us // 2
        per = chunks[0].shape[-3]
        return call(
            functools.partial(expand_kernel, cfg, units, plan, halves),
            outs,
            [meta, *chunks, theirs],
            scratch=[
                pltpu.VMEM((units.n, per, 16, 128), BF),
                pltpu.VMEM((2, units.n, shared, 16, 128), BF),
            ],
            us=4,
            name=name,
        )

    units_q = Units(cfg, lo, [D // 2] * 4, [QW, QW, KW, KW])
    parts_q = call(
        functools.partial(pack_qkv_kernel, cfg, units_q),
        [((units_q.u, 16, 128), BF)] * lo,
        [meta, akeep_q, swap_cores(asend_q), akeep_kv, swap_cores(asend_kv), ograds, bgrad_q]
        + [bgrad_kv],
        scratch=[pltpu.VMEM((lo, units_q.u, 16, 128), BF)],
        us=0.01,
        name="pack_qkv",
    )
    dnormed, hidden, *parts_q = after(dnormed, hidden, *parts_q)
    (dpart,) = call(
        functools.partial(down_kernel, cfg),
        [((T, D + AW), BF)],
        [meta, hidden, down_weight, dside],
        us=3,
        name="down_proj",
    )
    dn_other = swap_cores(dnormed)
    near_f = permute(cfg, sum_f, near)
    sum_q = add([parts_q[0]] + [permute(cfg, parts_q[j], j) for j in range(1, lo)])
    sum_q, dn_other, dpart, sum_f, near_f = after(sum_q, dn_other, dpart, sum_f, near_f)
    all_f = to_plane(jnp.stack([sum_f, near_f]))
    (input_rows,) = call(
        functools.partial(input_grad_kernel, cfg),
        [((T, D), BF)],
        [meta, x, gain_a, grad_mixed, dnormed, dn_other],
        us=0.01,
        name="input_grad",
    )
    got_q, input_rows = after(permute(cfg, sum_q, near), input_rows)
    sum_q = add([sum_q, got_q])
    got_q, *all_f = after(permute(cfg, sum_q, far), *all_f)
    sum_q, dpart = after(add([sum_q, got_q]), dpart)
    pieces_q = to_plane(sum_q)
    (out_rows,) = call(
        functools.partial(output_kernel, cfg),
        [((T, D), BF)],
        [meta, mixed, dpart, swap_cores(dpart), down_adapt_out],
        us=0.01,
        name="output",
    )
    gate_in, up_in, down_out, gate_out, up_out, down_in = expand(
        units_f,
        all_f,
        other_core(units_f, all_f, False),
        [(0, 0, True), (0, 1, True), (0, 2, False), (1, 0, False), (1, 1, False), (1, 2, True)],
        False,
        [((D, AW), F32), ((D, AW), F32), ((AW, D), F32)]
        + [((AW, cfg.F), F32), ((AW, cfg.F), F32), ((cfg.F, AW), F32)],
        "expand_ffn",
    )
    down_out, out_rows, *pieces_q = after(down_out, out_rows, *pieces_q)
    theirs_q = other_core(units_q, pieces_q, True)
    out_in, query_out, key_out, value_out = expand(
        units_q,
        pieces_q,
        parts_q[0].reshape(1, units_q.u, 16, 128),
        [(1, 0, True), (1, 1, False), (1, 2, False), (1, 3, False)],
        True,
        [((QW, AW), F32), ((AW, QW), F32), ((AW, KW), F32), ((AW, KW), F32)],
        "expand_own",
    )
    theirs_q, out_in = after(theirs_q, out_in)
    query_in, key_in, value_in, out_out = expand(
        units_q,
        pieces_q,
        theirs_q,
        [(0, 0, True), (0, 1, True), (0, 2, True), (0, 3, False)],
        True,
        [((D, AW), F32)] * 3 + [((AW, D), F32)],
        "expand_qkv",
    )
    return (
        out_rows.reshape(T, 1, D),
        input_rows.reshape(T, 1, D),
        query_in,
        query_out,
        key_in,
        key_out,
        value_in,
        value_out,
        out_in,
        out_out,
        gate_in,
        gate_out,
        up_in,
        up_out,
        down_in,
        down_out,
    )


def solution(mesh):
    return jax.shard_map(
        per_device,
        mesh=mesh,
        in_specs=(
            P(None, "ctx", None), P(), P(None, "wa"), P(None, "wa"), P(None, "wa"), P(), P(),
            P("wa", None), P(), P(None, "wa"), P(None, "wa"), P("wa", None), P(), P(None, "wa"),
            P(), P(None, "wa"), P(), P(None, "wa"), P("wa", None), P(), P(), P(None, "wa"), P(),
            P(None, "wa"), P("wa", None), P(), P(), P(), P(None, "ctx", None),
        ),
        out_specs=(
            P(None, "ctx", None), P(None, "ctx", None), P(), P(None, "wa"), P(), P(None, "wa"), P(),
            P(None, "wa"), P("wa", None), P(), P(), P(None, "wa"), P(), P(None, "wa"),
            P("wa", None), P(),
        ),
        check_vma=False,
    )
```

```python
import functools
import math

import jax
import jax.numpy as jnp
import numpy as np
from jax import lax
from jax.experimental import pallas as pl
from jax.experimental.pallas import tpu as pltpu
from jax.sharding import PartitionSpec as P

RANK = 16
DOC_MIN = 200

norm_eps = 1e-05
theta_base = 1000000.0
BF = jnp.bfloat16
F32 = jnp.float32
LOG2E = 1.4426950408889634
STEP, STEP_QUERY = 11, 11
FFN_TILE, FFN_STEP = 256, 3
VMEM_SMALL = 28 * 1024 * 1024
VMEM_LARGE = 56 * 1024 * 1024


def mm(left, right):
    return jnp.dot(left, right, preferred_element_type=F32)


def mm_nt(left, right):
    return lax.dot_general(left, right, (((1,), (1,)), ((), ())), preferred_element_type=F32)


def mm_tn(left, right):
    return lax.dot_general(left, right, (((0,), (0,)), ((), ())), preferred_element_type=F32)


def iota(shape, dim):
    return lax.broadcasted_iota(jnp.int32, shape, dim)


class Cfg:
    def __init__(self, tokens, n_ctx, heads_kv, groups, head_dim, docs, adapt_width, width, hidden):
        self.T = tokens
        self.n = n_ctx
        self.G = heads_kv
        self.lo = n_ctx // heads_kv
        self.groups = groups
        self.hd = head_dim
        self.docs = docs
        self.AW = adapt_width
        self.slots = min(docs, adapt_width // RANK)
        self.S = self.slots * RANK
        self.D = width
        self.F = hidden
        self.R = max(16, min(tokens, 512 // n_ctx))
        self.NT = tokens // self.R
        self.span = self.R * n_ctx
        self.QH = self.G * self.R
        self.KT = n_ctx * self.R


class Meta:
    def __init__(self, extra, adapter, items=None):
        self.refs, self.docs, self.items = (extra, adapter), extra.shape[0], items

    def __getitem__(self, i):
        if i < 2:
            return lax.axis_index(("ctx", "wa")[i])
        return self.refs[(i - 2) // self.docs][(i - 2) % self.docs]


def with_meta(kernel, count):
    return lambda *refs: kernel(Meta(*refs[:count]), *refs[count:])


def doc_starts(cfg, meta):
    out = [jnp.int32(0)]
    for j in range(cfg.docs):
        out.append(out[-1] + meta[2 + j] + (DOC_MIN - 1))
    return out


def start_of(starts, token):
    out = jnp.zeros_like(token)
    for s in starts[1:-1]:
        out = jnp.where(token >= s, s, out)
    return out


def end_of(starts, token):
    out = starts[1]
    for j in range(1, len(starts) - 1):
        out = jnp.where(token >= starts[j], starts[j + 1], out)
    return out


def adapter_mask(cfg, meta):
    token = iota((cfg.T, cfg.AW), 0) * cfg.n + meta[0]
    starts = doc_starts(cfg, meta)
    adapter = jnp.full((cfg.T, cfg.AW), meta[2 + cfg.docs], jnp.int32)
    for j in range(1, cfg.docs):
        adapter = jnp.where(token >= starts[j], meta[2 + cfg.docs + j], adapter)
    return (adapter == iota((cfg.T, cfg.AW), 1) // RANK).astype(F32)


def slot_select(cfg, meta):
    row = iota((cfg.AW, cfg.S), 0)
    col = iota((cfg.AW, cfg.S), 1)
    if cfg.S == cfg.AW:
        return (row == col).astype(BF)
    target = jnp.full((cfg.AW, cfg.S), -1, jnp.int32)
    for s in range(cfg.slots):
        mine = meta[2 + cfg.docs + s]
        again = jnp.int32(0)
        for e in range(s):
            again = jnp.where(meta[2 + cfg.docs + e] == mine, 1, again)
        base = jnp.where(again == 1, -4 * cfg.AW, mine * RANK)
        target = jnp.where(col // RANK == s, base + col % RANK, target)
    return (row == target).astype(BF)


def block_mean(values, hd):
    part = min(values.shape[1], 256)
    ones = (iota((part, part), 0) // hd == iota((part, part), 1) // hd).astype(BF)
    out = []
    for at in range(0, values.shape[1], part):
        piece = values[:, at : at + part]
        high = piece.astype(BF)
        low = (piece - high.astype(F32)).astype(BF)
        out.append((mm(high, ones) + mm(low, ones)) * (1.0 / hd))
    return jnp.concatenate(out, axis=1)


def swap_halves(values, hd):
    width = values.shape[1]
    half = hd // 2
    first = iota(values.shape, 1) % hd < half
    return jnp.where(first, pltpu.roll(values, width - half, 1), pltpu.roll(values, half, 1))


def lanes(values, copies):
    return jnp.concatenate([values] * copies, axis=1) if copies > 1 else values


def params(large=False, **kw):
    limit = VMEM_SMALL if lax.axis_size("ctx") <= 16 and not large else VMEM_LARGE
    return pltpu.CompilerParams(vmem_limit_bytes=limit, **kw)


SMEM = pl.BlockSpec(memory_space=pltpu.SMEM)


def cost(us):
    return pl.CostEstimate(flops=int(us * 1.15e9), bytes_accessed=0, transcendentals=0)


def call(kernel, outs, ins, scratch=(), us=1.0, name=None, large=False, in_place=0, lists=0):
    count = len(ins[0])
    ins = [*ins[0], *ins[1:]]
    return pl.pallas_call(
        with_meta(kernel, count),
        out_shape=[jax.ShapeDtypeStruct(s, d) for s, d in outs],
        in_specs=[SMEM] * count
        + [pl.BlockSpec(memory_space=pl.ANY)] * in_place
        + [pl.BlockSpec(memory_space=pltpu.VMEM)] * (len(ins) - count - in_place),
        out_specs=[pl.BlockSpec(memory_space=pltpu.VMEM)] * (len(outs) - lists) + [SMEM] * lists,
        scratch_shapes=list(scratch),
        compiler_params=params(large),
        cost_estimate=cost(us),
        name=name,
    )(*ins)


def head_prep(cfg, cos, sin, raw, g):
    hd = cfg.hd
    copies = raw.shape[1] // hd
    scaled = raw * lax.rsqrt(block_mean(raw * raw, hd) + norm_eps) * lanes(g[...], copies)
    per = raw.shape[1] // cos.shape[1]
    return scaled * lanes(cos[...], per) + swap_halves(scaled, hd) * lanes(sin[...], per)


def rotation(cfg, meta, inverse, cos, sin):
    width, half = 2 * cfg.hd, cfg.hd // 2
    blocks = width // half
    rows = cfg.T // blocks
    lane = iota((rows, width), 1)
    token = ((lane // half) * rows + iota((rows, width), 0)) * cfg.n + meta[0]
    angle = (token - start_of(doc_starts(cfg, meta), token)).astype(F32) * inverse[...]
    sign = jnp.where(lane % cfg.hd < half, -1.0, 1.0)
    for out, values, scale in ((cos, jnp.cos(angle), None), (sin, jnp.sin(angle), sign)):
        for b in range(blocks):
            part = pltpu.roll(values, width - b * half, 1) if b else values
            part = jnp.where(lane < half, part, 0.0)
            size = half
            while size < width:
                part = part + pltpu.roll(part, size, 1)
                size *= 2
            out[b * rows : (b + 1) * rows, :] = part if scale is None else part * scale


def key_value_kernel(cfg, meta, *refs):
    G, hd = cfg.G, cfg.hd
    sources, (gain, kg, inverse), refs = refs[:7], refs[7:10], refs[10:]
    kv_out, refs = refs[:G], refs[G:]
    raw_ref, sides_ref, normed_ref, cos, sin, *scratch = refs
    buffers, sems, kv_scr = scratch[:7], scratch[7], scratch[8]
    copies = [
        pltpu.make_async_copy(source, buffer, sems.at[i])
        for i, (source, buffer) in enumerate(zip(sources, buffers))
    ]
    for copy in copies:
        copy.start()
    x_buf, ak, av, wk, bk, wv, bv = buffers
    rotation(cfg, meta, inverse, cos, sin)
    mask = adapter_mask(cfg, meta)
    select = slot_select(cfg, meta)
    copies[0].wait()
    x = x_buf[...].astype(F32)
    rr = lax.rsqrt(jnp.mean(x * x, axis=-1, keepdims=True) + norm_eps)
    normed = (x * rr * gain[...]).astype(BF)
    normed_ref[...] = normed
    for copy in copies[1:]:
        copy.wait()
    raws = []
    for i, (w, a, b) in enumerate(((wk, ak, bk), (wv, av, bv))):
        side = (mask * mm(normed, a[...])).astype(BF)
        sides_ref[i] = mm(side, select).astype(BF)
        raws.append(mm(normed, w[...]) + mm(side, b[...]))
    kraw, vraw = raws
    raw_ref[...] = kraw
    key = head_prep(cfg, cos, sin, kraw, kg).astype(BF)
    value = vraw.astype(BF)
    for h in range(G):
        at = slice(h * hd, (h + 1) * hd)
        kv_scr[h] = jnp.concatenate([key[:, at], value[:, at]], axis=1)
    hi = meta[0] // cfg.lo
    for k in range(G):
        kv_out[k][...] = kv_scr[hi ^ k]


def query_kernel(cfg, meta, normed_ref, cos, sin, w, a, b, g, *refs):
    G = cfg.G
    q_out, raw_ref, side_ref, items, q_scr = refs[:G], *refs[G:]
    list_items(cfg, doc_starts(cfg, meta), items)
    normed = normed_ref[...]
    side = (adapter_mask(cfg, meta) * mm(normed, a[...])).astype(BF)
    side_ref[0] = mm(side, slot_select(cfg, meta)).astype(BF)
    raw = mm(normed, w[...]) + mm(side, b[...])
    raw_ref[...] = raw
    query = head_prep(cfg, cos, sin, raw, g).astype(BF)
    gw = cfg.groups * cfg.hd
    for h in range(G):
        q_scr[h] = query[:, h * gw : (h + 1) * gw]
    hi = meta[0] // cfg.lo
    for k in range(G):
        q_out[k][...] = q_scr[hi ^ k]


def tile_of(cfg, pieces, t):
    rows = pl.ds(pl.multiple_of(t * cfg.R, cfg.R), cfg.R)
    return jnp.concatenate([piece[rows, :] for piece in pieces], axis=0)


def list_items(cfg, starts, items):
    def per_query(qt, count):
        def one(s, at):
            items[0, at] = qt
            items[1, at] = s
            return at + 1

        return lax.fori_loop(start_of(starts, qt * cfg.span) // cfg.span, qt + 1, one, count)

    count = lax.fori_loop(0, cfg.NT, per_query, 0)
    for i in range(STEP - 1):
        items[0, count + i] = 0
        items[1, count + i] = cfg.NT - 1
    items[0, items.shape[1] - 1] = count


def steps_of(items, step):
    return (items[0, items.shape[1] - 1] + step - 1) // step


def items_shape(cfg):
    return ((2, cfg.NT * (cfg.NT + 1) // 2 + STEP), jnp.int32)


def split_pieces(ref, count):
    return [ref.at[i] for i in range(count)]


def message_pieces(cfg, ref):
    return [ref.at[pl.ds(k * cfg.T, cfg.T)] for k in range(cfg.G)]


def token_in_span(cfg, meta, index):
    hi, lo = meta[0] // cfg.lo, meta[0] % cfg.lo
    piece, row = index // cfg.R, index % cfg.R
    j, k = piece // cfg.G, piece % cfg.G
    return row * cfg.n + (hi ^ k) * cfg.lo + (lo ^ j)


def pad_queries(cfg, qq, side):
    hd = cfg.hd
    wide = qq.astype(F32)
    first = iota(wide.shape, 1) < hd
    rolled = pltpu.roll(wide, hd, 1)
    if side == 0:
        parts = [jnp.where(first, wide, 0.0), jnp.where(first, rolled, 0.0)]
    else:
        parts = [jnp.where(first, 0.0, rolled), jnp.where(first, 0.0, wide)]
    return jnp.concatenate(parts, axis=0).astype(BF)


def attend_kernel(cfg, meta, *refs):
    G, R, hd, QH = cfg.G, cfg.R, cfg.hd, cfg.QH
    q_in, own, others = refs[:G], refs[G], refs[G + 1 : G + cfg.lo]
    rest = refs[G + cfg.lo :]
    o_out, o_all, linv, q_scr, acc_scr, first_scr = rest[:G], *rest[G:]
    kv_pieces = split_pieces(own, G)
    for ref in others:
        kv_pieces = kv_pieces + split_pieces(ref, G)
    starts = doc_starts(cfg, meta)
    items = meta.items
    scale = hd ** (-0.5) * LOG2E
    key_off = token_in_span(cfg, meta, iota((1, cfg.KT), 1))
    row_off = token_in_span(cfg, meta, iota((2 * QH, 1), 0) % QH)
    key_lanes = iota((cfg.KT, 2 * hd), 1) < hd
    for t in range(cfg.NT):
        q_scr[t] = pad_queries(cfg, tile_of(cfg, q_in, t), 0)
        acc_scr[t] = jnp.zeros((2 * QH, 2 * hd), F32)
        first_scr[t] = start_of(starts, row_off + t * cfg.span)

    def step(i, carry):
        parts = []
        for u in range(STEP):
            qt, s = items[0, i * STEP + u], items[1, i * STEP + u]
            kv = tile_of(cfg, kv_pieces, s)
            token = row_off + qt * cfg.span
            key_token = key_off + s * cfg.span
            e = jnp.exp2(mm_nt(q_scr[qt], kv) * scale)
            e = jnp.where((key_token <= token) & (key_token >= first_scr[qt]), e, 0.0)
            parts.append((qt, mm(e.astype(BF), jnp.where(key_lanes, jnp.ones_like(kv), kv))))
        for qt, part in parts:
            acc_scr[qt] += part
        return carry

    lax.fori_loop(0, steps_of(items, STEP), step, 0)
    half = iota((QH, 2 * hd), 1) < hd
    for t in range(cfg.NT):
        acc = acc_scr[t]
        inv0 = 1.0 / acc[:QH]
        inv1 = 1.0 / acc[QH:]
        out0 = pltpu.roll(acc[:QH], hd, 1) * inv0
        out1 = acc[QH:] * pltpu.roll(inv1, hd, 1)
        out = jnp.where(half, out0, out1).astype(BF)
        inv = jnp.where(half, inv0, pltpu.roll(inv1, hd, 1))
        rows = slice(t * R, (t + 1) * R)
        for k in range(G):
            o_out[k][rows, :] = out[k * R : (k + 1) * R]
            o_all[k, rows, :] = out[k * R : (k + 1) * R]
            linv[k, rows, :] = inv[k * R : (k + 1) * R]


def head_sums(cfg, prod):
    pick = (iota((16, prod.shape[1]), 1) // cfg.hd == iota((16, prod.shape[1]), 0)).astype(BF)
    high = prod.astype(BF)
    low = (prod - high.astype(F32)).astype(BF)
    return mm_nt(pick, high) + mm_nt(pick, low)


def scale_kernel(cfg, meta, *refs):
    G, T, R, NT, QH = cfg.G, cfg.T, cfg.R, cfg.NT, cfg.QH
    go, linv, o_all, out, scr, delta = refs[:G], refs[G], refs[G + 1], refs[G + 2], *refs[G + 3 :]
    delta[...] = jnp.zeros_like(delta)
    for k in range(G):
        scaled = (go[k][...].astype(F32) * linv[k]).astype(BF)
        out[k * T : (k + 1) * T, :] = scaled
        prod = scaled.astype(F32) * o_all[k].astype(F32)
        for t in range(NT):
            scr[t, k * R : (k + 1) * R, :] = prod[t * R : (t + 1) * R]
    for t in range(NT):
        sums = head_sums(cfg, scr[t])
        for h in range(cfg.groups):
            delta[h * NT + t : h * NT + t + 1, :QH] = sums[h : h + 1]
    high = delta[...].astype(BF)
    at = G * T
    rows = cfg.groups * NT
    out[at : at + rows, :] = high
    out[at + rows : at + 2 * rows, :] = (delta[...] - high.astype(F32)).astype(BF)


def grad_query_kernel(cfg, meta, *refs):
    G, R, hd, QH = cfg.G, cfg.R, cfg.hd, cfg.QH
    q_in, own, others = refs[:G], refs[G], refs[G + 1 : G + cfg.lo]
    go_ref, o_ref = refs[G + cfg.lo : G + cfg.lo + 2]
    rest = refs[G + cfg.lo + 2 :]
    dq_out, q_scr, go_scr, delta_scr, acc_scr, first_scr = rest[:G], *rest[G:]
    kv_pieces = split_pieces(own, G)
    for ref in others:
        kv_pieces = kv_pieces + split_pieces(ref, G)
    starts = doc_starts(cfg, meta)
    items = meta.items
    scale = hd ** (-0.5) * LOG2E
    key_off = token_in_span(cfg, meta, iota((1, cfg.KT), 1))
    row_off = token_in_span(cfg, meta, iota((2 * QH, 1), 0) % QH)
    half = iota((QH, 2 * hd), 1) < hd
    for t in range(cfg.NT):
        go = tile_of(cfg, message_pieces(cfg, go_ref), t)
        prod = go.astype(F32) * tile_of(cfg, split_pieces(o_ref, G), t).astype(F32)
        q_scr[t] = pad_queries(cfg, tile_of(cfg, q_in, t), 0)
        go_scr[t] = pad_queries(cfg, go, 1)
        delta_scr[t, :QH] = jnp.sum(jnp.where(half, prod, 0.0), axis=1, keepdims=True)
        delta_scr[t, QH:] = jnp.sum(jnp.where(half, 0.0, prod), axis=1, keepdims=True)
        acc_scr[t] = jnp.zeros((2 * QH, 2 * hd), F32)
        first_scr[t] = start_of(starts, row_off + t * cfg.span)

    def step(i, carry):
        parts = []
        for u in range(STEP_QUERY):
            qt, s = items[0, i * STEP_QUERY + u], items[1, i * STEP_QUERY + u]
            kv = tile_of(cfg, kv_pieces, s)
            token = row_off + qt * cfg.span
            key_token = key_off + s * cfg.span
            e = jnp.exp2(mm_nt(q_scr[qt], kv) * scale)
            ds = e * (mm_nt(go_scr[qt], kv) - delta_scr[qt])
            ds = jnp.where((key_token <= token) & (key_token >= first_scr[qt]), ds, 0.0)
            parts.append((qt, mm(ds.astype(BF), kv)))
        for qt, part in parts:
            acc_scr[qt] += part
        return carry

    lax.fori_loop(0, steps_of(items, STEP_QUERY), step, 0)
    for t in range(cfg.NT):
        acc = acc_scr[t]
        out = jnp.where(half, acc[:QH], pltpu.roll(acc[QH:], hd, 1)) * hd ** (-0.5)
        out = out.astype(BF)
        for k in range(G):
            dq_out[k][t * R : (t + 1) * R, :] = out[k * R : (k + 1) * R]


def grad_key_kernel(cfg, meta, *refs):
    G, T, R, hd, lo, QH, NT = cfg.G, cfg.T, cfg.R, cfg.hd, cfg.lo, cfg.QH, cfg.NT
    own = refs[0]
    q_refs, go_refs = (refs[1 + i * lo : 1 + (i + 1) * lo] for i in range(2))
    rest = refs[1 + 2 * lo :]
    dkv_out, key_scr, value_scr, delta_scr, gk_scr, gv_scr = rest[:G], *rest[G:]
    q_pieces = [piece for ref in q_refs for piece in split_pieces(ref, G)]
    go_pieces = [piece for ref in go_refs for piece in message_pieces(cfg, ref)]
    starts = doc_starts(cfg, meta)
    items = meta.items
    scale = hd ** (-0.5) * LOG2E
    rows = cfg.groups * NT
    for j in range(lo):
        sums = go_refs[j][G * T : G * T + 2 * rows, :].astype(F32)
        sums = sums[:rows] + sums[rows:]
        for t in range(NT):
            for h in range(cfg.groups):
                at = h * NT + t
                delta_scr[t, h : h + 1, j * QH : (j + 1) * QH] = sums[at : at + 1, :QH]
    query_off = token_in_span(cfg, meta, iota((1, cfg.KT), 1))
    row_off = token_in_span(cfg, meta, iota((2 * QH, 1), 0) % QH)
    first = iota((QH, 2 * hd), 1) < hd
    for t in range(NT):
        kv = tile_of(cfg, split_pieces(own, G), t).astype(F32)
        rolled = pltpu.roll(kv, hd, 1)
        keys = [jnp.where(first, kv, 0.0), jnp.where(first, 0.0, rolled)]
        values = [jnp.where(first, rolled, 0.0), jnp.where(first, 0.0, kv)]
        key_scr[t] = jnp.concatenate(keys, axis=0).astype(BF)
        value_scr[t] = jnp.concatenate(values, axis=0).astype(BF)
        gk_scr[t] = jnp.zeros((2 * QH, 2 * hd), F32)
        gv_scr[t] = jnp.zeros((2 * QH, 2 * hd), F32)

    def step(i, carry):
        parts = []
        for u in range(STEP):
            t, kt = items[0, i * STEP + u], items[1, i * STEP + u]
            queries, grads = tile_of(cfg, q_pieces, t), tile_of(cfg, go_pieces, t)
            key_token = row_off + kt * cfg.span
            token = query_off + t * cfg.span
            e = jnp.exp2(mm_nt(key_scr[kt], queries) * scale)
            e = jnp.where((key_token <= token) & (key_token >= start_of(starts, token)), e, 0.0)
            dp = mm_nt(value_scr[kt], grads)
            delta = delta_scr[t]
            ds = [
                (e[:QH] * (dp[:QH] - delta[0:1])).astype(BF),
                (e[QH:] * (dp[QH:] - delta[1:2])).astype(BF),
            ]
            ds = jnp.concatenate(ds, axis=0)
            parts.append((kt, mm(ds, queries), mm(e.astype(BF), grads)))
        for kt, gk, gv in parts:
            gk_scr[kt] += gk
            gv_scr[kt] += gv
        return carry

    lax.fori_loop(0, steps_of(items, STEP), step, 0)
    for t in range(NT):
        gk, gv = gk_scr[t], gv_scr[t]
        gk = (gk[:QH] + pltpu.roll(gk[QH:], hd, 1)) * hd ** (-0.5)
        gv = pltpu.roll(gv[:QH], hd, 1) + gv[QH:]
        out = jnp.where(first, gk, gv).astype(BF)
        for k in range(G):
            dkv_out[k][t * R : (t + 1) * R, :] = out[k * R : (k + 1) * R]


def place_pieces(cfg, hi, scr, pieces):
    w = pieces[0].shape[1]
    for k in range(cfg.G):
        at = pl.multiple_of((hi ^ k) * w, w)
        scr[:, pl.ds(at, w)] = pieces[k][...]


def out_kernel(cfg, meta, *refs):
    G = cfg.G
    wo, ao, part, attn = refs[G:]
    place_pieces(cfg, meta[0] // cfg.lo, attn, refs[:G])
    rows = attn[...]
    part[:, : cfg.D] = mm(rows, wo[...]).astype(BF)
    part[:, cfg.D :] = mm(rows, ao[...]).astype(BF)


def tiles_of(i, count):
    return [
        pl.ds(pl.multiple_of(i * (count * FFN_TILE) + j * FFN_TILE, FFN_TILE), FFN_TILE)
        for j in range(count)
    ]


def hidden_grad_kernel(cfg, meta, cot_ref, wd, bd, ad, out, turned):
    cot = cot_ref[...]
    side = (adapter_mask(cfg, meta) * mm_nt(cot, bd[...])).astype(BF)
    turned[...] = mm(side, slot_select(cfg, meta)).T.astype(BF)

    def part(i, carry):
        for at in tiles_of(i, FFN_STEP):
            out[:, at] = mm_nt(cot, wd[at, :]) + mm_nt(side, ad[at, :])
        return carry

    lax.fori_loop(0, cfg.F // (FFN_STEP * FFN_TILE), part, 0)


def ffn_kernel(
    cfg, units, meta, x_ref, own, other, bo, gain, wg, wu, bg, bu, ag, au, ad, cot_ref, gh, gst,
    mixed_ref, dfn_ref, hidden_scr, side_ref, oside, *refs,
):
    D, F = cfg.D, cfg.F
    chunks, (gg_scr, gu_scr, grads) = refs[: cfg.lo], refs[cfg.lo :]
    flip = meta[0] % cfg.lo
    mask = adapter_mask(cfg, meta)
    select = slot_select(cfg, meta)
    compact = lambda side: mm(side, select).T.astype(BF)
    total = own[...].astype(F32) + other[...].astype(F32)
    out_side = (mask * total[:, D:]).astype(BF)
    oside[...] = mm(out_side, select).astype(BF)
    mixed = x_ref[...].astype(F32) + total[:, :D] + mm(out_side, bo[...])
    mixed_ref[...] = mixed
    rr = lax.rsqrt(jnp.mean(mixed * mixed, axis=-1, keepdims=True) + norm_eps)
    normed = (mixed * rr * gain[...]).astype(BF)
    side_g = (mask * mm(normed, ag[...])).astype(BF)
    side_u = (mask * mm(normed, au[...])).astype(BF)
    turned = compact(side_g), compact(side_u), gst[...]

    def part(i, carry):
        for at in tiles_of(i, FFN_STEP):
            grad_hidden = gh[:, at]
            gate = mm(normed, wg[:, at]) + mm(side_g, bg[:, at])
            upper = mm(normed, wu[:, at]) + mm(side_u, bu[:, at])
            sigma = 1.0 / (1.0 + jnp.exp(-gate))
            silu = gate * sigma
            hidden_scr[:, at] = (silu * upper).astype(BF)
            gg_scr[:, at] = (grad_hidden * upper * (sigma + silu * (1.0 - sigma))).astype(BF)
            gu_scr[:, at] = (grad_hidden * silu).astype(BF)
        return carry

    lax.fori_loop(0, F // (FFN_STEP * FFN_TILE), part, 0)
    tile = FFN_TILE
    side_g = (mask * mm_nt(gg_scr[...], bg[...])).astype(BF)
    side_u = (mask * mm_nt(gu_scr[...], bu[...])).astype(BF)
    side_sum = mm(hidden_scr[...], ad[...])
    for d in range(0, D, tile):
        at = slice(d, d + tile)
        dfn = mm_nt(gg_scr[...], wg[at, :]) + mm_nt(gu_scr[...], wu[at, :])
        dfn_ref[:, at] = (dfn + mm_nt(side_g, ag[at, :]) + mm_nt(side_u, au[at, :])).astype(BF)
    side_ref[...] = side_sum.astype(BF)
    side_d = (mask * side_sum).astype(BF)
    for i, (side, right) in enumerate(((side_g, normed), (side_u, normed), (side_d, cot_ref[...]))):
        units.store(grads, 0, i, mm(compact(side), right).astype(BF))
    for i, right in enumerate((gg_scr, gu_scr, hidden_scr)):
        units.store(grads, 1, i, mm(turned[i], right[...]).astype(BF))
    units.clear_spare(grads)
    for j, chunk in enumerate(chunks):
        for half in range(2):
            chunk[half] = grads[2 * (j ^ flip) + half]


def ffn_call(cfg, units, meta, *ins):
    T, D, F, AW, S = cfg.T, cfg.D, cfg.F, cfg.AW, cfg.S
    return call(
        functools.partial(ffn_kernel, cfg, units),
        [((T, D), F32), ((T, D), BF), ((T, F), BF), ((T, AW), BF), ((T, S), BF)]
        + [((2, units.u, 16, 128), BF)] * cfg.lo,
        [meta, *ins],
        scratch=[pltpu.VMEM((T, F), BF)] * 2 + [pltpu.VMEM((units.n, units.u, 16, 128), BF)],
        us=14,
        name="ffn",
    )


def mixed_grad_kernel(cfg, meta, *refs):
    G, D = cfg.G, cfg.D
    mixed_ref, own, other, cot, gain = refs[:5]
    o_in = refs[5 : 5 + G]
    wo, ao, bo, oside = refs[5 + G : 9 + G]
    rest = refs[9 + G :]
    gm_ref, ograds, go_out, attn, go_scr, gm_scr = rest[0], rest[1], rest[2 : 2 + G], *rest[2 + G :]
    hi = meta[0] // cfg.lo
    mixed = mixed_ref[...]
    w = (own[...].astype(F32) + other[...].astype(F32)) * gain[...]
    rr = lax.rsqrt(jnp.mean(mixed * mixed, axis=-1, keepdims=True) + norm_eps)
    inner = jnp.mean(w * mixed, axis=-1, keepdims=True)
    gm = cot[...].astype(F32) + rr * w - (rr * rr * rr * inner) * mixed
    gm_ref[...] = gm
    gmb = gm.astype(BF)
    gm_scr[...] = gmb
    mask = adapter_mask(cfg, meta)
    select = slot_select(cfg, meta)
    grad_side = (mask * mm_nt(gmb, bo[...])).astype(BF)
    go = (mm_nt(gmb, wo[...]) + mm_nt(grad_side, ao[...])).astype(BF)
    w = cfg.groups * cfg.hd
    for h in range(G):
        go_scr[h] = go[:, h * w : (h + 1) * w]
    for k in range(G):
        go_out[k][...] = go_scr[hi ^ k]
    place_pieces(cfg, hi, attn, o_in)
    ograds[0] = mm(mm(grad_side, select).T.astype(BF), attn[...]).astype(BF)
    half = D // 2
    mine = gm_scr[:, pl.ds(pl.multiple_of(meta[1] * half, half), half)]
    ograds[1] = mm(oside[...].astype(F32).T.astype(BF), mine).astype(BF)


def down_kernel(cfg, meta, hidden, wd, side, part):
    part[:, : cfg.D] = mm(hidden[...], wd[...]).astype(BF)
    part[:, cfg.D :] = side[...]


def output_kernel(cfg, meta, mixed, own, other, bd, out_ref):
    D = cfg.D
    total = own[...].astype(F32) + other[...].astype(F32)
    side = (adapter_mask(cfg, meta) * total[:, D:]).astype(BF)
    out_ref[...] = (mixed[...] + total[:, :D] + mm(side, bd[...])).astype(BF)


def head_back(cfg, cos, sin, grad, raw, g):
    hd = cfg.hd
    copies = raw.shape[1] // hd
    per = raw.shape[1] // cos.shape[1]
    un = grad * lanes(cos[...], per) - swap_halves(grad, hd) * lanes(sin[...], per)
    w = un * lanes(g[...], copies)
    rr = lax.rsqrt(block_mean(raw * raw, hd) + norm_eps)
    return rr * w - rr * rr * rr * raw * block_mean(w * raw, hd)


def half_lanes(cfg, meta):
    half = cfg.D // 2
    keep = pl.ds(pl.multiple_of(meta[1] * half, half), half)
    send = pl.ds(pl.multiple_of((1 - meta[1]) * half, half), half)
    return keep, send


def query_back_kernel(cfg, meta, *refs):
    G, S = cfg.G, cfg.S
    normed, raw, sides, cos, sin, gain, w, a, b, part, bgrad, akeep, asend, dq_scr, a_scr = refs[G:]
    place_pieces(cfg, meta[0] // cfg.lo, dq_scr, refs[:G])
    g = head_back(cfg, cos, sin, dq_scr[...].astype(F32), raw[...], gain).astype(BF)
    select = slot_select(cfg, meta)
    grad_side = (adapter_mask(cfg, meta) * mm_nt(g, b[...])).astype(BF)
    part[...] = mm_nt(g, w[...]) + mm_nt(grad_side, a[...])
    a_scr[...] = mm(mm(grad_side, select).T.astype(BF), normed[...])
    bgrad[...] = mm(sides[0].astype(F32).T.astype(BF), g).astype(BF)
    keep, send = half_lanes(cfg, meta)
    akeep[...] = a_scr[:, keep].astype(BF)
    asend[...] = a_scr[:, send].astype(BF)


def key_value_side_kernel(cfg, meta, *refs):
    G, S, hd = cfg.G, cfg.S, cfg.hd
    dkv_in = refs[:G]
    normed, raw, cos, sin, gain, bk, bv, mine, got, *refs = refs[G:]
    grads, out_sides, akeep, asend, chunk, dkv_scr, a_scr = refs
    half_shared(meta, mine, got, chunk)
    place_pieces(cfg, meta[0] // cfg.lo, dkv_scr, dkv_in)
    mask = adapter_mask(cfg, meta)
    select = slot_select(cfg, meta)
    dkv = dkv_scr[...]
    dk = jnp.concatenate([dkv[:, 2 * h * hd : (2 * h + 1) * hd] for h in range(G)], axis=1)
    dv = jnp.concatenate([dkv[:, (2 * h + 1) * hd : (2 * h + 2) * hd] for h in range(G)], axis=1)
    gk = head_back(cfg, cos, sin, dk.astype(F32), raw[...], gain).astype(BF)
    for i, (g, b) in enumerate(((gk, bk), (dv, bv))):
        grad_side = (mask * mm_nt(g, b[...])).astype(BF)
        grads[i] = g
        out_sides[i] = grad_side
        a_scr[i * S : (i + 1) * S, :] = mm(mm(grad_side, select).T.astype(BF), normed[...])
    keep, send = half_lanes(cfg, meta)
    akeep[...] = a_scr[:, keep].astype(BF)
    asend[...] = a_scr[:, send].astype(BF)


def key_value_back_kernel(
    cfg, meta, grads, grad_sides, sides, wk, wv, ak, av, qpart, part, bgrad
):
    total = qpart[...]
    width = grads.shape[2]
    for i, (w, a) in enumerate(((wk, ak), (wv, av))):
        total = total + mm_nt(grads[i], w[...]) + mm_nt(grad_sides[i], a[...])
        bgrad[:, i * width : (i + 1) * width] = mm(
            sides[i].astype(F32).T.astype(BF), grads[i]
        ).astype(BF)
    part[...] = total.astype(BF)


def input_grad_kernel(cfg, meta, x_ref, gain, gm, own, other, out):
    x = x_ref[...].astype(F32)
    w = (own[...].astype(F32) + other[...].astype(F32)) * gain[...]
    rr = lax.rsqrt(jnp.mean(x * x, axis=-1, keepdims=True) + norm_eps)
    inner = jnp.mean(w * x, axis=-1, keepdims=True)
    out[...] = (gm[...] + rr * w - (rr * rr * rr * inner) * x).astype(BF)


class Units:
    def __init__(self, cfg, n, shared, private):
        self.n = n
        self.high = cfg.S // 16
        self.shared, self.private = shared, private
        self.us, self.up = self.per_chunk(shared), self.per_chunk(private)
        self.u = self.us + self.up

    def per_chunk(self, widths):
        return -(-sum(w // 128 for w in widths) * self.high // self.n)

    def places(self, which):
        widths, per, base = (
            (self.shared, self.us, 0) if which == 0 else (self.private, self.up, self.us)
        )
        at, out = 0, []
        for w in widths:
            spots = []
            for c in range(w // 128):
                for a in range(self.high):
                    spots.append((at // per, base + at % per, a, c))
                    at += 1
            out.append(spots)
        return out

    def spare(self):
        out = []
        for widths, per, base in ((self.shared, self.us, 0), (self.private, self.up, self.us)):
            count = sum(w // 128 for w in widths) * self.high
            out += [(i // per, base + i % per) for i in range(count, per * self.n)]
        return out

    def store(self, out, which, array, values, first=0):
        widths, per, base = (
            (self.shared, self.us, 0) if which == 0 else (self.private, self.up, self.us)
        )
        at = sum(w // 128 for w in widths[:array]) * self.high + first * self.high
        for c in range(values.shape[1] // 128):
            for a in range(self.high):
                unit = at + c * self.high + a
                out[unit // per, base + unit % per] = values[
                    a * 16 : a * 16 + 16, c * 128 : c * 128 + 128
                ]

    def clear_spare(self, out):
        for chunk, off in self.spare():
            out[chunk, off] = jnp.zeros((16, 128), BF)


def pack(units, scr, flip, outs, arrays):
    for i, values in enumerate(arrays):
        which = int(i >= len(units.shared))
        units.store(scr, which, i - which * len(units.shared), values)
    units.clear_spare(scr)
    for j, out in enumerate(outs):
        out[...] = scr[j ^ flip]


def add_halves(keep, got, count):
    total = (keep[...].astype(F32) + got[...].astype(F32)).astype(BF)
    rows = total.shape[0] // count
    return [total[i * rows : (i + 1) * rows] for i in range(count)]


def pack_qkv_kernel(cfg, units, meta, keep_q, got_q, keep, got, ograds, bq, bkv, *outs):
    scr, outs = outs[-1], outs[:-1]
    kw = bkv.shape[1] // 2
    shared = add_halves(keep_q, got_q, 1) + add_halves(keep, got, 2) + [ograds[1]]
    private = [ograds[0], bq[...], bkv[:, :kw], bkv[:, kw:]]
    pack(units, scr, meta[0] % cfg.lo, outs, shared + private)


def split_sum_kernel(cfg, meta, *refs):
    *terms, keep, send = refs
    bit = (meta[0] // cfg.lo) % 2
    for out, half in ((keep, bit), (send, 1 - bit)):
        total = terms[0][half].astype(F32)
        for term in terms[1:]:
            total = total + term[half].astype(F32)
        out[...] = total.astype(BF)


def sum_shared_kernel(meta, mine, got, out, shared):
    total = (mine[...].astype(F32) + got[...].astype(F32)).astype(BF)
    out[...] = total
    shared[...] = total[: shared.shape[0]]


def half_shared(meta, mine, got, out):
    count = got.shape[0]
    at = pl.ds(meta[1] * (count // 2), count // 2)
    out[: count // 2] = (mine[at].astype(F32) + got[at].astype(F32)).astype(BF)
    out[count // 2 :] = mine[count:]


def unpack(read, spots):
    cols = {}
    for chunk, off, a, c in spots:
        cols.setdefault(c, []).append(read(chunk, off))
    return jnp.concatenate([jnp.concatenate(cols[c], axis=0) for c in sorted(cols)], axis=1)


def expand_kernel(cfg, units, plan, halves, meta, *refs):
    own_in, other_in, outs = refs[: cfg.lo], refs[cfg.lo], refs[cfg.lo + 1 : -2]
    own, shared = refs[-2:]
    flip = meta[0] % cfg.lo
    wa = meta[1]
    count = shared.shape[2]
    for j in range(cfg.lo):
        if halves:
            if any(which == 1 for which, _, _ in plan):
                own[j ^ flip] = own_in[j][...]
            if any(which == 0 for which, _, _ in plan):
                shared[wa, j ^ flip] = own_in[j][:count]
                shared[1 - wa, j ^ flip] = other_in[j]
            continue
        for r in range(2):
            at = 2 * (j ^ flip) + (r ^ ((meta[0] // cfg.lo) % 2))
            own[at] = own_in[j][r]
            shared[wa, at] = own_in[j][r, :count]
            shared[1 - wa, at] = other_in[j, r]
    select = slot_select(cfg, meta)

    def write(out, values, transposed, at):
        width = values.shape[1]
        if transposed:
            out[at : at + width, :] = lax.dot_general(
                values, select, (((0,), (1,)), ((), ())), preferred_element_type=F32
            )
        else:
            out[:, at : at + width] = mm(select, values)

    for (which, i, transposed), out in zip(plan, outs):
        spots = units.places(which)[i]
        if which == 1:
            shift = 0 if halves else count
            write(out, unpack(lambda chunk, off: own[chunk, off - shift], spots), transposed, 0)
        elif halves:
            for w in range(2):
                values = unpack(lambda chunk, off: shared[w, chunk, off], spots)
                write(out, values, transposed, w * values.shape[1])
        else:
            values = unpack(lambda chunk, off: shared[off // count, chunk, off % count], spots)
            write(out, values, transposed, 0)


def upper_bits(cfg):
    bits, bit = [], cfg.n // 2
    while bit >= cfg.lo:
        bits.append(bit)
        bit //= 2
    return bits


def after(*values):
    return lax.optimization_barrier(values)


def swap_cores(value):
    return lax.ppermute(value, "wa", [(0, 1), (1, 0)])


def permute(cfg, value, bits):
    return lax.ppermute(value, "ctx", [(i, i ^ bits) for i in range(cfg.n)])


def per_device(
    hidden_in, attn_gain, query_weight, key_weight, value_weight, query_gain, key_gain, out_weight,
    ffn_gain, gate_weight, up_weight, down_weight, query_adapt_in, query_adapt_out, key_adapt_in,
    key_adapt_out, value_adapt_in, value_adapt_out, out_adapt_in, out_adapt_out, gate_adapt_in,
    gate_adapt_out, up_adapt_in, up_adapt_out, down_adapt_in, down_adapt_out, document_extra,
    document_adapter, cotangent,
):
    head_dim = query_gain.shape[0]
    cfg = Cfg(
        tokens=hidden_in.shape[0],
        n_ctx=lax.axis_size("ctx"),
        heads_kv=key_weight.shape[1] // head_dim,
        groups=query_weight.shape[1] // key_weight.shape[1],
        head_dim=head_dim,
        docs=document_extra.shape[0],
        adapt_width=query_adapt_in.shape[1],
        width=hidden_in.shape[2],
        hidden=gate_weight.shape[1],
    )
    T, D, G, S, AW, n, lo = cfg.T, cfg.D, cfg.G, cfg.S, cfg.AW, cfg.n, cfg.lo
    gw = cfg.groups * head_dim
    QW, KW = query_weight.shape[1], key_weight.shape[1]
    meta = (document_extra, document_adapter)
    x = hidden_in.reshape(T, D)
    cot = cotangent.reshape(T, D)
    gain_a = attn_gain.reshape(1, D)
    gain_f = ffn_gain.reshape(1, D)
    qg = query_gain.reshape(1, head_dim)
    kg = key_gain.reshape(1, head_dim)

    lane = np.arange(2 * head_dim) % (head_dim // 2)
    inverse = np.exp(lane * (-2.0 * math.log(theta_base) / head_dim)).astype(np.float32)[None, :]

    piece = ((T, gw), BF)
    fetched = [
        x, key_adapt_in, value_adapt_in, key_weight, key_adapt_out, value_weight, value_adapt_out,
    ]
    first = call(
        functools.partial(key_value_kernel, cfg),
        [piece] * G
        + [((T, KW), F32), ((2, T, S), BF), ((T, D), BF)]
        + [((T, 2 * head_dim), F32)] * 2,
        [meta, *fetched, gain_a, kg, inverse],
        scratch=[pltpu.VMEM(value.shape, value.dtype) for value in fetched]
        + [pltpu.SemaphoreType.DMA((len(fetched),)), pltpu.VMEM((G, T, 2 * head_dim), BF)],
        us=4,
        name="key_value",
        in_place=len(fetched),
        large=True,
    )
    kv_send = first[:G]
    kraw, sides, normed, cos, sin = first[G:]

    def to_heads(pieces):
        return [pieces[0]] + [permute(cfg, pieces[k], k * lo) for k in range(1, G)]

    def add(values):
        return sum(value.astype(F32) for value in values).astype(BF)

    def to_plane(value):
        return [value] + [permute(cfg, value, j) for j in range(1, lo)]

    kv_heads = to_heads(kv_send)
    second = call(
        functools.partial(query_kernel, cfg),
        [piece] * G + [((T, QW), F32), ((1, T, S), BF), items_shape(cfg)],
        [meta, normed, cos, sin, query_weight, query_adapt_in, query_adapt_out, qg],
        scratch=[pltpu.VMEM((G, T, gw), BF)],
        us=3,
        name="query",
        lists=1,
        large=True,
    )
    q_send, (qraw, side_q, items) = second[:G], second[G:]
    listed = (*meta, items)
    both = list(after(*kv_heads, *q_send))
    kv_heads, q_send = both[:G], both[G:]
    kv = to_plane(jnp.stack(kv_heads))
    q = to_heads(q_send)
    grad_hidden, gst = call(
        functools.partial(hidden_grad_kernel, cfg),
        [((T, cfg.F), F32), ((S, T), BF)],
        [meta, cot, down_weight, down_adapt_out, down_adapt_in],
        us=3,
        name="hidden_grad",
    )
    grad_hidden, *both = after(grad_hidden, *kv, *q)
    kv, q = both[:lo], both[lo:]
    tiles = lambda dtype, width=gw: pltpu.VMEM((cfg.NT, 2 * cfg.QH, width), dtype)
    attn = call(
        functools.partial(attend_kernel, cfg),
        [piece] * G + [((G, T, gw), BF), ((G, T, gw), F32)],
        [listed] + q + kv,
        scratch=[tiles(BF), tiles(F32), tiles(jnp.int32, 1)],
        us=12,
        name="attend",
    )
    o_send, o_all, linv = attn[:G], attn[G], attn[G + 1]
    o = to_heads(o_send)
    q_stack, _ = after(jnp.stack(q), o_send[0])
    q_plane = to_plane(q_stack)
    (opart,) = call(
        functools.partial(out_kernel, cfg),
        [((T, D + AW), BF)],
        [meta] + o + [out_weight, out_adapt_in],
        scratch=[pltpu.VMEM((T, QW), BF)],
        us=3,
        name="out_proj",
    )
    units_f = Units(cfg, 2 * lo, [D] * 3, [cfg.F] * 3)
    ffn = ffn_call(
        cfg, units_f, meta, x, opart, swap_cores(opart), out_adapt_out, gain_f, gate_weight, up_weight,
        gate_adapt_out, up_adapt_out, gate_adapt_in, up_adapt_in, down_adapt_in,
        cot, grad_hidden, gst,
    )
    mixed, dfn, hidden, dside, oside, *parts_f = ffn
    dfn, *q_plane = after(dfn, *q_plane)
    mg = call(
        functools.partial(mixed_grad_kernel, cfg),
        [((T, D), F32), ((2, S, D // 2), BF)] + [piece] * G,
        [meta, mixed, dfn, swap_cores(dfn), cot, gain_f]
        + o
        + [out_weight, out_adapt_in, out_adapt_out, oside],
        scratch=[pltpu.VMEM((T, QW), BF), pltpu.VMEM((G, T, gw), BF), pltpu.VMEM((T, D), BF)],
        us=0.01,
        name="mixed_grad",
    )
    grad_mixed, ograds, go_send = mg[0], mg[1], mg[2:]
    go_heads = to_heads(go_send)
    parts_f = [parts_f[0]] + [permute(cfg, parts_f[j], j) for j in range(1, lo)]
    message = G * T + -(-2 * cfg.groups * cfg.NT // 16) * 16
    (go_all,) = call(
        functools.partial(scale_kernel, cfg),
        [((message, gw), BF)],
        [meta] + go_heads + [linv, o_all],
        scratch=[
            pltpu.VMEM((cfg.NT, cfg.QH, gw), F32),
            pltpu.VMEM((cfg.groups * cfg.NT, gw), F32),
        ],
        us=0.01,
        name="scale",
    )
    go_all, *parts_f = after(go_all, *parts_f)
    sum_f, send_f = call(
        functools.partial(split_sum_kernel, cfg),
        [((units_f.u, 16, 128), BF)] * 2,
        [meta, *parts_f],
        us=0.01,
        name="split_sum",
    )
    go_plane = to_plane(go_all)
    dq_send = call(
        functools.partial(grad_query_kernel, cfg),
        [piece] * G,
        [listed] + q + kv + [go_all, o_all],
        scratch=[tiles(BF), tiles(BF), tiles(F32, 1), tiles(F32), tiles(jnp.int32, 1)],
        us=13.5,
        name="grad_query",
    )
    near, far = upper_bits(cfg)[1], upper_bits(cfg)[0]
    got_f, *dq_send = after(permute(cfg, send_f, near), *dq_send)
    sum_f = add([sum_f, got_f])
    dq = to_heads(dq_send)
    dkv_send = call(
        functools.partial(grad_key_kernel, cfg),
        [piece] * G,
        [listed, kv[0]] + q_plane + go_plane,
        scratch=[tiles(BF), tiles(BF), pltpu.VMEM((cfg.NT, 16, cfg.KT), F32), tiles(F32)]
        + [tiles(F32)],
        us=16,
        name="grad_key",
    )
    both = list(after(*dq, *dkv_send))
    dq, dkv_send = both[:G], both[G:]
    dkv = to_heads(dkv_send)
    qpart, bgrad_q, akeep_q, asend_q = call(
        functools.partial(query_back_kernel, cfg),
        [((T, D), F32), ((S, QW), BF), ((S, D // 2), BF), ((S, D // 2), BF)],
        [meta]
        + dq
        + [
            normed, qraw, side_q, cos, sin, qg, query_weight, query_adapt_in, query_adapt_out,
        ],
        scratch=[pltpu.VMEM((T, QW), BF), pltpu.VMEM((S, D), F32)],
        us=0.01,
        name="query_back",
    )
    got_f, qpart = after(permute(cfg, sum_f, far), qpart)
    sum_f, shared_f = call(
        sum_shared_kernel,
        [((units_f.u, 16, 128), BF), ((units_f.us, 16, 128), BF)],
        [meta, sum_f, got_f],
        us=0.01,
        name="sum_shared",
    )
    shared_f, qpart, *dkv = after(swap_cores(shared_f), qpart, *dkv)
    kv_grads, kv_sides, akeep_kv, asend_kv, sum_f = call(
        functools.partial(key_value_side_kernel, cfg),
        [((2, T, KW), BF), ((2, T, AW), BF), ((2 * S, D // 2), BF), ((2 * S, D // 2), BF)]
        + [((units_f.u - units_f.us // 2, 16, 128), BF)],
        [meta]
        + dkv
        + [normed, kraw, cos, sin, kg, key_adapt_out, value_adapt_out, sum_f, shared_f],
        scratch=[pltpu.VMEM((T, 2 * KW), BF), pltpu.VMEM((2 * S, D), F32)],
        us=0.01,
        name="key_value_side",
    )
    dnormed, bgrad_kv = call(
        functools.partial(key_value_back_kernel, cfg),
        [((T, D), BF), ((S, 2 * KW), BF)],
        [meta, kv_grads, kv_sides, sides, key_weight, value_weight, key_adapt_in, value_adapt_in]
        + [qpart],
        us=0.01,
        name="key_value_back",
    )

    def other_core(units, chunks, halves):
        shared = units.us if halves else units.us // 2
        return swap_cores(jnp.stack([chunk[..., :shared, :, :] for chunk in chunks]))

    def expand(units, chunks, theirs, plan, halves, outs, name):
        shared = units.us if halves else units.us // 2
        per = chunks[0].shape[-3]
        return call(
            functools.partial(expand_kernel, cfg, units, plan, halves),
            outs,
            [meta, *chunks, theirs],
            scratch=[
                pltpu.VMEM((units.n, per, 16, 128), BF),
                pltpu.VMEM((2, units.n, shared, 16, 128), BF),
            ],
            us=4,
            name=name,
        )

    units_q = Units(cfg, lo, [D // 2] * 4, [QW, QW, KW, KW])
    parts_q = call(
        functools.partial(pack_qkv_kernel, cfg, units_q),
        [((units_q.u, 16, 128), BF)] * lo,
        [meta, akeep_q, swap_cores(asend_q), akeep_kv, swap_cores(asend_kv), ograds, bgrad_q]
        + [bgrad_kv],
        scratch=[pltpu.VMEM((lo, units_q.u, 16, 128), BF)],
        us=0.01,
        name="pack_qkv",
    )
    dnormed, hidden, *parts_q = after(dnormed, hidden, *parts_q)
    (dpart,) = call(
        functools.partial(down_kernel, cfg),
        [((T, D + AW), BF)],
        [meta, hidden, down_weight, dside],
        us=3,
        name="down_proj",
    )
    dn_other = swap_cores(dnormed)
    near_f = permute(cfg, sum_f, near)
    sum_q = add([parts_q[0]] + [permute(cfg, parts_q[j], j) for j in range(1, lo)])
    sum_q, dn_other, dpart, sum_f, near_f = after(sum_q, dn_other, dpart, sum_f, near_f)
    all_f = to_plane(jnp.stack([sum_f, near_f]))
    (input_rows,) = call(
        functools.partial(input_grad_kernel, cfg),
        [((T, D), BF)],
        [meta, x, gain_a, grad_mixed, dnormed, dn_other],
        us=0.01,
        name="input_grad",
    )
    got_q, input_rows = after(permute(cfg, sum_q, near), input_rows)
    sum_q = add([sum_q, got_q])
    got_q, *all_f = after(permute(cfg, sum_q, far), *all_f)
    sum_q, dpart = after(add([sum_q, got_q]), dpart)
    pieces_q = to_plane(sum_q)
    (out_rows,) = call(
        functools.partial(output_kernel, cfg),
        [((T, D), BF)],
        [meta, mixed, dpart, swap_cores(dpart), down_adapt_out],
        us=0.01,
        name="output",
    )
    gate_in, up_in, down_out, gate_out, up_out, down_in = expand(
        units_f,
        all_f,
        other_core(units_f, all_f, False),
        [(0, 0, True), (0, 1, True), (0, 2, False), (1, 0, False), (1, 1, False), (1, 2, True)],
        False,
        [((D, AW), F32), ((D, AW), F32), ((AW, D), F32)]
        + [((AW, cfg.F), F32), ((AW, cfg.F), F32), ((cfg.F, AW), F32)],
        "expand_ffn",
    )
    down_out, out_rows, *pieces_q = after(down_out, out_rows, *pieces_q)
    theirs_q = other_core(units_q, pieces_q, True)
    out_in, query_out, key_out, value_out = expand(
        units_q,
        pieces_q,
        parts_q[0].reshape(1, units_q.u, 16, 128),
        [(1, 0, True), (1, 1, False), (1, 2, False), (1, 3, False)],
        True,
        [((QW, AW), F32), ((AW, QW), F32), ((AW, KW), F32), ((AW, KW), F32)],
        "expand_own",
    )
    theirs_q, out_in = after(theirs_q, out_in)
    query_in, key_in, value_in, out_out = expand(
        units_q,
        pieces_q,
        theirs_q,
        [(0, 0, True), (0, 1, True), (0, 2, True), (0, 3, False)],
        True,
        [((D, AW), F32)] * 3 + [((AW, D), F32)],
        "expand_qkv",
    )
    return (
        out_rows.reshape(T, 1, D),
        input_rows.reshape(T, 1, D),
        query_in,
        query_out,
        key_in,
        key_out,
        value_in,
        value_out,
        out_in,
        out_out,
        gate_in,
        gate_out,
        up_in,
        up_out,
        down_in,
        down_out,
    )


def solution(mesh):
    return jax.shard_map(
        per_device,
        mesh=mesh,
        in_specs=(
            P(None, "ctx", None), P(), P(None, "wa"), P(None, "wa"), P(None, "wa"), P(), P(),
            P("wa", None), P(), P(None, "wa"), P(None, "wa"), P("wa", None), P(), P(None, "wa"),
            P(), P(None, "wa"), P(), P(None, "wa"), P("wa", None), P(), P(), P(None, "wa"), P(),
            P(None, "wa"), P("wa", None), P(), P(), P(), P(None, "ctx", None),
        ),
        out_specs=(
            P(None, "ctx", None), P(None, "ctx", None), P(), P(None, "wa"), P(), P(None, "wa"), P(),
            P(None, "wa"), P("wa", None), P(), P(), P(None, "wa"), P(), P(None, "wa"),
            P("wa", None), P(),
        ),
        check_vma=False,
    )
```
